32 devices in a mesh: dp: 16 (over z, y, x), seq: 2 (over core).
Axes of the slice: x: 2, y: 2, z: 4, core: 2. Of those that a mesh axis runs over, the one named last changes fastest.
Arguments:
- block_input: bfloat16 [16, 2048, 512], P('dp', 'seq'), may hold values from -6 to 6
- mixer_gain: bfloat16 [512], P(('dp', 'seq')), may hold values from 0.099609375 to 1.8984375
- mixer_bias: bfloat16 [512], P(('dp', 'seq')), may hold values from -3 to 3
- in_proj: bfloat16 [512, 512], P(('dp', 'seq')), may hold values from -0.25 to 0.25
- kernel_param: bfloat16 [512, 192], P(('dp', 'seq')), may hold values from -6 to 6
- skip_gain: bfloat16 [512], P(('dp', 'seq')), may hold values from -4 to 4
- out_proj: bfloat16 [512, 512], P(('dp', 'seq')), may hold values from -0.25 to 0.25
- mlp_gain: bfloat16 [512], P(('dp', 'seq')), may hold values from 0.099609375 to 1.8984375
- mlp_bias: bfloat16 [512], P(('dp', 'seq')), may hold values from -3 to 3
- up_proj: bfloat16 [512, 2048], P(('dp', 'seq')), may hold values from -0.25 to 0.25
- down_proj: bfloat16 [512, 2048], P(('dp', 'seq')), may hold values from -0.125 to 0.125
- out_cotangent: bfloat16 [16, 2048, 512], P('dp', 'seq'), may hold values from -6 to 6
Outputs:
- block_output: bfloat16 [16, 2048, 512], P('dp', 'seq')
- input_grad: float32 [16, 2048, 512], P('dp', 'seq')
- mixer_gain_grad: float32 [512], P(('dp', 'seq'))
- mixer_bias_grad: float32 [512], P(('dp', 'seq'))
- in_proj_grad: float32 [512, 512], P(('dp', 'seq'))
- kernel_param_grad: float32 [512, 192], P(('dp', 'seq'))
- skip_gain_grad: float32 [512], P(('dp', 'seq'))
- out_proj_grad: float32 [512, 512], P(('dp', 'seq'))
- mlp_gain_grad: float32 [512], P(('dp', 'seq'))
- mlp_bias_grad: float32 [512], P(('dp', 'seq'))
- up_proj_grad: float32 [512, 2048], P(('dp', 'seq'))
- down_proj_grad: float32 [512, 2048], P(('dp', 'seq'))
The draws below stay inside these ranges and needn't reach their ends.
All inputs are finite; a program needn't handle non-finite values.
Results may differ from the reference program's by a relative error of at most 0.014.
Values may be sent and summed in bfloat16 or wider, within the bound.
No kernel may reach another device: no remote copies, remote signals or barrier semaphores. Data moves between devices by JAX's collectives and lax.ppermute only.
A program may use at most 128 MiB of HBM per device.

```python
import math
import jax
import jax.numpy as jnp
from jax import lax

D = 512
FF = 2048
TAPS = 32
SCALES = 6
FINE = 3
SEQ_LEN = 2048
POOL = 8
REACH = 224
CREACH = 224
OFFSET = 28
SEQS = 16


def shard_levels(rng, dims, cuts, smallest, high):
    factor_of, own = 1.0, jax.random.fold_in(rng, 6)
    for dim, shards_of in cuts:
        draws = jnp.exp(jax.random.uniform(jax.random.fold_in(own, dim), (shards_of,), jnp.float32, smallest / len(cuts), high / len(cuts)))
        factor_of = factor_of * jnp.repeat(draws, dims[dim] // shards_of).reshape([-1 if axis == dim else 1 for axis in range(len(dims))])
    return factor_of


def normal_values(own_key, shape, width, bound, cuts=(), kind=jnp.bfloat16):
    factor_of = shard_levels(own_key, shape, cuts, -0.22, 0.18) if cuts else 1.0
    entries = jax.random.normal(own_key, shape, jnp.float32) * width * factor_of
    return jnp.minimum(jnp.maximum(entries, -bound), bound).astype(kind)


def setup_inputs(seed: int = 0) -> dict:
    arg_keys = jax.random.split(jax.random.key(seed), 13)
    return {
        "block_input": normal_values(arg_keys[0], (SEQS, SEQ_LEN, D), 1.0, 6.0, ((0, 16), (1, 2))),
        "mixer_gain": jnp.clip(1.0 + 0.18 * jax.random.normal(arg_keys[1], (D,), jnp.float32), 0.099609375, 1.8984375).astype(jnp.bfloat16),
        "mixer_bias": normal_values(arg_keys[2], (D,), 0.5, 3.0, ((0, 32),)),
        "in_proj": normal_values(arg_keys[3], (D, D), D ** -0.5, 0.25, ((0, 32),)),
        "kernel_param": normal_values(arg_keys[4], (D, SCALES * TAPS), 1.0, 6.0, ((0, 32),)),
        "skip_gain": normal_values(arg_keys[5], (D,), 1.0, 4.0, ((0, 32),)),
        "out_proj": normal_values(arg_keys[6], (D, D), D ** -0.5, 0.25, ((0, 32),)),
        "mlp_gain": jnp.clip(1.0 + 0.18 * jax.random.normal(arg_keys[7], (D,), jnp.float32), 0.099609375, 1.8984375).astype(jnp.bfloat16),
        "mlp_bias": normal_values(arg_keys[8], (D,), 0.5, 3.0, ((0, 32),)),
        "up_proj": normal_values(arg_keys[9], (D, FF), D ** -0.5, 0.25, ((0, 32),)),
        "down_proj": normal_values(arg_keys[10], (D, FF), FF ** -0.5, 0.125, ((0, 32),)),
        "out_cotangent": normal_values(arg_keys[11], (SEQS, SEQ_LEN, D), 1.0, 6.0, ((0, 16), (1, 2))),
    }


@jax.custom_vjp
def low(v):
    return lax.optimization_barrier(v.astype(jnp.bfloat16)).astype(jnp.float32)

@jax.custom_vjp
def low_back(v):
    return v

def low_keep(v):
    return (low(v), None)

def low_pass(kept, grad):
    return (grad,)

def back_keep(v):
    return (v, None)

def back_low(kept, grad):
    return (low(grad),)
low.defvjp(low_keep, low_pass)
low_back.defvjp(back_keep, back_low)

def layer_norm(features, norm_gain, norm_bias):
    centre_val = features - lax.optimization_barrier(jnp.mean(features, axis=-1, keepdims=True))
    variance = lax.optimization_barrier(jnp.mean(centre_val * centre_val, axis=-1, keepdims=True))
    return centre_val * lax.rsqrt(variance + 1e-05) * norm_gain + norm_bias

def gelu_exact(values):
    return jax.nn.gelu(values, approximate=False)

def project(values, matrix, form):
    return jnp.einsum(form, values, matrix, precision=lax.Precision.HIGHEST)

def build_kernel(param_rows):
    fine_parts = []
    coarse_parts = []
    for scale_at in range(SCALES):
        columns = param_rows[:, scale_at * TAPS:(scale_at + 1) * TAPS].T
        if scale_at < FINE:
            fine_parts.append(jnp.repeat(columns, 2 ** scale_at, axis=0) * 0.5 ** scale_at)
        else:
            coarse_parts.append(jnp.repeat(columns, 2 ** (scale_at - FINE), axis=0) * 0.5 ** scale_at)
    raw_fine = jnp.concatenate(fine_parts, axis=0)
    raw_coarse = jnp.concatenate(coarse_parts, axis=0)
    squares = lax.optimization_barrier(jnp.sum(raw_fine * raw_fine, axis=0)) + lax.optimization_barrier(jnp.sum(raw_coarse * raw_coarse, axis=0))
    inverse = lax.rsqrt(squares + 1e-05)
    return (raw_fine * inverse, raw_coarse * inverse)

def tap_sum(source, kernel, start_at, length, stride):

    def one_tap(running, tap_at):
        window = lax.dynamic_slice_in_dim(source, start_at + stride * tap_at, length, 1)
        return (running + window * lax.dynamic_index_in_dim(kernel, tap_at, 0, False), None)
    running = jnp.zeros((source.shape[0], length, source.shape[2]), source.dtype)
    running, _ = lax.scan(jax.checkpoint(one_tap), running, jnp.arange(kernel.shape[0], dtype=jnp.int32))
    return running

def forward(weights, inputs):
    mixer_gain, mixer_bias, in_proj, kernel_param, skip_gain, out_proj, mlp_gain, mlp_bias, up_proj, down_proj = weights
    normed_in = low(layer_norm(inputs, mixer_gain, mixer_bias))
    mixed = low_back(low(project(normed_in, in_proj, 'std,de->ste')))
    fine_kernel, coarse_kernel = build_kernel(kernel_param)
    fine_kernel = low(fine_kernel)
    coarse_kernel = low(coarse_kernel)
    extended = jnp.pad(mixed, ((0, 0), (REACH, 0), (0, 0)))
    fine_part = tap_sum(extended, fine_kernel, REACH, SEQ_LEN, -1)
    pooled = low(lax.optimization_barrier(jnp.mean(mixed.reshape(mixed.shape[0], SEQ_LEN // POOL, POOL, D), axis=2)))
    padded_pool = jnp.pad(pooled, ((0, 0), (OFFSET + CREACH, 0), (0, 0)))
    coarse_part = tap_sum(padded_pool, coarse_kernel, CREACH, SEQ_LEN // POOL, -1)
    pre_act = low_back(fine_part + jnp.repeat(coarse_part, POOL, axis=1) + skip_gain * mixed)
    act = low(gelu_exact(pre_act))
    middle = inputs + low_back(project(act, out_proj, 'ste,ed->std'))
    normed_mid = low(layer_norm(middle, mlp_gain, mlp_bias))
    up_val = low_back(project(normed_mid, up_proj, 'std,df->stf'))
    hidden = low(gelu_exact(up_val))
    return middle + project(hidden, down_proj, 'stf,df->std')

def reference(block_input, mixer_gain, mixer_bias, in_proj, kernel_param, skip_gain, out_proj, mlp_gain, mlp_bias, up_proj, down_proj, out_cotangent):
    weights = tuple((member.astype(jnp.float32) for member in (mixer_gain, mixer_bias, in_proj, kernel_param, skip_gain, out_proj, mlp_gain, mlp_bias, up_proj, down_proj)))
    pair_size = math.gcd(SEQS, 2)
    inputs = block_input.astype(jnp.float32).reshape(SEQS // pair_size, pair_size, SEQ_LEN, D)
    cotangents = out_cotangent.astype(jnp.float32).reshape(SEQS // pair_size, pair_size, SEQ_LEN, D)

    def one_group(totals, group_pair):
        group_in, group_cot = group_pair
        result, pullback = jax.vjp(forward, weights, group_in)
        weight_grads, group_grad = pullback(group_cot)
        return (jax.tree.map(jnp.add, totals, weight_grads), (result, group_grad))
    zero_grads = jax.tree.map(jnp.zeros_like, weights)
    totals, (results, input_grads) = lax.scan(one_group, zero_grads, (inputs, cotangents))
    return (results.reshape(SEQS, SEQ_LEN, D).astype(jnp.bfloat16), input_grads.reshape(SEQS, SEQ_LEN, D), totals[0], totals[1], totals[2], totals[3], totals[4], totals[5], totals[6], totals[7], totals[8], totals[9])
```

```python
import math

import jax
import jax.numpy as jnp
import numpy as np
from jax import lax
from jax.sharding import PartitionSpec as P

TAPS = 32
SCALES = 6
FINE = 3
FREQ = 256
BLOCK = 256
POOL = 8
OFFSET = 28
F32 = jnp.float32
BF16 = jnp.bfloat16


def odd_basis(positions):
    angle = np.pi * np.outer(np.arange(FREQ) + 0.5, positions) / FREQ
    return np.concatenate([np.cos(angle), -np.sin(angle)], axis=0)


def tap_basis(first_scale, start):
    columns = []
    for scale_at in range(FINE):
        wide = 2**scale_at
        lag = start + TAPS * (wide - 1)
        for tap in range(TAPS):
            columns.append(odd_basis(lag + tap * wide + np.arange(wide)).sum(axis=1))
    return np.stack(columns, axis=1)


def bf16_const(array):
    return jnp.asarray(np.asarray(array, np.float32).astype(jnp.bfloat16))


def dot(a, b, contract=((1,), (0,))):
    return lax.dot_general(a, b, (contract, ((), ())), preferred_element_type=F32)


def normal_parts(values):
    scaled = values * np.float32(math.sqrt(0.5))
    cdf = 0.5 + 0.5 * lax.erf(scaled)
    pdf = jnp.exp(-scaled * scaled) * np.float32(1 / math.sqrt(2 * math.pi))
    return cdf, pdf


def split_dp(count):
    edge = round((count / 2) ** (1 / 3))
    return (2 * edge, edge * edge) if 2 * edge**3 == count else (1, count)


def swap_route(count, mask):
    return [(i, i ^ mask) for i in range(count)]


def gather_rows(shard):
    dp_count = lax.axis_size("dp")
    nz, nxy = split_dp(dp_count)
    pieces = [shard] + [
        lax.ppermute(shard, "dp", swap_route(dp_count, k * nxy)) for k in range(1, nz)
    ]
    held = jnp.stack(pieces)
    pieces = [held] + [lax.ppermute(held, "dp", swap_route(dp_count, k)) for k in range(1, nxy)]
    held = jnp.stack(pieces)
    held = jnp.stack([held, lax.ppermute(held, "seq", [(0, 1), (1, 0)])])
    me, core = lax.axis_index("dp"), lax.axis_index("seq")
    where = jnp.arange(dp_count) ^ me
    flat = held.reshape((2, dp_count) + shard.shape)
    order = (where % nxy) * nz + where // nxy
    flat = jnp.take(jnp.take(flat, order, axis=1), jnp.arange(2) ^ core, axis=0)
    return jnp.swapaxes(flat, 0, 1).reshape((dp_count * 2 * shard.shape[0],) + shard.shape[1:])


def reduce_rows(term):
    dp_count = lax.axis_size("dp")
    core = lax.axis_index("seq")
    rows = term.shape[0] // (2 * dp_count)
    shaped = term.reshape((dp_count, 2, rows) + term.shape[1:])
    other = lax.dynamic_index_in_dim(shaped, 1 - core, 1, False).astype(BF16)
    mine = lax.dynamic_index_in_dim(shaped, core, 1, False)
    half = (mine + lax.ppermute(other, "seq", [(0, 1), (1, 0)]).astype(F32)).astype(BF16)
    spread = lax.all_to_all(half, "dp", split_axis=0, concat_axis=0, tiled=True)
    return jnp.sum(spread.astype(F32), axis=0)


def normalize(features):
    centre = features - jnp.mean(features, axis=-1, keepdims=True)
    inverse = lax.rsqrt(jnp.mean(centre * centre, axis=-1, keepdims=True) + 1e-05)
    return centre * inverse, inverse


def norm_back(xhat, inverse, scaled):
    return inverse * (
        scaled
        - jnp.mean(scaled, axis=-1, keepdims=True)
        - xhat * jnp.mean(scaled * xhat, axis=-1, keepdims=True)
    )


def halves(spectrum):
    return spectrum[:FREQ], spectrum[FREQ:]


def body(
    block_input,
    mixer_gain,
    mixer_bias,
    in_proj,
    kernel_param,
    skip_gain,
    out_proj,
    mlp_gain,
    mlp_bias,
    up_proj,
    down_proj,
    out_cotangent,
):
    core = lax.axis_index("seq")
    _, length, feats = block_input.shape
    hidden_count = up_proj.shape[1]
    blocks = length // BLOCK
    pooled_len = length // POOL
    x_own = block_input[0]
    cot = out_cotangent[0]
    x_prior = lax.ppermute(x_own, "seq", [(0, 1)])

    vectors = jnp.stack([mixer_gain, mixer_bias, skip_gain, mlp_gain, mlp_bias], axis=1)
    packed = gather_rows(jnp.concatenate([in_proj, kernel_param, vectors], axis=1))
    proj_out = gather_rows(out_proj)
    proj_mlp = gather_rows(jnp.concatenate([up_proj, down_proj], axis=1))
    proj_in = packed[:, :feats]
    param = packed[:, feats : feats + TAPS * SCALES].astype(F32)
    vec = packed[:, feats + TAPS * SCALES :].astype(F32).T
    gain_one, bias_one, skip, gain_two, bias_two = (vec[i : i + 1] for i in range(5))
    proj_up, proj_down = proj_mlp[:, :hidden_count], proj_mlp[:, hidden_count:]

    basis = bf16_const(odd_basis(np.arange(BLOCK)))
    basis_pool = bf16_const(odd_basis(np.arange(-pooled_len, pooled_len)))
    fine_basis = bf16_const(tap_basis(0, 0))
    coarse_basis = bf16_const(tap_basis(FINE, OFFSET))
    sign = jnp.asarray(((-1.0) ** np.arange(FREQ)).astype(np.float32))[:, None]
    pool_rows = np.kron(np.eye(BLOCK // POOL), np.ones((1, POOL)))
    back_pool = bf16_const(
        np.repeat(odd_basis(np.arange(pooled_len)).T, POOL, axis=0)
    )

    tap_scale = jnp.asarray(np.repeat(0.5 ** np.arange(SCALES), TAPS).astype(np.float32))[None]
    tap_wide = jnp.asarray(
        np.repeat(2.0 ** (np.arange(SCALES) % FINE), TAPS).astype(np.float32)
    )[None]

    def taps_of(rows):
        raw = rows * tap_scale
        inverse = lax.rsqrt(jnp.sum(raw * raw * tap_wide, axis=1, keepdims=True) + 1e-05)
        return raw * inverse, inverse

    taps = taps_of(param)[0].astype(BF16)
    fine_h = halves(dot(fine_basis, taps[:, : TAPS * FINE], ((1,), (1,))))
    coarse_h = halves(dot(coarse_basis, taps[:, TAPS * FINE :], ((1,), (1,))))

    xhat, inv_one = normalize(x_own.astype(F32))
    xhat_prior, _ = normalize(x_prior.astype(F32))
    mixed = dot((xhat * gain_one + bias_one).astype(BF16), proj_in).astype(BF16)
    mixed_prior = dot((xhat_prior * gain_one + bias_one).astype(BF16), proj_in).astype(BF16)
    mixed_prior = jnp.where(core > 0, mixed_prior, jnp.zeros_like(mixed_prior))
    mixed_all = jnp.concatenate([mixed_prior, mixed], axis=0)
    pooled = (
        jnp.sum(mixed_all.astype(F32).reshape(2 * pooled_len, POOL, feats), axis=1) / POOL
    ).astype(BF16)

    def span(source, at):
        return source[at * BLOCK : (at + 1) * BLOCK]

    z_mixed = [halves(dot(basis, span(mixed_all, blocks - 1 + at))) for at in range(blocks + 1)]
    window = []
    for at in range(blocks):
        (pr, pi), (zr, zi) = z_mixed[at], z_mixed[at + 1]
        window.append((zr - sign * pi, zi + sign * pr))
    pool_win = halves(dot(basis_pool, pooled))

    def product(h, w):
        return jnp.concatenate([h[0] * w[0] - h[1] * w[1], h[0] * w[1] + h[1] * w[0]]).astype(BF16)

    def conj_product(h, w):
        return jnp.concatenate([h[0] * w[0] + h[1] * w[1], h[0] * w[1] - h[1] * w[0]]).astype(BF16)

    inverse_scale = np.float32(1 / FREQ)
    coarse_y = product(coarse_h, pool_win)
    coarse_part = dot(back_pool, coarse_y)
    fine_part = jnp.concatenate(
        [dot(basis, product(fine_h, window[at]), ((0,), (0,))) for at in range(blocks)]
    )
    mixed_f = mixed.astype(F32)
    pre_act = (fine_part + coarse_part) * inverse_scale + skip * mixed_f
    cdf_one, pdf_one = normal_parts(pre_act)
    act = (pre_act * cdf_one).astype(BF16)
    slope_one = cdf_one + pre_act * pdf_one
    middle = x_own.astype(F32) + dot(act, proj_out)

    xhat_two, inv_two = normalize(middle)
    normed_mid = (xhat_two * gain_two + bias_two).astype(BF16)
    up_val = dot(normed_mid, proj_up)
    cdf_two, pdf_two = normal_parts(up_val)
    hidden = (up_val * cdf_two).astype(BF16)
    block_output = (middle + dot(hidden, proj_down, ((1,), (1,)))).astype(BF16)
    down_grad = dot(cot, hidden, ((0,), (0,)))
    grad_up = (dot(cot, proj_down) * (cdf_two + up_val * pdf_two)).astype(BF16)
    up_grad = dot(normed_mid, grad_up, ((0,), (0,)))
    grad_nmid = dot(grad_up, proj_up, ((1,), (1,)))
    gain_two_grad = jnp.sum(grad_nmid * xhat_two, axis=0)
    bias_two_grad = jnp.sum(grad_nmid, axis=0)
    grad_mid = cot.astype(F32) + norm_back(xhat_two, inv_two, grad_nmid * gain_two)
    mlp_sums = reduce_rows(jnp.concatenate([up_grad, down_grad], axis=1))

    grad_branch = grad_mid.astype(BF16)
    out_grad = dot(act, grad_branch, ((0,), (0,)))
    grad_pre = (dot(grad_branch, proj_out, ((1,), (1,))) * slope_one).astype(BF16)
    grad_cpool = jnp.sum(
        grad_pre.astype(F32).reshape(pooled_len, POOL, feats), axis=1
    ).astype(BF16)
    after = lax.ppermute(
        jnp.concatenate([grad_pre[:BLOCK], grad_cpool], axis=0), "seq", [(1, 0)]
    )
    grad_all = jnp.concatenate([grad_pre, after[:BLOCK]], axis=0)
    z_grad = [halves(dot(basis, span(grad_all, at))) for at in range(blocks + 1)]
    z_pool = halves(dot(basis[:, :pooled_len], grad_cpool))
    z_pool_all = halves(
        dot(basis, jnp.concatenate([grad_cpool, after[BLOCK:]], axis=0))
    )

    def corr(g, w):
        return jnp.concatenate([g[0] * w[0] + g[1] * w[1], g[1] * w[0] - g[0] * w[1]])

    fine_s = sum(corr(z_grad[at], window[at]) for at in range(blocks)).astype(BF16)
    coarse_s = corr(z_pool, pool_win).astype(BF16)
    tap_sums = (
        jnp.concatenate(
            [dot(fine_s, fine_basis, ((0,), (0,))), dot(coarse_s, coarse_basis, ((0,), (0,)))],
            axis=1,
        )
        * inverse_scale
    )
    pieces = []
    for at in range(blocks):
        (zr, zi), (nr, ni) = z_grad[at], z_grad[at + 1]
        pieces.append(
            dot(basis, conj_product(fine_h, (zr + sign * ni, zi - sign * nr)), ((0,), (0,)))
        )
    pool_back = dot(back_pool, conj_product(coarse_h, z_pool_all))
    grad_mixed = (
        (jnp.concatenate(pieces) + pool_back * np.float32(1 / POOL)) * inverse_scale
        + skip * grad_pre.astype(F32)
    ).astype(BF16)
    in_back = dot(xhat.astype(BF16), grad_mixed, ((0,), (0,)))
    mixed_sum = jnp.sum(grad_mixed.astype(F32), axis=0, keepdims=True)
    gain_column, bias_column = gain_one.T, bias_one.T
    in_grad = gain_column * in_back + bias_column * mixed_sum
    proj_in_f = proj_in.astype(F32)
    gain_one_grad = jnp.sum(proj_in_f * in_back, axis=1)
    bias_one_grad = jnp.sum(proj_in_f * mixed_sum, axis=1)
    columns = jnp.stack([gain_one_grad, bias_one_grad, gain_two_grad, bias_two_grad], axis=1)
    mixer_sums = reduce_rows(jnp.concatenate([in_grad, out_grad, tap_sums, columns], axis=1))
    grad_nin = dot(grad_mixed, proj_in, ((1,), (1,)))
    input_grad = grad_mid + norm_back(xhat, inv_one, grad_nin * gain_one)

    tap_rows = mixer_sums[:, 2 * feats : 2 * feats + TAPS * SCALES]
    own_taps, own_inverse = taps_of(kernel_param.astype(F32))
    along = jnp.sum(tap_rows * own_taps, axis=1, keepdims=True)
    param_grad = tap_scale * own_inverse * (tap_rows - tap_wide * own_taps * along)
    tail = mixer_sums[:, 2 * feats + TAPS * SCALES :]
    return (
        block_output[None],
        input_grad[None],
        tail[:, 0],
        tail[:, 1],
        mixer_sums[:, :feats],
        param_grad,
        tap_rows[:, 0],
        mixer_sums[:, feats : 2 * feats],
        tail[:, 2],
        tail[:, 3],
        mlp_sums[:, :hidden_count],
        mlp_sums[:, hidden_count:],
    )


def solution(mesh):
    rows = P(("dp", "seq"), None)
    vector = P(("dp", "seq"))
    tokens = P("dp", "seq", None)
    return jax.shard_map(
        body,
        mesh=mesh,
        in_specs=(
            tokens, vector, vector, rows, rows, vector, rows, vector, vector, rows, rows, tokens,
        ),
        out_specs=(
            tokens, tokens, vector, vector, rows, rows, vector, rows, vector, vector, rows, rows,
        ),
        check_vma=False,
    )
```

```python
import math

import jax
import jax.numpy as jnp
import numpy as np
from jax import lax
from jax.experimental import pallas as pl
from jax.experimental.pallas import tpu as pltpu
from jax.sharding import PartitionSpec as P

TAPS = 32
SCALES = 6
FINE = 3
FREQ = 256
HALF = FREQ // 2
BLOCK = 256
POOL = 8
OFFSET = 28
TILE = 512
WIDE = 512
PACK = 768
F32 = jnp.float32
BF16 = jnp.bfloat16
NT = ((1,), (1,))
TN = ((0,), (0,))


def odd_basis(positions):
    order = np.concatenate([np.arange(0, FREQ, 2), np.arange(1, FREQ, 2)])
    angle = np.pi * np.outer(order + 0.5, positions) / FREQ
    return np.concatenate([np.cos(angle), -np.sin(angle)], axis=0)


def tap_basis(start, first):
    columns = np.zeros((2 * FREQ, 256))
    for scale_at in range(FINE):
        wide = 2**scale_at
        lag = start + TAPS * (wide - 1)
        for tap in range(TAPS):
            at = first + scale_at * TAPS + tap
            columns[:, at] = odd_basis(lag + tap * wide + np.arange(wide)).sum(axis=1)
    return columns


def bf16_const(array):
    return jnp.asarray(np.asarray(array, np.float32).astype(jnp.bfloat16))


def dot(a, b, contract=((1,), (0,))):
    return lax.dot_general(a, b, (contract, ((), ())), preferred_element_type=F32)


def normal_parts(values):
    cdf = 0.5 + 0.5 * lax.erf(values * np.float32(math.sqrt(0.5)))
    pdf = jnp.exp(-0.5 * values * values) * np.float32(1 / math.sqrt(2 * math.pi))
    return cdf, pdf


def split_dp(count):
    edge = round((count / 2) ** (1 / 3))
    return (2 * edge, edge * edge) if 2 * edge**3 == count else (1, count)


def swap_route(count, mask):
    return [(i, i ^ mask) for i in range(count)]


SWAP = [(0, 1), (1, 0)]


def tie(value, *others):
    return lax.optimization_barrier((value, *others))[0]


def gather_far(shard):
    dp_count = lax.axis_size("dp")
    nz, nxy = split_dp(dp_count)
    return jnp.stack(
        [shard]
        + [lax.ppermute(shard, "dp", swap_route(dp_count, k * nxy)) for k in range(1, nz)]
    )


def gather_near(held):
    dp_count = lax.axis_size("dp")
    _, nxy = split_dp(dp_count)
    return [held] + [lax.ppermute(held, "dp", swap_route(dp_count, k)) for k in range(1, nxy)]


def gather_core(pieces):
    return pieces + [lax.ppermute(piece, "seq", SWAP) for piece in pieces]


def row_places():
    dp_count = lax.axis_size("dp")
    nz, nxy = split_dp(dp_count)
    me, core = lax.axis_index("dp"), lax.axis_index("seq")
    by_dp = (jnp.arange(nz)[None, :] * nxy + jnp.arange(nxy)[:, None]) ^ me
    where = by_dp[None] * 2 + (jnp.arange(2)[:, None, None] ^ core)
    return where.reshape(-1).astype(jnp.int32)


def in_order(pieces, where):
    rows = pieces[0].shape[1]
    if rows % 16 == 0:
        return pieces, where
    flat = jnp.concatenate(pieces)
    full = jnp.take(flat, jnp.argsort(where), axis=0).reshape(1, -1, flat.shape[2])
    return [full], jnp.zeros((1,), jnp.int32)


def reduce_core(grads, *before):
    dp_count = lax.axis_size("dp")
    nz, nxy = split_dp(dp_count)
    if len(grads) == 1:
        core, me = lax.axis_index("seq"), lax.axis_index("dp")
        shaped = grads[0].reshape(dp_count, 2, -1, grads[0].shape[1])
        order = (jnp.arange(nz)[None, :] * nxy + jnp.arange(nxy)[:, None]) ^ me
        shaped = jnp.take(shaped, order.reshape(-1), axis=0)
        grads = [
            lax.dynamic_index_in_dim(shaped, 1 - core, 1, False),
            lax.dynamic_index_in_dim(shaped, core, 1, False),
        ]
    send, keep = grads
    got = lax.ppermute(send, "seq", SWAP)
    got = tie(got, *before)
    total = (keep.astype(F32) + got.astype(F32)).astype(BF16)
    return [total[k * nz : (k + 1) * nz] for k in range(nxy)]


def spread_near(pieces):
    dp_count = lax.axis_size("dp")
    return [pieces[0]] + [
        lax.ppermute(pieces[k], "dp", swap_route(dp_count, k)) for k in range(1, len(pieces))
    ]


def spread_far(part):
    dp_count = lax.axis_size("dp")
    nz, nxy = split_dp(dp_count)
    return [part[0]] + [
        lax.ppermute(part[k], "dp", swap_route(dp_count, k * nxy)) for k in range(1, nz)
    ]


def add_up(pieces, dtype=F32):
    total = pieces[0].astype(F32)
    for piece in pieces[1:]:
        total = total + piece.astype(F32)
    return total.astype(dtype)


def load_rows(where_ref, pieces, target, sem):
    copies = []
    at = 0
    for piece in pieces:
        count, rows, _ = piece.shape
        for i in range(count):
            start = pl.multiple_of(where_ref[at] * rows, 16)
            copies.append(
                pltpu.make_async_copy(piece.at[i], target.at[pl.ds(start, rows), :], sem)
            )
            at += 1
    for copy in copies:
        copy.start()
    return copies


def span(at, size=BLOCK):
    return pl.ds(at * size, size)


def norm_stats(features):
    centre = features - jnp.mean(features, axis=-1, keepdims=True)
    inverse = lax.rsqrt(jnp.mean(centre * centre, axis=-1, keepdims=True) + 1e-05)
    return centre * inverse, inverse


def norm_back(xhat, inverse, scaled):
    return inverse * (
        scaled
        - jnp.mean(scaled, axis=-1, keepdims=True)
        - xhat * jnp.mean(scaled * xhat, axis=-1, keepdims=True)
    )


def quarters(spectrum):
    return [spectrum[i * HALF : (i + 1) * HALF].astype(F32) for i in range(4)]


def add_before(now, past):
    (re, ro, ie, io), (pre, pro, pie, pio) = now, past
    return re - pie, ro + pio, ie + pre, io - pro


def add_after(now, later):
    (re, ro, ie, io), (nre, nro, nie, nio) = now, later
    return re + nie, ro - nio, ie - nre, io + nro


def product(a, b):
    (are, aro, aie, aio), (bre, bro, bie, bio) = a, b
    return (
        are * bre - aie * bie,
        aro * bro - aio * bio,
        are * bie + aie * bre,
        aro * bio + aio * bro,
    )


def conj_product(a, b):
    (are, aro, aie, aio), (bre, bro, bie, bio) = a, b
    return (
        are * bre + aie * bie,
        aro * bro + aio * bio,
        are * bie - aie * bre,
        aro * bio - aio * bro,
    )


def stacked(parts):
    return jnp.concatenate([part.astype(BF16) for part in parts], axis=0)


def put_quarters(ref, at, parts):
    for i, part in enumerate(parts):
        ref[at, i * HALF : (i + 1) * HALF, :] = part.astype(ref.dtype)


def pack_kernel(in_ref, param_ref, out_ref, up_ref, down_ref, *rest):
    vectors, (first_ref, rest_ref, param, small, sem) = rest[:5], rest[5:]
    rows, feats = in_ref.shape
    half = up_ref.shape[1] // 2
    at = 0
    copies = [
        pltpu.make_async_copy(in_ref, first_ref.at[:, pl.ds(0, feats)], sem),
        pltpu.make_async_copy(param_ref, param, sem),
    ]
    for i, vector in enumerate(vectors):
        copies.append(pltpu.make_async_copy(vector, small.at[i], sem))
    for source, start, size in (
        (out_ref, 0, feats), (up_ref, 0, half), (down_ref, 0, half), (up_ref, half, half),
        (down_ref, half, half),
    ):
        copies.append(
            pltpu.make_async_copy(
                source.at[:, pl.ds(start, size)], rest_ref.at[:, pl.ds(at, size)], sem
            )
        )
        at += size
    for copy in copies:
        copy.start()
    for copy in copies:
        copy.wait()
    spare = PACK - feats - param.shape[1]
    row = lax.broadcasted_iota(jnp.int32, (rows, rows), 0)
    lane = lax.broadcasted_iota(jnp.int32, (rows, rows), 1)
    slot = lax.broadcasted_iota(jnp.int32, (rows, spare), 1)
    block = jnp.zeros((rows, spare), F32)
    for i in range(len(vectors)):
        value = small[i].astype(F32)
        column = jnp.sum(jnp.where(row == lane, value, 0.0), axis=1, keepdims=True)
        block = jnp.where(slot == i, column, block)
    tail = jnp.concatenate([param[...].astype(F32), block], axis=1)
    first_ref[:, feats:] = tail.astype(BF16)


def prepare_kernel(x_ref, cot_ref, xhat_ref, xhat_t_ref, inv_ref, cot_t_ref, cot_copy_ref, x_copy_ref, sem):
    blocks = x_ref.shape[0] // BLOCK
    copies = []
    for source, target, which in ((x_ref, x_copy_ref, 0), (cot_ref, cot_copy_ref, 1)):
        for at in range(blocks):
            copies.append(
                pltpu.make_async_copy(source.at[span(at), :], target.at[span(at), :], sem.at[which, at])
            )
    for copy in copies:
        copy.start()
    for at in range(blocks):
        copies[at].wait()
        xhat, inverse = norm_stats(x_copy_ref[span(at), :].astype(F32))
        xhat = xhat.astype(BF16)
        xhat_ref[span(at), :] = xhat
        xhat_t_ref[:, span(at)] = xhat.T
        inv_ref[span(at), :] = jnp.broadcast_to(inverse, (BLOCK, 128))
    for at in range(blocks):
        copies[blocks + at].wait()
        cot_t_ref[:, span(at)] = cot_copy_ref[span(at), :].T


def prior_kernel(x_ref, xhat_ref):
    for at in range(x_ref.shape[0] // BLOCK):
        xhat_ref[span(at), :] = norm_stats(x_ref[span(at), :].astype(F32))[0].astype(BF16)


def forward_kernel(
    n_pieces, core_ref, where_ref, xhat_ref, prior_ref, basis, basis_t, basis_pool, back_pool,
    fine_basis, coarse_basis, pool_rows, scale_ref, wide_ref, *rest,
):
    pieces, rest = rest[:n_pieces], rest[n_pieces:]
    weights, vec_ref, fine_h_ref, coarse_h_ref, win_ref, pool_win_ref, act_ref, slope_ref = rest[:8]
    mixed_ref, pooled_ref, sem = rest[8:]
    for copy in load_rows(where_ref, pieces, weights, sem):
        copy.wait()
    feats = xhat_ref.shape[1]
    blocks = xhat_ref.shape[0] // BLOCK
    tail = weights[:, feats : feats + 256].astype(F32)
    raw = tail * scale_ref[...]
    inverse = lax.rsqrt(jnp.sum(raw * raw * wide_ref[...], axis=1, keepdims=True) + 1e-05)
    taps = (raw * inverse).astype(BF16)
    vec = tail[:, 128:256].T[64:72]
    vec_ref[...] = vec
    gain, bias, skip = vec[0:1], vec[1:2], vec[2:3]
    fine_h = dot(fine_basis[...], taps, NT)
    coarse_h = dot(coarse_basis[...], taps, NT)
    fine_h_ref[...] = fine_h
    coarse_h_ref[...] = coarse_h
    proj = weights[:, :feats]
    has_prior = core_ref[0].astype(F32)
    per = BLOCK // POOL
    past = None
    for at in range(blocks):
        normed = (prior_ref[span(at), :].astype(F32) * gain + bias).astype(BF16)
        mixed = (dot(normed, proj) * has_prior).astype(BF16)
        pooled_ref[span(at, per), :] = dot(pool_rows[...], mixed).astype(BF16)
        if at == blocks - 1:
            past = quarters(dot(basis[...], mixed))
    for at in range(blocks):
        normed = (xhat_ref[span(at), :].astype(F32) * gain + bias).astype(BF16)
        mixed = dot(normed, proj).astype(BF16)
        mixed_ref[span(at), :] = mixed
        pooled_ref[span(blocks + at, per), :] = dot(pool_rows[...], mixed).astype(BF16)
    pool_win = dot(basis_pool[...], pooled_ref[...])
    pool_win_ref[...] = pool_win.astype(BF16)
    coarse_y = stacked(product(quarters(coarse_h), quarters(pool_win)))
    fine_q = quarters(fine_h)
    for at in range(blocks):
        mixed = mixed_ref[span(at), :]
        now = quarters(dot(basis[...], mixed))
        window = add_before(now, past)
        past = now
        put_quarters(win_ref, at, window)
        total = dot(basis_t[...], stacked(product(fine_q, window)))
        total = total + dot(back_pool[span(at), :], coarse_y)
        pre_act = total * np.float32(1 / FREQ) + skip * mixed.astype(F32)
        cdf, pdf = normal_parts(pre_act)
        act_ref[span(at), :] = (pre_act * cdf).astype(BF16)
        slope_ref[span(at), :] = (cdf + pre_act * pdf).astype(BF16)


def place_of(core_ref, grad_refs):
    nz, nxy = split_dp(grad_refs[0].shape[0])
    return core_ref[0], core_ref[1] // nxy, core_ref[1] % nxy, nz, nxy


def put_rows(refs, columns, value, place):
    value = value.astype(BF16)
    if len(refs) == 1:
        refs[0][:, columns] = value
        return
    send_ref, keep_ref = refs
    count, rows, _ = send_ref.shape
    core, me_z, me_xy, nz, nxy = place
    for at in range(count):
        slot = ((at % nxy) ^ me_xy) * nz + ((at // nxy) ^ me_z)
        first = value[2 * at * rows : (2 * at + 1) * rows]
        second = value[(2 * at + 1) * rows : (2 * at + 2) * rows]
        send_ref[slot, :, columns] = jnp.where(core == 0, second, first)
        keep_ref[slot, :, columns] = jnp.where(core == 0, first, second)


def hidden_part(place, normed_ref, normed_t_ref, cot_ref, cot_t_ref, up_at, down_at, weights, hidden_ref, grad_up_ref, grad_refs):
    length = normed_ref.shape[0]
    count = hidden_ref.shape[1]
    for at in range(0, count, WIDE):
        columns = slice(at, at + WIDE)
        up = weights[:, up_at + at : up_at + at + WIDE]
        down = weights[:, down_at + at : down_at + at + WIDE]
        for row in range(0, length, TILE):
            rows = slice(row, row + TILE)
            up_val = dot(normed_ref[rows, :], up)
            grad_hidden = dot(cot_ref[rows, :], down)
            cdf, pdf = normal_parts(up_val)
            hidden_ref[rows, columns] = (up_val * cdf).astype(BF16)
            grad_up_ref[rows, columns] = (grad_hidden * (cdf + up_val * pdf)).astype(BF16)
        put_rows(grad_refs, slice(at, at + WIDE), dot(normed_t_ref[...], grad_up_ref[:, columns]), place)
        put_rows(grad_refs, slice(count + at, count + at + WIDE), dot(cot_t_ref[...], hidden_ref[:, columns]), place)


def middle_first_kernel(
    n_pieces, core_ref, where_ref, act_ref, x_ref, cot_ref, cot_t_ref, vec_ref, *rest
):
    pieces, rest = rest[:n_pieces], rest[n_pieces:]
    (proj_ref, mid_ref, xhat_ref, inv_ref, normed_ref, normed_t_ref, back_ref), rest = rest[:7], rest[7:]
    *grad_refs, weights, hidden_ref, grad_up_ref, sem = rest
    copies = load_rows(where_ref, pieces, weights, sem)
    length, feats = x_ref.shape
    count = hidden_ref.shape[1]
    gain, bias = vec_ref[3:4, :], vec_ref[4:5, :]
    for copy in copies:
        copy.wait()
    proj_ref[...] = weights[:, :feats]
    for at in range(length // BLOCK):
        mid = x_ref[span(at), :].astype(F32) + dot(act_ref[span(at), :], proj_ref[...])
        xhat, inverse = norm_stats(mid)
        normed = (xhat * gain + bias).astype(BF16)
        mid_ref[span(at), :] = mid
        xhat_ref[span(at), :] = xhat
        inv_ref[span(at), :] = jnp.broadcast_to(inverse, (BLOCK, 128))
        normed_ref[span(at), :] = normed
        normed_t_ref[:, span(at)] = normed.T
    hidden_part(
        place_of(core_ref, grad_refs), normed_ref, normed_t_ref, cot_ref, cot_t_ref, feats, feats + count, weights,
        hidden_ref, grad_up_ref, grad_refs,
    )
    for row in range(0, length, TILE):
        rows = slice(row, row + TILE)
        mid_ref[rows, :] += dot(hidden_ref[rows, :], weights[:, feats + count :], NT)
        back_ref[rows, :] = dot(grad_up_ref[rows, :], weights[:, feats : feats + count], NT)


def middle_second_kernel(
    n_pieces, core_ref, where_ref, cot_ref, cot_t_ref, normed_ref, normed_t_ref, *rest
):
    pieces, rest = rest[:n_pieces], rest[n_pieces:]
    (hidden_ref, grad_up_ref, weights), rest = rest[:3], rest[3:]
    *grad_refs, sem = rest
    for copy in load_rows(where_ref, pieces, weights, sem):
        copy.wait()
    hidden_part(
        place_of(core_ref, grad_refs), normed_ref, normed_t_ref, cot_ref, cot_t_ref, 0, hidden_ref.shape[1], weights,
        hidden_ref, grad_up_ref, grad_refs,
    )


def middle_third_kernel(
    slope_ref, cot_ref, vec_ref, pool_rows, proj_ref, mid_ref, xhat_ref, inv_ref, back_ref,
    hidden_ref, grad_up_ref, weights, out_ref, mid_grad_ref, vec_grad_ref, pre_grad_ref, halo_ref,
):
    length, feats = mid_ref.shape
    count = hidden_ref.shape[1]
    gain = vec_ref[3:4, :]
    gain_grad = jnp.zeros((8, feats), F32)
    bias_grad = jnp.zeros((8, feats), F32)
    per = BLOCK // POOL
    for at in range(length // BLOCK):
        out_ref[span(at), :] = (
            mid_ref[span(at), :] + dot(hidden_ref[span(at), :], weights[:, count:], NT)
        ).astype(BF16)
        grad_normed = back_ref[span(at), :] + dot(grad_up_ref[span(at), :], weights[:, :count], NT)
        xhat = xhat_ref[span(at), :]
        bias_grad = bias_grad + jnp.sum(grad_normed.reshape(BLOCK // 8, 8, feats), axis=0)
        gain_grad = gain_grad + jnp.sum((grad_normed * xhat).reshape(BLOCK // 8, 8, feats), axis=0)
        grad_mid = cot_ref[span(at), :].astype(F32) + norm_back(
            xhat, inv_ref[span(at), 0:1], grad_normed * gain
        )
        mid_grad_ref[span(at), :] = grad_mid
        grad_act = dot(grad_mid.astype(BF16), proj_ref[...], NT)
        grad_pre = (grad_act * slope_ref[span(at), :].astype(F32)).astype(BF16)
        pre_grad_ref[span(at), :] = grad_pre
        if at == 0:
            halo_ref[0:BLOCK, :] = grad_pre
        halo_ref[pl.ds(BLOCK + at * per, per), :] = (
            dot(pool_rows[...], grad_pre) * np.float32(POOL)
        ).astype(BF16)
    vec_grad_ref[0:1, :] = jnp.sum(gain_grad, axis=0, keepdims=True)
    vec_grad_ref[1:2, :] = jnp.sum(bias_grad, axis=0, keepdims=True)
    vec_grad_ref[2:8, :] = jnp.zeros((6, feats), F32)


def taps_kernel(
    act_ref, mid_grad_ref, pre_grad_ref, halo_ref, win_ref, pool_win_ref, basis, fine_basis,
    coarse_basis, out_grad_ref, tap_grad_ref, z_ref, mid_bf_ref,
):
    length, feats = act_ref.shape
    blocks = length // BLOCK
    total = None
    for at in range(blocks):
        mid_bf_ref[span(at), :] = mid_grad_ref[span(at), :].astype(BF16)
        z = dot(basis[...], pre_grad_ref[span(at), :])
        z_ref[at] = z.astype(BF16)
        term = conj_product(quarters(win_ref[at]), quarters(z))
        total = term if total is None else [a + b for a, b in zip(total, term)]
    out_grad_ref[...] = dot(act_ref[...], mid_bf_ref[...], TN).astype(BF16)
    pooled = length // POOL
    z_pool = dot(basis[:, 0:pooled], halo_ref[BLOCK : BLOCK + pooled, :])
    pool_term = conj_product(quarters(pool_win_ref[...]), quarters(z_pool))
    tap_grad_ref[...] = (
        (dot(stacked(total), fine_basis[...], TN) + dot(stacked(pool_term), coarse_basis[...], TN))
        * np.float32(1 / FREQ)
    ).astype(BF16)


def backward_kernel(
    core_ref, z_ref, halo_ref, next_ref, pre_grad_ref, fine_h_ref, coarse_h_ref, basis, basis_t, back_pool,
    weights, vec_ref, vec_grad_ref, xhat_ref, xhat_t_ref, inv_ref, mid_grad_ref, out_grad_ref, tap_grad_ref, input_grad_ref, *rest
):
    *grad_refs, mixed_grad_ref, pool_ref = rest
    place = place_of(core_ref, grad_refs)
    length, feats = xhat_ref.shape
    blocks = length // BLOCK
    pooled = length // POOL
    gain, bias, skip = vec_ref[0:1, :], vec_ref[1:2, :], vec_ref[2:3, :]
    fine_q = quarters(fine_h_ref[...])
    pool_ref[0:pooled, :] = halo_ref[BLOCK : BLOCK + pooled, :]
    pool_ref[pooled : 2 * pooled, :] = next_ref[BLOCK : BLOCK + pooled, :]
    z_pool = quarters(dot(basis[...], pool_ref[...]))
    coarse_y = stacked([v * np.float32(1 / POOL) for v in conj_product(quarters(coarse_h_ref[...]), z_pool)])
    later = quarters(dot(basis[...], next_ref[0:BLOCK, :]))
    sums = jnp.zeros((8, feats), F32)
    for at in reversed(range(blocks)):
        now = quarters(z_ref[at])
        y = stacked(conj_product(fine_q, add_after(now, later)))
        later = now
        total = dot(basis_t[...], y) + dot(back_pool[span(at), :], coarse_y)
        grad_mixed = (
            total * np.float32(1 / FREQ) + skip * pre_grad_ref[span(at), :].astype(F32)
        ).astype(BF16)
        mixed_grad_ref[span(at), :] = grad_mixed
        sums = sums + jnp.sum(grad_mixed.astype(F32).reshape(BLOCK // 8, 8, feats), axis=0)
    back = dot(xhat_t_ref[...], mixed_grad_ref[...])
    mixed_sum = jnp.sum(sums, axis=0, keepdims=True)
    padded = jnp.concatenate([vec_ref[...], vec_grad_ref[...], jnp.zeros((112, feats), F32)], axis=0)
    columns = padded.T
    put_rows(grad_refs, slice(0, feats), columns[:, 0:1] * back + columns[:, 1:2] * mixed_sum, place)
    put_rows(grad_refs, slice(feats, 2 * feats), out_grad_ref[...], place)
    put_rows(grad_refs, slice(2 * feats, 2 * feats + 256), tap_grad_ref[...], place)
    proj = weights[:, 0:feats]
    proj_f = proj.astype(F32)
    gain_grad = jnp.sum(proj_f * back, axis=1, keepdims=True)
    bias_grad = jnp.sum(proj_f * mixed_sum, axis=1, keepdims=True)
    lane = lax.broadcasted_iota(jnp.int32, (feats, 128), 1)
    columns = jnp.where(lane == 0, gain_grad, jnp.where(lane == 1, bias_grad, columns))
    put_rows(grad_refs, slice(2 * feats + 256, 2 * feats + 384), columns, place)
    for at in range(blocks):
        grad_normed = dot(mixed_grad_ref[span(at), :], proj, NT)
        input_grad_ref[span(at), :] = mid_grad_ref[span(at), :] + norm_back(
            xhat_ref[span(at), :].astype(F32), inv_ref[span(at), 0:1], grad_normed * gain
        )


def call(kernel, operands, outs, scratch=(), flops=0, spaces=None, limit=12):
    spaces = spaces or [pltpu.VMEM] * len(operands)
    operands = [
        pltpu.with_memory_space_constraint(operand, pltpu.HBM) if space is pltpu.HBM else operand
        for operand, space in zip(operands, spaces)
    ]
    return pl.pallas_call(
        kernel,
        out_shape=[jax.ShapeDtypeStruct(shape, dtype) for shape, dtype in outs],
        in_specs=[pl.BlockSpec(memory_space=space) for space in spaces],
        out_specs=[pl.BlockSpec(memory_space=pltpu.VMEM)] * len(outs),
        scratch_shapes=list(scratch),
        compiler_params=pltpu.CompilerParams(vmem_limit_bytes=limit << 20),
        cost_estimate=pl.CostEstimate(flops=4 * flops, bytes_accessed=8 << 20, transcendentals=0),
    )(*operands)


def body(
    block_input,
    mixer_gain,
    mixer_bias,
    in_proj,
    kernel_param,
    skip_gain,
    out_proj,
    mlp_gain,
    mlp_bias,
    up_proj,
    down_proj,
    out_cotangent,
):
    core = lax.axis_index("seq")
    _, length, feats = block_input.shape
    hidden = up_proj.shape[1]
    half = hidden // 2
    blocks = length // BLOCK
    pooled = length // POOL
    taps = TAPS * SCALES
    own_rows = in_proj.shape[0]
    x_own, cot = block_input[0], out_cotangent[0]
    x_prior = lax.ppermute(x_own, "seq", [(0, 1)])
    vectors = [v.reshape(1, -1) for v in (mixer_gain, mixer_bias, skip_gain, mlp_gain, mlp_bias)]
    first, shard = call(
        pack_kernel,
        [in_proj, kernel_param, out_proj, up_proj, down_proj, *vectors],
        [((own_rows, PACK), BF16), ((own_rows, feats + 2 * hidden), BF16)],
        [
            pltpu.VMEM(kernel_param.shape, BF16), pltpu.VMEM((5, 1, own_rows), BF16),
            pltpu.SemaphoreType.DMA,
        ],
        spaces=[pltpu.HBM] * 10,
    )
    basis_np = odd_basis(np.arange(BLOCK))
    basis, basis_t = bf16_const(basis_np), bf16_const(basis_np.T)
    basis_pool = bf16_const(odd_basis(np.arange(-pooled, pooled)))
    back_pool = bf16_const(np.repeat(odd_basis(np.arange(pooled)).T, POOL, axis=0))
    fine_basis = bf16_const(tap_basis(0, 0))
    coarse_basis = bf16_const(tap_basis(OFFSET, TAPS * FINE))
    pool_rows = bf16_const(np.kron(np.eye(BLOCK // POOL), np.ones((1, POOL))) / POOL)
    scale_np = np.zeros((1, 256), np.float32)
    scale_np[0, :taps] = np.repeat(0.5 ** np.arange(SCALES), TAPS)
    wide_np = np.zeros((1, 256), np.float32)
    wide_np[0, :taps] = np.repeat(2.0 ** (np.arange(SCALES) % FINE), TAPS)

    xhat, xhat_t, inv_one, cot_t, cot, x_own = call(
        prepare_kernel,
        [x_own, cot],
        [
            ((length, feats), BF16), ((feats, length), BF16), ((length, 128), F32),
            ((feats, length), BF16), ((length, feats), BF16), ((length, feats), BF16),
        ],
        [pltpu.SemaphoreType.DMA((2, blocks))],
        spaces=[pltpu.HBM] * 2,
    )
    (prior_hat,) = call(prior_kernel, [x_prior], [((length, feats), BF16)])
    where = row_places()
    first = tie(gather_far(first), xhat, prior_hat)
    held = gather_far(tie(shard, xhat))
    first = gather_core(gather_near(first))
    held = tie(held, *first)
    first, first_at = in_order(first, where)
    held_a, held_b = held[:, :, : feats + 2 * half], held[:, :, feats + 2 * half :]
    pieces_a = gather_near(held_a)
    any_space, smem = pl.ANY, pltpu.SMEM
    core_at = jnp.stack([core, lax.axis_index("dp")]).astype(jnp.int32)
    n_first = len(first)
    weights, vec, fine_h, coarse_h, window, pool_win, act, slope = call(
        lambda *refs: forward_kernel(n_first, *refs),
        [
            core_at, first_at, xhat, prior_hat, basis, basis_t, basis_pool,
            back_pool, fine_basis, coarse_basis, pool_rows, jnp.asarray(scale_np), jnp.asarray(wide_np),
            *first,
        ],
        [
            ((feats, PACK), BF16), ((8, feats), F32), ((2 * FREQ, feats), F32),
            ((2 * FREQ, feats), F32), ((blocks, 2 * FREQ, feats), BF16), ((2 * FREQ, feats), BF16),
            ((length, feats), BF16), ((length, feats), BF16),
        ],
        [
            pltpu.VMEM((length, feats), BF16), pltpu.VMEM((2 * pooled, feats), BF16),
            pltpu.SemaphoreType.DMA,
        ],
        flops=6 << 30,
        spaces=[smem, smem] + [pltpu.VMEM] * 11 + [any_space] * n_first,
    )
    pieces_a, a_at = in_order(gather_core(list(tie(tuple(pieces_a), act))), where)
    pieces_b = gather_near(tie(held_b, act))
    n_a = len(pieces_a)
    rows = own_rows


    def grad_shapes(columns):
        if rows % 16 == 0:
            return [((feats // (2 * rows), rows, columns), BF16)] * 2
        return [((feats, columns), BF16)]

    token_f32, token_bf16 = ((length, feats), F32), ((length, feats), BF16)
    proj_out, mid, xhat_two, inv_two, normed, normed_t, back, *grads_a = call(
        lambda *refs: middle_first_kernel(n_a, *refs),
        [core_at, a_at, act, x_own, cot, cot_t, vec, *pieces_a],
        [
            ((feats, feats), BF16), token_f32, token_f32, ((length, 128), F32), token_bf16,
            ((feats, length), BF16), token_f32, *grad_shapes(2 * half),
        ],
        [
            pltpu.VMEM((feats, feats + 2 * half), BF16), pltpu.VMEM((length, half), BF16),
            pltpu.VMEM((length, half), BF16), pltpu.SemaphoreType.DMA,
        ],
        flops=8 << 30,
        spaces=[smem, smem] + [pltpu.VMEM] * 5 + [any_space] * n_a,
    )
    pieces_b, b_at = in_order(gather_core(list(tie(tuple(pieces_b), mid))), where)
    n_b = len(pieces_b)
    hidden_b, grad_up_b, weights_b, *grads_b = call(
        lambda *refs: middle_second_kernel(n_b, *refs),
        [core_at, b_at, cot, cot_t, normed, normed_t, *pieces_b],
        [((length, half), BF16), ((length, half), BF16), ((feats, 2 * half), BF16), *grad_shapes(2 * half)],
        [pltpu.SemaphoreType.DMA],
        flops=5 << 30,
        spaces=[smem, smem] + [pltpu.VMEM] * 4 + [any_space] * n_b,
    )
    near_a = reduce_core(grads_a)
    hidden_b = tie(hidden_b, *near_a)
    spread_a = spread_near(near_a)
    block_output, grad_mid, vec_grad, grad_pre, halo = call(
        middle_third_kernel,
        [
            slope, cot, vec, pool_rows, proj_out, mid, xhat_two, inv_two, back, hidden_b, grad_up_b,
            weights_b,
        ],
        [token_bf16, token_f32, ((8, feats), F32), token_bf16, ((BLOCK + pooled, feats), BF16)],
        flops=4 << 30,
    )
    after = lax.ppermute(halo, "seq", [(1, 0)])
    near_b = reduce_core(grads_b)
    grad_pre = tie(grad_pre, *near_b)
    spread_b = spread_near(near_b)
    out_grad, tap_grad, z_grad = call(
        taps_kernel,
        [act, grad_mid, grad_pre, halo, window, pool_win, basis, fine_basis, coarse_basis],
        [
            ((feats, feats), BF16), ((feats, 256), BF16), ((blocks, 2 * FREQ, feats), BF16),
        ],
        [pltpu.VMEM((length, feats), BF16)],
        flops=2 << 30,
    )
    part_a = add_up(tie(tuple(spread_a), z_grad), BF16)
    z_grad = tie(z_grad, part_a)
    far_a = spread_far(part_a)
    input_grad, *grads_c = call(
        backward_kernel,
        [
            core_at, z_grad, halo, after, grad_pre, fine_h, coarse_h, basis, basis_t, back_pool, weights,
            vec, vec_grad, xhat, xhat_t, inv_one, grad_mid, out_grad, tap_grad,
        ],
        [token_f32, *grad_shapes(2 * feats + 384)],
        [pltpu.VMEM((length, feats), BF16), pltpu.VMEM((2 * pooled, feats), BF16)],
        flops=4 << 30,
        spaces=[smem] + [pltpu.VMEM] * 18,
    )
    part_b = add_up(tie(tuple(spread_b), input_grad), BF16)
    far_b = spread_far(part_b)
    spread_c = spread_near(reduce_core(grads_c, part_b))
    far_c = spread_far(add_up(spread_c, BF16))
    sums_a, sums_b, mixer_sums = add_up(far_a), add_up(far_b), add_up(far_c)

    tap_rows = mixer_sums[:, 2 * feats : 2 * feats + taps]
    tap_scale, tap_wide = jnp.asarray(scale_np[:, :taps]), jnp.asarray(wide_np[:, :taps])
    raw = kernel_param.astype(F32) * tap_scale
    inverse = lax.rsqrt(jnp.sum(raw * raw * tap_wide, axis=1, keepdims=True) + 1e-05)
    own_taps = raw * inverse
    along = jnp.sum(tap_rows * own_taps, axis=1, keepdims=True)
    param_grad = tap_scale * inverse * (tap_rows - tap_wide * own_taps * along)
    tail = mixer_sums[:, 2 * feats + 256 :]
    return (
        block_output[None],
        input_grad[None],
        tail[:, 0],
        tail[:, 1],
        mixer_sums[:, :feats],
        param_grad,
        tap_rows[:, 0],
        mixer_sums[:, feats : 2 * feats],
        tail[:, 8],
        tail[:, 9],
        jnp.concatenate([sums_a[:, :half], sums_b[:, :half]], axis=1),
        jnp.concatenate([sums_a[:, half:], sums_b[:, half:]], axis=1),
    )


def solution(mesh):
    rows = P(("dp", "seq"), None)
    vector = P(("dp", "seq"))
    tokens = P("dp", "seq", None)
    return jax.shard_map(
        body,
        mesh=mesh,
        in_specs=(
            tokens, vector, vector, rows, rows, vector, rows, vector, vector, rows, rows, tokens,
        ),
        out_specs=(
            tokens, tokens, vector, vector, rows, rows, vector, rows, vector, vector, rows, rows,
        ),
        check_vma=False,
    )
```

```python
import math

import jax
import jax.numpy as jnp
import numpy as np
from jax import lax
from jax.experimental import pallas as pl
from jax.experimental.pallas import tpu as pltpu
from jax.sharding import PartitionSpec as P

TAPS = 32
SCALES = 6
FINE = 3
FREQ = 256
HALF = FREQ // 2
BLOCK = 256
POOL = 8
OFFSET = 28
TILE = 512
WIDE = 512
PACK = 768
F32 = jnp.float32
BF16 = jnp.bfloat16
NT = ((1,), (1,))
TN = ((0,), (0,))


def odd_basis(positions):
    order = np.concatenate([np.arange(0, FREQ, 2), np.arange(1, FREQ, 2)])
    angle = np.pi * np.outer(order + 0.5, positions) / FREQ
    return np.concatenate([np.cos(angle), -np.sin(angle)], axis=0)


def tap_basis(start, first):
    columns = np.zeros((2 * FREQ, 256))
    for scale_at in range(FINE):
        wide = 2**scale_at
        lag = start + TAPS * (wide - 1)
        for tap in range(TAPS):
            at = first + scale_at * TAPS + tap
            columns[:, at] = odd_basis(lag + tap * wide + np.arange(wide)).sum(axis=1)
    return columns


def bf16_const(array):
    return jnp.asarray(np.asarray(array, np.float32).astype(jnp.bfloat16))


def dot(a, b, contract=((1,), (0,))):
    return lax.dot_general(a, b, (contract, ((), ())), preferred_element_type=F32)


def normal_parts(values):
    cdf = 0.5 + 0.5 * lax.erf(values * np.float32(math.sqrt(0.5)))
    pdf = jnp.exp(-0.5 * values * values) * np.float32(1 / math.sqrt(2 * math.pi))
    return cdf, pdf


def split_dp(count):
    edge = round((count / 2) ** (1 / 3))
    return (2 * edge, edge * edge) if 2 * edge**3 == count else (1, count)


def swap_route(count, mask):
    return [(i, i ^ mask) for i in range(count)]


SWAP = [(0, 1), (1, 0)]


def tie(value, *others):
    return lax.optimization_barrier((value, *others))[0]


def far_steps():
    nz, _ = split_dp(lax.axis_size("dp"))
    return [1 << bit for bit in reversed(range(nz.bit_length() - 1))]


def from_line(held, step):
    dp_count = lax.axis_size("dp")
    _, nxy = split_dp(dp_count)
    return lax.ppermute(held, "dp", swap_route(dp_count, step * nxy))


def paired(held, got):
    return jnp.stack([held, got], axis=1).reshape((-1,) + held.shape[1:])


def gather_line(held, step):
    return paired(held, from_line(held, step))


def gather_far(shard):
    held = shard[None]
    for step in far_steps():
        held = gather_line(held, step)
    return held


def gather_near(held):
    dp_count = lax.axis_size("dp")
    _, nxy = split_dp(dp_count)
    return [held] + [lax.ppermute(held, "dp", swap_route(dp_count, k)) for k in range(1, nxy)]


def gather_core(pieces):
    held = jnp.concatenate(pieces)
    return [held, lax.ppermute(held, "seq", SWAP)]


def gather_plane(held):
    dp_count = lax.axis_size("dp")
    _, nxy = split_dp(dp_count)
    if nxy != 4:
        return gather_near(held)
    by_x = lax.ppermute(held, "dp", swap_route(dp_count, 1))
    by_y = lax.ppermute(held, "dp", swap_route(dp_count, 2))
    if held.shape[0] == 1:
        return [held, by_x, by_y, lax.ppermute(by_y, "dp", swap_route(dp_count, 1))]
    cut = held.shape[0] // 2
    return [
        held, by_x, by_y, lax.ppermute(by_y[:cut], "dp", swap_route(dp_count, 1)),
        lax.ppermute(by_x[cut:], "dp", swap_route(dp_count, 2)),
    ]


def row_place(at, count, plane_first, core_ref):
    nz, nxy = split_dp(count)
    other, at = divmod(at, count)
    if plane_first:
        z, xy = divmod(at, nxy)
    else:
        xy, z = divmod(at, nz)
    return ((z * nxy + xy) ^ core_ref[1]) * 2 + (other ^ core_ref[0])


def in_order(pieces, plane_first):
    if pieces[0].shape[1] % 16 == 0:
        return pieces
    dp_count = lax.axis_size("dp")
    nz, nxy = split_dp(dp_count)
    me, core = lax.axis_index("dp"), lax.axis_index("seq")
    by_dp = jnp.arange(dp_count).reshape(nz, nxy) ^ me
    by_dp = by_dp if plane_first else by_dp.T
    where = by_dp[None] * 2 + (jnp.arange(2)[:, None, None] ^ core)
    flat = jnp.concatenate(pieces)
    return [jnp.take(flat, jnp.argsort(where.reshape(-1)), axis=0).reshape(1, -1, flat.shape[2])]


def reduce_core(grads, *before):
    dp_count = lax.axis_size("dp")
    nz, nxy = split_dp(dp_count)
    if len(grads) == 1:
        core, me = lax.axis_index("seq"), lax.axis_index("dp")
        shaped = grads[0].reshape(dp_count, 2, -1, grads[0].shape[1])
        order = (jnp.arange(nz)[None, :] * nxy + jnp.arange(nxy)[:, None]) ^ me
        shaped = jnp.take(shaped, order.reshape(-1), axis=0)
        grads = [
            lax.dynamic_index_in_dim(shaped, 1 - core, 1, False),
            lax.dynamic_index_in_dim(shaped, core, 1, False),
        ]
    send, keep = grads
    got = lax.ppermute(send, "seq", SWAP)
    got = tie(got, *before)
    total = (keep.astype(F32) + got.astype(F32)).astype(BF16)
    return [total[k * nz : (k + 1) * nz] for k in range(nxy)]


def spread_near(pieces):
    dp_count = lax.axis_size("dp")
    return [pieces[0]] + [
        lax.ppermute(pieces[k], "dp", swap_route(dp_count, k)) for k in range(1, len(pieces))
    ]


def spread_far(part):
    dp_count = lax.axis_size("dp")
    nz, nxy = split_dp(dp_count)
    return [part[0]] + [
        lax.ppermute(part[k], "dp", swap_route(dp_count, k * nxy)) for k in range(1, nz)
    ]


def add_up(pieces, dtype=F32):
    total = pieces[0].astype(F32)
    for piece in pieces[1:]:
        total = total + piece.astype(F32)
    return total.astype(dtype)


def load_rows(core_ref, pieces, target, plane_first):
    if len(pieces) == 1:
        target[...] = pieces[0][0]
        return
    count = target.shape[0] // (2 * pieces[0].shape[1])
    at = 0
    for piece in pieces:
        held, rows, _ = piece.shape
        for i in range(held):
            start = row_place(at, count, plane_first, core_ref) * rows
            target[pl.ds(pl.multiple_of(start, 16), rows), :] = piece[i]
            at += 1


def span(at, size=BLOCK):
    return pl.ds(at * size, size)


def norm_stats(features):
    centre = features - jnp.mean(features, axis=-1, keepdims=True)
    inverse = lax.rsqrt(jnp.mean(centre * centre, axis=-1, keepdims=True) + 1e-05)
    return centre * inverse, inverse


def norm_back(xhat, inverse, scaled):
    return inverse * (
        scaled
        - jnp.mean(scaled, axis=-1, keepdims=True)
        - xhat * jnp.mean(scaled * xhat, axis=-1, keepdims=True)
    )


def quarters(spectrum):
    return [spectrum[i * HALF : (i + 1) * HALF].astype(F32) for i in range(4)]


def add_before(now, past):
    (re, ro, ie, io), (pre, pro, pie, pio) = now, past
    return re - pie, ro + pio, ie + pre, io - pro


def add_after(now, later):
    (re, ro, ie, io), (nre, nro, nie, nio) = now, later
    return re + nie, ro - nio, ie - nre, io + nro


def product(a, b):
    (are, aro, aie, aio), (bre, bro, bie, bio) = a, b
    return (
        are * bre - aie * bie,
        aro * bro - aio * bio,
        are * bie + aie * bre,
        aro * bio + aio * bro,
    )


def conj_product(a, b):
    (are, aro, aie, aio), (bre, bro, bie, bio) = a, b
    return (
        are * bre + aie * bie,
        aro * bro + aio * bio,
        are * bie - aie * bre,
        aro * bio - aio * bro,
    )


def stacked(parts):
    return jnp.concatenate([part.astype(BF16) for part in parts], axis=0)


def put_quarters(ref, at, parts):
    for i, part in enumerate(parts):
        ref[at, i * HALF : (i + 1) * HALF, :] = part.astype(ref.dtype)


def pack_kernel(core_ref, in_ref, param_ref, out_ref, up_ref, down_ref, *rest):
    vectors, (a_ref, b_ref, param, small, sem) = rest[:5], rest[5:]
    rows, feats = in_ref.shape
    half = up_ref.shape[1] // 2
    copies = [
        pltpu.make_async_copy(in_ref, a_ref.at[:, pl.ds(0, feats)], sem),
        pltpu.make_async_copy(param_ref, param, sem),
    ]
    for i, vector in enumerate(vectors):
        copies.append(pltpu.make_async_copy(vector, small.at[i], sem))
    for source, start, size, target, at in (
        (out_ref, 0, feats, a_ref, PACK), (up_ref, 0, half, a_ref, PACK + feats),
        (down_ref, 0, half, a_ref, PACK + feats + half), (up_ref, half, half, b_ref, 0),
        (down_ref, half, half, b_ref, half),
    ):
        copies.append(
            pltpu.make_async_copy(
                source.at[:, pl.ds(start, size)], target.at[:, pl.ds(at, size)], sem
            )
        )
    for copy in copies:
        copy.start()
    for copy in copies:
        copy.wait()
    spare = PACK - feats - param.shape[1]
    row = lax.broadcasted_iota(jnp.int32, (rows, rows), 0)
    lane = lax.broadcasted_iota(jnp.int32, (rows, rows), 1)
    slot = lax.broadcasted_iota(jnp.int32, (rows, spare), 1)
    block = jnp.zeros((rows, spare), F32)
    for i in range(len(vectors)):
        value = small[i].astype(F32)
        column = jnp.sum(jnp.where(row == lane, value, 0.0), axis=1, keepdims=True)
        block = jnp.where(slot == i, column, block)
    tail = jnp.concatenate([param[...].astype(F32), block], axis=1)
    a_ref[:, feats:PACK] = tail.astype(BF16)


def prepare_kernel(x_ref, cot_ref, xhat_ref, inv_ref, cot_t_ref, cot_copy, x_copy, sem):
    blocks = x_ref.shape[0] // BLOCK
    copies = []
    for source, target, which in ((x_ref, x_copy, 0), (cot_ref, cot_copy, 1)):
        for at in range(blocks):
            copies.append(
                pltpu.make_async_copy(source.at[span(at), :], target.at[span(at), :], sem.at[which, at])
            )
    for copy in copies:
        copy.start()
    for at in range(blocks):
        copies[at].wait()
        xhat, inverse = norm_stats(x_copy[span(at), :].astype(F32))
        xhat_ref[span(at), :] = xhat.astype(BF16)
        inv_ref[span(at), :] = jnp.broadcast_to(inverse, (BLOCK, 128))
    for at in range(blocks):
        copies[blocks + at].wait()
        cot_t_ref[:, span(at)] = cot_copy[span(at), :].T


def prior_kernel(x_ref, xhat_ref):
    for at in range(x_ref.shape[0] // BLOCK):
        xhat_ref[span(at), :] = norm_stats(x_ref[span(at), :].astype(F32))[0].astype(BF16)


def forward_kernel(
    n_pieces, core_ref, xhat_ref, prior_ref, basis, basis_t, basis_pool, back_pool,
    fine_basis, coarse_basis, pool_rows, scale_ref, wide_ref, *rest,
):
    pieces, rest = rest[:n_pieces], rest[n_pieces:]
    weights, vec_ref, fine_h_ref, coarse_h_ref, win_ref, pool_win_ref, act_ref, slope_ref = rest[:8]
    mixed_ref, pooled_ref = rest[8:]
    load_rows(core_ref, pieces, weights, False)
    feats = xhat_ref.shape[1]
    blocks = xhat_ref.shape[0] // BLOCK
    tail = weights[:, feats : feats + 256].astype(F32)
    raw = tail * scale_ref[...]
    inverse = lax.rsqrt(jnp.sum(raw * raw * wide_ref[...], axis=1, keepdims=True) + 1e-05)
    taps = (raw * inverse).astype(BF16)
    vec = tail[:, 128:256].T[64:72]
    vec_ref[...] = vec
    gain, bias, skip = vec[0:1], vec[1:2], vec[2:3]
    fine_h = dot(fine_basis[...], taps, NT)
    coarse_h = dot(coarse_basis[...], taps, NT)
    fine_h_ref[...] = fine_h.astype(BF16)
    coarse_h_ref[...] = coarse_h.astype(BF16)
    proj = weights[:, :feats]
    has_prior = core_ref[0].astype(F32)
    per = BLOCK // POOL
    past = None
    for at in range(blocks):
        normed = (prior_ref[span(at), :].astype(F32) * gain + bias).astype(BF16)
        mixed = (dot(normed, proj) * has_prior).astype(BF16)
        pooled_ref[span(at, per), :] = dot(pool_rows[...], mixed).astype(BF16)
        if at == blocks - 1:
            past = quarters(dot(basis[...], mixed))
    for at in range(blocks):
        normed = (xhat_ref[span(at), :].astype(F32) * gain + bias).astype(BF16)
        mixed = dot(normed, proj).astype(BF16)
        mixed_ref[span(at), :] = mixed
        pooled_ref[span(blocks + at, per), :] = dot(pool_rows[...], mixed).astype(BF16)
    pool_win = dot(basis_pool[...], pooled_ref[...])
    pool_win_ref[...] = pool_win.astype(BF16)
    coarse_y = stacked(product(quarters(coarse_h), quarters(pool_win)))
    fine_q = quarters(fine_h)
    for at in range(blocks):
        mixed = mixed_ref[span(at), :]
        now = quarters(dot(basis[...], mixed))
        window = add_before(now, past)
        past = now
        put_quarters(win_ref, at, window)
        total = dot(basis_t[...], stacked(product(fine_q, window)))
        total = total + dot(back_pool[span(at), :], coarse_y)
        pre_act = total * np.float32(1 / FREQ) + skip * mixed.astype(F32)
        cdf, pdf = normal_parts(pre_act)
        act_ref[span(at), :] = (pre_act * cdf).astype(BF16)
        slope_ref[span(at), :] = (cdf + pre_act * pdf).astype(BF16)


def place_of(core_ref, grad_refs):
    nz, nxy = split_dp(grad_refs[0].shape[0])
    return core_ref[0], core_ref[1] // nxy, core_ref[1] % nxy, nz, nxy


def put_rows(refs, columns, value, place):
    value = value.astype(BF16)
    if len(refs) == 1:
        refs[0][:, columns] = value
        return
    send_ref, keep_ref = refs
    count, rows, _ = send_ref.shape
    core, me_z, me_xy, nz, nxy = place
    for at in range(count):
        slot = ((at % nxy) ^ me_xy) * nz + ((at // nxy) ^ me_z)
        first = value[2 * at * rows : (2 * at + 1) * rows]
        second = value[(2 * at + 1) * rows : (2 * at + 2) * rows]
        send_ref[slot, :, columns] = jnp.where(core == 0, second, first)
        keep_ref[slot, :, columns] = jnp.where(core == 0, first, second)


def hidden_part(place, normed_ref, normed_t_ref, cot_ref, cot_t_ref, up_at, down_at, weights, hidden_ref, grad_up_ref, grad_refs):
    length = normed_ref.shape[0]
    count = hidden_ref.shape[1]
    for at in range(0, count, WIDE):
        columns = slice(at, at + WIDE)
        up = weights[:, up_at + at : up_at + at + WIDE]
        down = weights[:, down_at + at : down_at + at + WIDE]
        for row in range(0, length, TILE):
            rows = slice(row, row + TILE)
            up_val = dot(normed_ref[rows, :], up)
            grad_hidden = dot(cot_ref[rows, :], down)
            cdf, pdf = normal_parts(up_val)
            hidden_ref[rows, columns] = (up_val * cdf).astype(BF16)
            grad_up_ref[rows, columns] = (grad_hidden * (cdf + up_val * pdf)).astype(BF16)
        put_rows(grad_refs, slice(at, at + WIDE), dot(normed_t_ref[...], grad_up_ref[:, columns]), place)
        put_rows(grad_refs, slice(count + at, count + at + WIDE), dot(cot_t_ref[...], hidden_ref[:, columns]), place)


def middle_first_kernel(
    n_pieces, core_ref, act_ref, x_ref, cot_ref, cot_t_ref, vec_ref, *rest
):
    pieces, rest = rest[:n_pieces], rest[n_pieces:]
    (proj_ref, mid_ref, xhat_ref, inv_ref, normed_ref, normed_t_ref, hidden_ref, grad_up_ref), rest = rest[:8], rest[8:]
    weights, *grad_refs = rest
    load_rows(core_ref, pieces, weights, False)
    length, feats = x_ref.shape
    count = hidden_ref.shape[1]
    gain, bias = vec_ref[3:4, :], vec_ref[4:5, :]
    proj_ref[...] = weights[:, :feats]
    for at in range(length // BLOCK):
        mid = x_ref[span(at), :].astype(F32) + dot(act_ref[span(at), :], proj_ref[...])
        xhat, inverse = norm_stats(mid)
        normed = (xhat * gain + bias).astype(BF16)
        mid_ref[span(at), :] = mid
        xhat_ref[span(at), :] = xhat
        inv_ref[span(at), :] = jnp.broadcast_to(inverse, (BLOCK, 128))
        normed_ref[span(at), :] = normed
        normed_t_ref[:, span(at)] = normed.T
    hidden_part(
        place_of(core_ref, grad_refs), normed_ref, normed_t_ref, cot_ref, cot_t_ref, feats, feats + count,
        weights, hidden_ref, grad_up_ref, grad_refs,
    )


def middle_second_kernel(
    n_pieces, core_ref, cot_ref, cot_t_ref, normed_ref, normed_t_ref, *rest
):
    pieces, rest = rest[:n_pieces], rest[n_pieces:]
    hidden_ref, grad_up_ref, weights, *grad_refs = rest
    load_rows(core_ref, pieces, weights, True)
    hidden_part(
        place_of(core_ref, grad_refs), normed_ref, normed_t_ref, cot_ref, cot_t_ref, 0,
        hidden_ref.shape[1], weights, hidden_ref, grad_up_ref, grad_refs,
    )


def middle_third_kernel(
    slope_ref, cot_ref, vec_ref, pool_rows, proj_ref, xhat_ref, inv_ref, up_a_ref, up_b_ref, weights_a,
    weights_b, mid_grad_ref, vec_grad_ref, pre_grad_ref, halo_ref,
):
    length, feats = xhat_ref.shape
    count = up_a_ref.shape[1]
    gain = vec_ref[3:4, :]
    gain_grad = jnp.zeros((8, feats), F32)
    bias_grad = jnp.zeros((8, feats), F32)
    per = BLOCK // POOL
    for at in range(length // BLOCK):
        grad_normed = dot(up_a_ref[span(at), :], weights_a[:, feats : feats + count], NT)
        grad_normed = grad_normed + dot(up_b_ref[span(at), :], weights_b[:, :count], NT)
        xhat = xhat_ref[span(at), :]
        bias_grad = bias_grad + jnp.sum(grad_normed.reshape(BLOCK // 8, 8, feats), axis=0)
        gain_grad = gain_grad + jnp.sum((grad_normed * xhat).reshape(BLOCK // 8, 8, feats), axis=0)
        grad_mid = cot_ref[span(at), :].astype(F32) + norm_back(
            xhat, inv_ref[span(at), 0:1], grad_normed * gain
        )
        mid_grad_ref[span(at), :] = grad_mid
        grad_act = dot(grad_mid.astype(BF16), proj_ref[...], NT)
        grad_pre = (grad_act * slope_ref[span(at), :].astype(F32)).astype(BF16)
        pre_grad_ref[span(at), :] = grad_pre
        if at == 0:
            halo_ref[0:BLOCK, :] = grad_pre
        halo_ref[pl.ds(BLOCK + at * per, per), :] = (
            dot(pool_rows[...], grad_pre) * np.float32(POOL)
        ).astype(BF16)
    vec_grad_ref[0:1, :] = jnp.sum(gain_grad, axis=0, keepdims=True)
    vec_grad_ref[1:2, :] = jnp.sum(bias_grad, axis=0, keepdims=True)
    vec_grad_ref[2:8, :] = jnp.zeros((6, feats), F32)


def output_kernel(mid_ref, hidden_a_ref, hidden_b_ref, weights_a, weights_b, out_ref):
    length, feats = mid_ref.shape
    count = hidden_a_ref.shape[1]
    for at in range(length // BLOCK):
        total = mid_ref[span(at), :] + dot(hidden_a_ref[span(at), :], weights_a[:, feats + count :], NT)
        total = total + dot(hidden_b_ref[span(at), :], weights_b[:, count:], NT)
        out_ref[span(at), :] = total.astype(BF16)


def taps_kernel(
    act_ref, mid_grad_ref, pre_grad_ref, halo_ref, win_ref, pool_win_ref, basis, fine_basis,
    coarse_basis, out_grad_ref, tap_grad_ref, z_ref, mid_bf_ref,
):
    length, feats = act_ref.shape
    blocks = length // BLOCK
    total = None
    for at in range(blocks):
        mid_bf_ref[span(at), :] = mid_grad_ref[span(at), :].astype(BF16)
        z = dot(basis[...], pre_grad_ref[span(at), :])
        z_ref[at] = z.astype(BF16)
        term = conj_product(quarters(win_ref[at]), quarters(z))
        total = term if total is None else [a + b for a, b in zip(total, term)]
    out_grad_ref[...] = dot(act_ref[...], mid_bf_ref[...], TN).astype(BF16)
    pooled = length // POOL
    z_pool = dot(basis[:, 0:pooled], halo_ref[BLOCK : BLOCK + pooled, :])
    pool_term = conj_product(quarters(pool_win_ref[...]), quarters(z_pool))
    tap_grad_ref[...] = (
        (dot(stacked(total), fine_basis[...], TN) + dot(stacked(pool_term), coarse_basis[...], TN))
        * np.float32(1 / FREQ)
    ).astype(BF16)


def backward_kernel(
    core_ref, z_ref, halo_ref, next_ref, pre_grad_ref, fine_h_ref, coarse_h_ref, basis, basis_t, back_pool,
    weights, vec_ref, vec_grad_ref, xhat_ref, out_grad_ref, tap_grad_ref, mixed_grad_ref, *rest
):
    *grad_refs, pool_ref = rest
    place = place_of(core_ref, grad_refs)
    length, feats = xhat_ref.shape
    blocks = length // BLOCK
    pooled = length // POOL
    gain, bias, skip = vec_ref[0:1, :], vec_ref[1:2, :], vec_ref[2:3, :]
    fine_q = quarters(fine_h_ref[...])
    pool_ref[0:pooled, :] = halo_ref[BLOCK : BLOCK + pooled, :]
    pool_ref[pooled : 2 * pooled, :] = next_ref[BLOCK : BLOCK + pooled, :]
    z_pool = quarters(dot(basis[...], pool_ref[...]))
    coarse_y = stacked([v * np.float32(1 / POOL) for v in conj_product(quarters(coarse_h_ref[...]), z_pool)])
    later = quarters(dot(basis[...], next_ref[0:BLOCK, :]))
    sums = jnp.zeros((8, feats), F32)
    for at in reversed(range(blocks)):
        now = quarters(z_ref[at])
        y = stacked(conj_product(fine_q, add_after(now, later)))
        later = now
        total = dot(basis_t[...], y) + dot(back_pool[span(at), :], coarse_y)
        grad_mixed = (
            total * np.float32(1 / FREQ) + skip * pre_grad_ref[span(at), :].astype(F32)
        ).astype(BF16)
        mixed_grad_ref[span(at), :] = grad_mixed
        sums = sums + jnp.sum(grad_mixed.astype(F32).reshape(BLOCK // 8, 8, feats), axis=0)
    back = dot(xhat_ref[...], mixed_grad_ref[...], TN)
    mixed_sum = jnp.sum(sums, axis=0, keepdims=True)
    padded = jnp.concatenate([vec_ref[...], vec_grad_ref[...], jnp.zeros((112, feats), F32)], axis=0)
    columns = padded.T
    put_rows(grad_refs, slice(0, feats), columns[:, 0:1] * back + columns[:, 1:2] * mixed_sum, place)
    put_rows(grad_refs, slice(feats, 2 * feats), out_grad_ref[...], place)
    put_rows(grad_refs, slice(2 * feats, 2 * feats + 256), tap_grad_ref[...], place)
    proj = weights[:, 0:feats]
    proj_f = proj.astype(F32)
    gain_grad = jnp.sum(proj_f * back, axis=1, keepdims=True)
    bias_grad = jnp.sum(proj_f * mixed_sum, axis=1, keepdims=True)
    lane = lax.broadcasted_iota(jnp.int32, (feats, 128), 1)
    columns = jnp.where(lane == 0, gain_grad, jnp.where(lane == 1, bias_grad, columns))
    put_rows(grad_refs, slice(2 * feats + 256, 2 * feats + 384), columns, place)


def input_kernel(mixed_grad_ref, weights, vec_ref, xhat_ref, inv_ref, mid_grad_ref, input_grad_ref):
    length, feats = xhat_ref.shape
    proj = weights[:, 0:feats]
    for at in range(length // BLOCK):
        grad_normed = dot(mixed_grad_ref[span(at), :], proj, NT)
        input_grad_ref[span(at), :] = mid_grad_ref[span(at), :] + norm_back(
            xhat_ref[span(at), :].astype(F32), inv_ref[span(at), 0:1], grad_normed * vec_ref[0:1, :]
        )


def final_kernel(param_ref, scale_ref, wide_ref, *rest):
    sources, outs = rest[: len(rest) - 10], rest[len(rest) - 10 :]
    count = len(sources) // 2
    up_ref, down_ref, in_ref, out_ref, param_grad_ref = outs[:5]
    totals = []
    for group in range(2):
        total = sources[group * count][...].astype(F32)
        for k in range(1, count):
            total = total + sources[group * count + k][...].astype(F32)
        totals.append(total)
    mlp, mixer = totals
    half = mlp.shape[1] // 4
    up_ref[:, :half], up_ref[:, half:] = mlp[:, :half], mlp[:, 2 * half : 3 * half]
    down_ref[:, :half], down_ref[:, half:] = mlp[:, half : 2 * half], mlp[:, 3 * half :]
    feats = in_ref.shape[1]
    in_ref[...] = mixer[:, :feats]
    out_ref[...] = mixer[:, feats : 2 * feats]
    taps = param_ref.shape[1]
    tap_rows = mixer[:, 2 * feats : 2 * feats + taps]
    scale, wide = scale_ref[:, :taps], wide_ref[:, :taps]
    raw = param_ref[...].astype(F32) * scale
    inverse = lax.rsqrt(jnp.sum(raw * raw * wide, axis=1, keepdims=True) + 1e-05)
    own = raw * inverse
    along = jnp.sum(tap_rows * own, axis=1, keepdims=True)
    param_grad_ref[...] = scale * inverse * (tap_rows - wide * own * along)
    tail = mixer[:, 2 * feats + 256 :]
    rows = tail.shape[0]
    diagonal = lax.broadcasted_iota(jnp.int32, (rows, rows), 0) == lax.broadcasted_iota(
        jnp.int32, (rows, rows), 1
    )
    columns = (tail[:, 0:1], tail[:, 1:2], tap_rows[:, 0:1], tail[:, 8:9], tail[:, 9:10])
    for ref, column in zip(outs[5:], columns):
        ref[...] = jnp.sum(jnp.where(diagonal, column, 0.0), axis=0, keepdims=True)


def call(kernel, operands, outs, scratch=(), flops=0, spaces=None, limit=12):
    spaces = spaces or [pltpu.VMEM] * len(operands)
    operands = [
        pltpu.with_memory_space_constraint(operand, pltpu.HBM) if space is pltpu.HBM else operand
        for operand, space in zip(operands, spaces)
    ]
    return pl.pallas_call(
        kernel,
        out_shape=[jax.ShapeDtypeStruct(shape, dtype) for shape, dtype in outs],
        in_specs=[pl.BlockSpec(memory_space=space) for space in spaces],
        out_specs=[pl.BlockSpec(memory_space=pltpu.VMEM)] * len(outs),
        scratch_shapes=list(scratch),
        compiler_params=pltpu.CompilerParams(vmem_limit_bytes=limit << 20),
        cost_estimate=pl.CostEstimate(flops=flops, bytes_accessed=1 << 16, transcendentals=0),
    )(*operands)


def body(
    block_input,
    mixer_gain,
    mixer_bias,
    in_proj,
    kernel_param,
    skip_gain,
    out_proj,
    mlp_gain,
    mlp_bias,
    up_proj,
    down_proj,
    out_cotangent,
):
    _, length, feats = block_input.shape
    hidden = up_proj.shape[1]
    half = hidden // 2
    blocks = length // BLOCK
    pooled = length // POOL
    taps = TAPS * SCALES
    own_rows = in_proj.shape[0]
    x_own, cot = block_input[0], out_cotangent[0]
    core_at = jnp.stack([lax.axis_index("seq"), lax.axis_index("dp")]).astype(jnp.int32)
    x_prior = lax.ppermute(x_own, "seq", [(0, 1)])
    vectors = [v.reshape(1, -1) for v in (mixer_gain, mixer_bias, skip_gain, mlp_gain, mlp_bias)]
    shard, shard_b = call(
        pack_kernel,
        [core_at, in_proj, kernel_param, out_proj, up_proj, down_proj, *vectors],
        [((own_rows, PACK + feats + 2 * half), BF16), ((own_rows, 2 * half), BF16)],
        [
            pltpu.VMEM(kernel_param.shape, BF16), pltpu.VMEM((5, 1, own_rows), BF16),
            pltpu.SemaphoreType.DMA,
        ],
        spaces=[pltpu.SMEM] + [pltpu.HBM] * 10,
    )
    basis_np = odd_basis(np.arange(BLOCK))
    basis, basis_t = bf16_const(basis_np), bf16_const(basis_np.T)
    basis_pool = bf16_const(odd_basis(np.arange(-pooled, pooled)))
    back_pool = bf16_const(np.repeat(odd_basis(np.arange(pooled)).T, POOL, axis=0))
    fine_basis = bf16_const(tap_basis(0, 0))
    coarse_basis = bf16_const(tap_basis(OFFSET, TAPS * FINE))
    pool_rows = bf16_const(np.kron(np.eye(BLOCK // POOL), np.ones((1, POOL))) / POOL)
    scale_np = np.zeros((1, 256), np.float32)
    scale_np[0, :taps] = np.repeat(0.5 ** np.arange(SCALES), TAPS)
    wide_np = np.zeros((1, 256), np.float32)
    wide_np[0, :taps] = np.repeat(2.0 ** (np.arange(SCALES) % FINE), TAPS)

    xhat, inv_one, cot_t = call(
        prepare_kernel,
        [x_own, cot],
        [((length, feats), BF16), ((length, 128), F32), ((feats, length), BF16)],
        [
            pltpu.VMEM((length, feats), BF16), pltpu.VMEM((length, feats), BF16),
            pltpu.SemaphoreType.DMA((2, blocks)),
        ],
        spaces=[pltpu.HBM] * 2,
    )
    (prior_hat,) = call(prior_kernel, [x_prior], [((length, feats), BF16)])
    held_b = jnp.concatenate(gather_plane(tie(shard_b, prior_hat)[None]))
    held = shard[None]
    for at, step in enumerate(far_steps()):
        got = from_line(held, step)
        got = tie(got, xhat) if at == 0 else got
        held = paired(held, got)
    held = tie(held, xhat, prior_hat, held_b)
    steps = far_steps()
    held_b = held_b[None]
    for step in steps[:-1]:
        held_b = gather_line(held_b, step)
    xhat_in = tie(xhat, held_b)
    first, held_a = held[:, :, :PACK], held[:, :, PACK:]
    first = gather_near(first)
    pieces_a = gather_plane(held_a)
    first = in_order(gather_core(first), False)
    smem = pltpu.SMEM
    n_first = len(first)
    weights, vec, fine_h, coarse_h, window, pool_win, act, slope = call(
        lambda *refs: forward_kernel(n_first, *refs),
        [
            core_at, xhat_in, prior_hat, basis, basis_t, basis_pool,
            back_pool, fine_basis, coarse_basis, pool_rows, jnp.asarray(scale_np), jnp.asarray(wide_np),
            *first,
        ],
        [
            ((feats, PACK), BF16), ((8, feats), F32), ((2 * FREQ, feats), BF16),
            ((2 * FREQ, feats), BF16), ((blocks, 2 * FREQ, feats), BF16), ((2 * FREQ, feats), BF16),
            ((length, feats), BF16), ((length, feats), BF16),
        ],
        [
            pltpu.VMEM((length, feats), BF16), pltpu.VMEM((2 * pooled, feats), BF16),
        ],
        flops=6 << 30,
        spaces=[smem] + [pltpu.VMEM] * (11 + n_first),
    )
    got_b = [from_line(held_b, step) for step in steps[-1:]]
    pieces_a = in_order(gather_core(list(tie(tuple(pieces_a), act))), False)
    n_a = len(pieces_a)
    rows = own_rows


    def grad_shapes(columns):
        if rows % 16 == 0:
            return [((feats // (2 * rows), rows, columns), BF16)] * 2
        return [((feats, columns), BF16)]

    token_f32, token_bf16 = ((length, feats), F32), ((length, feats), BF16)
    vmem = pltpu.VMEM
    proj_out, mid, xhat_two, inv_two, normed, normed_t, hidden_a, grad_up_a, weights_a, *grads_a = call(
        lambda *refs: middle_first_kernel(n_a, *refs),
        [core_at, act, x_own, cot, cot_t, vec, *pieces_a],
        [
            ((feats, feats), BF16), token_f32, token_f32, ((length, 128), F32), token_bf16,
            ((feats, length), BF16), ((length, half), BF16), ((length, half), BF16),
            ((feats, feats + 2 * half), BF16), *grad_shapes(2 * half),
        ],
        flops=8 << 30,
        spaces=[smem] + [vmem] * (5 + n_a),
    )
    for got in got_b:
        held_b = paired(held_b, tie(got, mid))
    held_b = held_b.reshape((-1,) + held_b.shape[2:])
    pieces_b = in_order(gather_core([held_b]), True)
    n_b = len(pieces_b)
    hidden_b, grad_up_b, weights_b, *grads_b = call(
        lambda *refs: middle_second_kernel(n_b, *refs),
        [core_at, cot, cot_t, normed, normed_t, *pieces_b],
        [((length, half), BF16), ((length, half), BF16), ((feats, 2 * half), BF16), *grad_shapes(2 * half)],
        flops=5 << 24,
        spaces=[smem] + [vmem] * (4 + n_b),
    )
    near_a = reduce_core(grads_a)
    grad_up_b = tie(grad_up_b, *near_a)
    spread_a = spread_near(near_a)
    grad_mid, vec_grad, grad_pre, halo = call(
        middle_third_kernel,
        [slope, cot, vec, pool_rows, proj_out, xhat_two, inv_two, grad_up_a, grad_up_b, weights_a, weights_b],
        [token_f32, ((8, feats), F32), token_bf16, ((BLOCK + pooled, feats), BF16)],
        flops=4 << 24,
    )
    after = lax.ppermute(halo, "seq", [(1, 0)])
    near_b = reduce_core(grads_b)
    grad_pre = tie(grad_pre, *near_b)
    spread_b = spread_near(near_b)
    out_grad, tap_grad, z_grad = call(
        taps_kernel,
        [act, grad_mid, grad_pre, halo, window, pool_win, basis, fine_basis, coarse_basis],
        [
            ((feats, feats), BF16), ((feats, 256), BF16), ((blocks, 2 * FREQ, feats), BF16),
        ],
        [pltpu.VMEM((length, feats), BF16)],
        flops=2 << 24,
    )
    z_grad = tie(z_grad, after)
    grad_mixed, *grads_c = call(
        backward_kernel,
        [
            core_at, z_grad, halo, after, grad_pre, fine_h, coarse_h, basis, basis_t, back_pool, weights,
            vec, vec_grad, xhat, out_grad, tap_grad,
        ],
        [token_bf16, *grad_shapes(2 * feats + 384)],
        [pltpu.VMEM((2 * pooled, feats), BF16)],
        flops=4 << 24,
        spaces=[smem] + [vmem] * 15,
    )
    (input_grad,) = call(
        input_kernel, [grad_mixed, weights, vec, xhat, inv_one, grad_mid], [token_f32], flops=2 << 24
    )
    part_a = add_up(tie(tuple(spread_a), grad_mixed), BF16)
    part_b = add_up(tie(tuple(spread_b), grad_mixed), BF16)
    part_ab = jnp.concatenate([part_a, part_b], axis=2)
    far_ab = spread_far(part_ab)
    near_c = reduce_core(grads_c, part_ab, input_grad)
    spread_c = spread_near(near_c)
    (block_output,) = call(
        output_kernel, [tie(mid, *near_c), hidden_a, hidden_b, weights_a, weights_b], [token_bf16], flops=4 << 24
    )
    far_c = spread_far(add_up(tie(tuple(spread_c), block_output), BF16))
    vector = ((1, rows), F32)
    up_sum, down_sum, in_sum, out_sum, param_sum, *vectors = call(
        final_kernel,
        [kernel_param, jnp.asarray(scale_np), jnp.asarray(wide_np), *far_ab, *far_c],
        [
            ((rows, hidden), F32), ((rows, hidden), F32), ((rows, feats), F32), ((rows, feats), F32),
            ((rows, taps), F32), vector, vector, vector, vector, vector,
        ],
    )
    gain_one, bias_one, skip_sum, gain_two, bias_two = (v.reshape(rows) for v in vectors)
    return (
        block_output[None], input_grad[None], gain_one, bias_one, in_sum, param_sum, skip_sum, out_sum,
        gain_two, bias_two, up_sum, down_sum,
    )


def solution(mesh):
    rows = P(("dp", "seq"), None)
    vector = P(("dp", "seq"))
    tokens = P("dp", "seq", None)
    return jax.shard_map(
        body,
        mesh=mesh,
        in_specs=(
            tokens, vector, vector, rows, rows, vector, rows, vector, vector, rows, rows, tokens,
        ),
        out_specs=(
            tokens, tokens, vector, vector, rows, rows, vector, rows, vector, vector, rows, rows,
        ),
        check_vma=False,
    )
```

```python
import math

import jax
import jax.numpy as jnp
import numpy as np
from jax import lax
from jax.experimental import pallas as pl
from jax.experimental.pallas import tpu as pltpu
from jax.sharding import PartitionSpec as P

TAPS = 32
SCALES = 6
FINE = 3
FREQ = 256
HALF = FREQ // 2
BLOCK = 256
POOL = 8
OFFSET = 28
TILE = 512
WIDE = 512
PACK = 768
F32 = jnp.float32
BF16 = jnp.bfloat16
NT = ((1,), (1,))
TN = ((0,), (0,))


def odd_basis(positions):
    order = np.concatenate([np.arange(0, FREQ, 2), np.arange(1, FREQ, 2)])
    angle = np.pi * np.outer(order + 0.5, positions) / FREQ
    return np.concatenate([np.cos(angle), -np.sin(angle)], axis=0)


def tap_basis(start, first):
    columns = np.zeros((2 * FREQ, 256))
    for scale_at in range(FINE):
        wide = 2**scale_at
        lag = start + TAPS * (wide - 1)
        for tap in range(TAPS):
            at = first + scale_at * TAPS + tap
            columns[:, at] = odd_basis(lag + tap * wide + np.arange(wide)).sum(axis=1)
    return columns


def bf16_const(array):
    return jnp.asarray(np.asarray(array, np.float32).astype(jnp.bfloat16))


def dot(a, b, contract=((1,), (0,))):
    return lax.dot_general(a, b, (contract, ((), ())), preferred_element_type=F32)


def normal_parts(values):
    cdf = 0.5 + 0.5 * lax.erf(values * np.float32(math.sqrt(0.5)))
    pdf = jnp.exp(-0.5 * values * values) * np.float32(1 / math.sqrt(2 * math.pi))
    return cdf, pdf


def split_dp(count):
    edge = round((count / 2) ** (1 / 3))
    return (2 * edge, edge * edge) if 2 * edge**3 == count else (1, count)


def swap_route(count, mask):
    return [(i, i ^ mask) for i in range(count)]


SWAP = [(0, 1), (1, 0)]


def tie(value, *others):
    return lax.optimization_barrier((value, *others))[0]


def far_steps():
    nz, _ = split_dp(lax.axis_size("dp"))
    return [1 << bit for bit in reversed(range(nz.bit_length() - 1))]


def from_line(held, step):
    dp_count = lax.axis_size("dp")
    _, nxy = split_dp(dp_count)
    return lax.ppermute(held, "dp", swap_route(dp_count, step * nxy))


def paired(held, got):
    return jnp.stack([held, got], axis=1).reshape((-1,) + held.shape[1:])


def gather_line(held, step):
    return paired(held, from_line(held, step))


def gather_far(shard):
    held = shard[None]
    for step in far_steps():
        held = gather_line(held, step)
    return held


def gather_near(held):
    dp_count = lax.axis_size("dp")
    _, nxy = split_dp(dp_count)
    return [held] + [lax.ppermute(held, "dp", swap_route(dp_count, k)) for k in range(1, nxy)]


def gather_core(pieces, parts=1):
    held = jnp.concatenate(pieces)
    size = held.shape[0] // parts
    held = [held[at * size : (at + 1) * size] for at in range(parts)]
    return held + [lax.ppermute(part, "seq", SWAP) for part in held]


def gather_plane(held):
    dp_count = lax.axis_size("dp")
    _, nxy = split_dp(dp_count)
    if nxy != 4:
        return gather_near(held)
    by_x = lax.ppermute(held, "dp", swap_route(dp_count, 1))
    by_y = lax.ppermute(held, "dp", swap_route(dp_count, 2))
    if held.shape[0] == 1:
        return [held, by_x, by_y, lax.ppermute(by_y, "dp", swap_route(dp_count, 1))]
    cut = held.shape[0] // 2
    return [
        held, by_x, by_y, lax.ppermute(by_y[:cut], "dp", swap_route(dp_count, 1)),
        lax.ppermute(by_x[cut:], "dp", swap_route(dp_count, 2)),
    ]


def row_place(at, count, plane_first, core_ref):
    nz, nxy = split_dp(count)
    other, at = divmod(at, count)
    if plane_first:
        z, xy = divmod(at, nxy)
    else:
        xy, z = divmod(at, nz)
    return ((z * nxy + xy) ^ core_ref[1]) * 2 + (other ^ core_ref[0])


def in_order(pieces, plane_first):
    if pieces[0].shape[1] % 16 == 0:
        return pieces
    dp_count = lax.axis_size("dp")
    nz, nxy = split_dp(dp_count)
    me, core = lax.axis_index("dp"), lax.axis_index("seq")
    by_dp = jnp.arange(dp_count).reshape(nz, nxy) ^ me
    by_dp = by_dp if plane_first else by_dp.T
    where = by_dp[None] * 2 + (jnp.arange(2)[:, None, None] ^ core)
    flat = jnp.concatenate(pieces)
    return [jnp.take(flat, jnp.argsort(where.reshape(-1)), axis=0).reshape(1, -1, flat.shape[2])]


def reduce_core(grads, *before):
    dp_count = lax.axis_size("dp")
    nz, nxy = split_dp(dp_count)
    if len(grads) == 1:
        core, me = lax.axis_index("seq"), lax.axis_index("dp")
        shaped = grads[0].reshape(dp_count, 2, -1, grads[0].shape[1])
        order = (jnp.arange(nz)[None, :] * nxy + jnp.arange(nxy)[:, None]) ^ me
        shaped = jnp.take(shaped, order.reshape(-1), axis=0)
        grads = [
            lax.dynamic_index_in_dim(shaped, 1 - core, 1, False),
            lax.dynamic_index_in_dim(shaped, core, 1, False),
        ]
    send, keep = grads
    got = lax.ppermute(send, "seq", SWAP)
    got = tie(got, *before)
    total = (keep.astype(F32) + got.astype(F32)).astype(BF16)
    return [total[k * nz : (k + 1) * nz] for k in range(nxy)]


def spread_near(pieces):
    dp_count = lax.axis_size("dp")
    return [pieces[0]] + [
        lax.ppermute(pieces[k], "dp", swap_route(dp_count, k)) for k in range(1, len(pieces))
    ]


def spread_far(part):
    dp_count = lax.axis_size("dp")
    nz, nxy = split_dp(dp_count)
    return [part[0]] + [
        lax.ppermute(part[k], "dp", swap_route(dp_count, k * nxy)) for k in range(1, nz)
    ]


def add_up(pieces, dtype=F32):
    total = pieces[0].astype(F32)
    for piece in pieces[1:]:
        total = total + piece.astype(F32)
    return total.astype(dtype)


def load_rows(core_ref, pieces, target, plane_first):
    if len(pieces) == 1:
        target[...] = pieces[0][0]
        return
    count = target.shape[0] // (2 * pieces[0].shape[1])
    at = 0
    for piece in pieces:
        held, rows, _ = piece.shape
        for i in range(held):
            start = row_place(at, count, plane_first, core_ref) * rows
            target[pl.ds(pl.multiple_of(start, 16), rows), :] = piece[i]
            at += 1


def span(at, size=BLOCK):
    return pl.ds(at * size, size)


def norm_stats(features):
    centre = features - jnp.mean(features, axis=-1, keepdims=True)
    inverse = lax.rsqrt(jnp.mean(centre * centre, axis=-1, keepdims=True) + 1e-05)
    return centre * inverse, inverse


def norm_back(xhat, inverse, scaled):
    return inverse * (
        scaled
        - jnp.mean(scaled, axis=-1, keepdims=True)
        - xhat * jnp.mean(scaled * xhat, axis=-1, keepdims=True)
    )


def quarters(spectrum):
    return [spectrum[i * HALF : (i + 1) * HALF].astype(F32) for i in range(4)]


def add_before(now, past):
    (re, ro, ie, io), (pre, pro, pie, pio) = now, past
    return re - pie, ro + pio, ie + pre, io - pro


def add_after(now, later):
    (re, ro, ie, io), (nre, nro, nie, nio) = now, later
    return re + nie, ro - nio, ie - nre, io + nro


def product(a, b):
    (are, aro, aie, aio), (bre, bro, bie, bio) = a, b
    return (
        are * bre - aie * bie,
        aro * bro - aio * bio,
        are * bie + aie * bre,
        aro * bio + aio * bro,
    )


def conj_product(a, b):
    (are, aro, aie, aio), (bre, bro, bie, bio) = a, b
    return (
        are * bre + aie * bie,
        aro * bro + aio * bio,
        are * bie - aie * bre,
        aro * bio - aio * bro,
    )


def stacked(parts):
    return jnp.concatenate([part.astype(BF16) for part in parts], axis=0)


def put_quarters(ref, at, parts):
    for i, part in enumerate(parts):
        ref[at, i * HALF : (i + 1) * HALF, :] = part.astype(ref.dtype)


def first_part(hidden):
    return hidden // 2


def pack_kernel(core_ref, in_ref, param_ref, out_ref, up_ref, down_ref, *rest):
    vectors, (a_ref, b_ref, param, small, sem) = rest[:5], rest[5:]
    rows, feats = in_ref.shape
    cut = first_part(up_ref.shape[1])
    left = up_ref.shape[1] - cut
    copies = [
        pltpu.make_async_copy(in_ref, a_ref.at[:, pl.ds(0, feats)], sem),
        pltpu.make_async_copy(param_ref, param, sem),
    ]
    for i, vector in enumerate(vectors):
        copies.append(pltpu.make_async_copy(vector, small.at[i], sem))
    for source, start, size, target, at in (
        (out_ref, 0, feats, a_ref, PACK), (up_ref, 0, cut, a_ref, PACK + feats),
        (down_ref, 0, cut, a_ref, PACK + feats + cut), (up_ref, cut, left, b_ref, 0),
        (down_ref, cut, left, b_ref, left),
    ):
        copies.append(
            pltpu.make_async_copy(
                source.at[:, pl.ds(start, size)], target.at[:, pl.ds(at, size)], sem
            )
        )
    for copy in copies:
        copy.start()
    for copy in copies:
        copy.wait()
    spare = PACK - feats - param.shape[1]
    row = lax.broadcasted_iota(jnp.int32, (rows, rows), 0)
    lane = lax.broadcasted_iota(jnp.int32, (rows, rows), 1)
    slot = lax.broadcasted_iota(jnp.int32, (rows, spare), 1)
    block = jnp.zeros((rows, spare), F32)
    for i in range(len(vectors)):
        value = small[i].astype(F32)
        column = jnp.sum(jnp.where(row == lane, value, 0.0), axis=1, keepdims=True)
        block = jnp.where(slot == i, column, block)
    tail = jnp.concatenate([param[...].astype(F32), block], axis=1)
    a_ref[:, feats:PACK] = tail.astype(BF16)


def prepare_kernel(x_ref, cot_ref, xhat_ref, inv_ref, cot_t_ref, cot_copy, x_copy, sem):
    blocks = x_ref.shape[0] // BLOCK
    copies = []
    for source, target, which in ((x_ref, x_copy, 0), (cot_ref, cot_copy, 1)):
        for at in range(blocks):
            copies.append(
                pltpu.make_async_copy(source.at[span(at), :], target.at[span(at), :], sem.at[which, at])
            )
    for copy in copies:
        copy.start()
    for at in range(blocks):
        copies[at].wait()
        xhat, inverse = norm_stats(x_copy[span(at), :].astype(F32))
        xhat_ref[span(at), :] = xhat.astype(BF16)
        inv_ref[span(at), :] = jnp.broadcast_to(inverse, (BLOCK, 128))
    for at in range(blocks):
        copies[blocks + at].wait()
        cot_t_ref[:, span(at)] = cot_copy[span(at), :].T


def prior_kernel(x_ref, xhat_ref):
    for at in range(x_ref.shape[0] // BLOCK):
        xhat_ref[span(at), :] = norm_stats(x_ref[span(at), :].astype(F32))[0].astype(BF16)


def forward_kernel(
    n_pieces, core_ref, xhat_ref, prior_ref, basis, basis_t, basis_pool, back_pool,
    fine_basis, coarse_basis, pool_rows, scale_ref, wide_ref, *rest,
):
    pieces, rest = rest[:n_pieces], rest[n_pieces:]
    weights, vec_ref, fine_h_ref, coarse_h_ref, win_ref, pool_win_ref, act_ref, slope_ref = rest[:8]
    mixed_ref, pooled_ref = rest[8:]
    load_rows(core_ref, pieces, weights, False)
    feats = xhat_ref.shape[1]
    blocks = xhat_ref.shape[0] // BLOCK
    tail = weights[:, feats : feats + 256].astype(F32)
    raw = tail * scale_ref[...]
    inverse = lax.rsqrt(jnp.sum(raw * raw * wide_ref[...], axis=1, keepdims=True) + 1e-05)
    taps = (raw * inverse).astype(BF16)
    vec = tail[:, 128:256].T[64:72]
    vec_ref[...] = vec
    gain, bias, skip = vec[0:1], vec[1:2], vec[2:3]
    fine_h = dot(fine_basis[...], taps, NT)
    coarse_h = dot(coarse_basis[...], taps, NT)
    fine_h_ref[...] = fine_h.astype(BF16)
    coarse_h_ref[...] = coarse_h.astype(BF16)
    proj = weights[:, :feats]
    has_prior = core_ref[0].astype(F32)
    per = BLOCK // POOL
    past = None
    for at in range(blocks):
        normed = (prior_ref[span(at), :].astype(F32) * gain + bias).astype(BF16)
        mixed = (dot(normed, proj) * has_prior).astype(BF16)
        pooled_ref[span(at, per), :] = dot(pool_rows[...], mixed).astype(BF16)
        if at == blocks - 1:
            past = quarters(dot(basis[...], mixed))
    for at in range(blocks):
        normed = (xhat_ref[span(at), :].astype(F32) * gain + bias).astype(BF16)
        mixed = dot(normed, proj).astype(BF16)
        mixed_ref[span(at), :] = mixed
        pooled_ref[span(blocks + at, per), :] = dot(pool_rows[...], mixed).astype(BF16)
    pool_win = dot(basis_pool[...], pooled_ref[...])
    pool_win_ref[...] = pool_win.astype(BF16)
    coarse_y = stacked(product(quarters(coarse_h), quarters(pool_win)))
    fine_q = quarters(fine_h)
    for at in range(blocks):
        mixed = mixed_ref[span(at), :]
        now = quarters(dot(basis[...], mixed))
        window = add_before(now, past)
        past = now
        put_quarters(win_ref, at, window)
        total = dot(basis_t[...], stacked(product(fine_q, window)))
        total = total + dot(back_pool[span(at), :], coarse_y)
        pre_act = total * np.float32(1 / FREQ) + skip * mixed.astype(F32)
        cdf, pdf = normal_parts(pre_act)
        act_ref[span(at), :] = (pre_act * cdf).astype(BF16)
        slope_ref[span(at), :] = (cdf + pre_act * pdf).astype(BF16)


def place_of(core_ref, grad_refs):
    nz, nxy = split_dp(grad_refs[0].shape[0])
    return core_ref[0], core_ref[1] // nxy, core_ref[1] % nxy, nz, nxy


def put_rows(refs, columns, value, place):
    value = value.astype(BF16)
    if len(refs) == 1:
        refs[0][:, columns] = value
        return
    send_ref, keep_ref = refs
    count, rows, _ = send_ref.shape
    core, me_z, me_xy, nz, nxy = place
    for at in range(count):
        slot = ((at % nxy) ^ me_xy) * nz + ((at // nxy) ^ me_z)
        first = value[2 * at * rows : (2 * at + 1) * rows]
        second = value[(2 * at + 1) * rows : (2 * at + 2) * rows]
        send_ref[slot, :, columns] = jnp.where(core == 0, second, first)
        keep_ref[slot, :, columns] = jnp.where(core == 0, first, second)


def hidden_part(place, normed_ref, normed_t_ref, cot_ref, cot_t_ref, up_at, down_at, weights, hidden_ref, grad_up_ref, grad_refs):
    length = normed_ref.shape[0]
    count = hidden_ref.shape[1]
    for at in range(0, count, WIDE):
        wide = min(WIDE, count - at)
        columns = slice(at, at + wide)
        up = weights[:, up_at + at : up_at + at + wide]
        down = weights[:, down_at + at : down_at + at + wide]
        for row in range(0, length, TILE):
            rows = slice(row, row + TILE)
            up_val = dot(normed_ref[rows, :], up)
            grad_hidden = dot(cot_ref[rows, :], down)
            cdf, pdf = normal_parts(up_val)
            hidden_ref[rows, columns] = (up_val * cdf).astype(BF16)
            grad_up_ref[rows, columns] = (grad_hidden * (cdf + up_val * pdf)).astype(BF16)
        put_rows(grad_refs, slice(at, at + wide), dot(normed_t_ref[...], grad_up_ref[:, columns]), place)
        put_rows(grad_refs, slice(count + at, count + at + wide), dot(cot_t_ref[...], hidden_ref[:, columns]), place)


def middle_first_kernel(
    n_pieces, core_ref, act_ref, x_ref, cot_ref, cot_t_ref, vec_ref, *rest
):
    pieces, rest = rest[:n_pieces], rest[n_pieces:]
    (proj_ref, mid_ref, xhat_ref, inv_ref, normed_ref, normed_t_ref, hidden_ref, grad_up_ref), rest = rest[:8], rest[8:]
    weights, *grad_refs = rest
    load_rows(core_ref, pieces, weights, False)
    length, feats = x_ref.shape
    count = hidden_ref.shape[1]
    gain, bias = vec_ref[3:4, :], vec_ref[4:5, :]
    proj_ref[...] = weights[:, :feats]
    for at in range(length // BLOCK):
        mid = x_ref[span(at), :].astype(F32) + dot(act_ref[span(at), :], proj_ref[...])
        xhat, inverse = norm_stats(mid)
        normed = (xhat * gain + bias).astype(BF16)
        mid_ref[span(at), :] = mid
        xhat_ref[span(at), :] = xhat
        inv_ref[span(at), :] = jnp.broadcast_to(inverse, (BLOCK, 128))
        normed_ref[span(at), :] = normed
        normed_t_ref[:, span(at)] = normed.T
    hidden_part(
        place_of(core_ref, grad_refs), normed_ref, normed_t_ref, cot_ref, cot_t_ref, feats, feats + count,
        weights, hidden_ref, grad_up_ref, grad_refs,
    )


def middle_second_kernel(
    n_pieces, core_ref, cot_ref, cot_t_ref, normed_ref, normed_t_ref, *rest
):
    pieces, rest = rest[:n_pieces], rest[n_pieces:]
    hidden_ref, grad_up_ref, weights, *grad_refs = rest
    load_rows(core_ref, pieces, weights, True)
    hidden_part(
        place_of(core_ref, grad_refs), normed_ref, normed_t_ref, cot_ref, cot_t_ref, 0,
        hidden_ref.shape[1], weights, hidden_ref, grad_up_ref, grad_refs,
    )


def middle_third_kernel(
    slope_ref, cot_ref, vec_ref, pool_rows, proj_ref, xhat_ref, inv_ref, up_a_ref, up_b_ref, weights_a,
    weights_b, mid_grad_ref, vec_grad_ref, pre_grad_ref, halo_ref,
):
    length, feats = xhat_ref.shape
    count, left = up_a_ref.shape[1], up_b_ref.shape[1]
    gain = vec_ref[3:4, :]
    gain_grad = jnp.zeros((8, feats), F32)
    bias_grad = jnp.zeros((8, feats), F32)
    per = BLOCK // POOL
    for at in range(length // BLOCK):
        grad_normed = dot(up_a_ref[span(at), :], weights_a[:, feats : feats + count], NT)
        grad_normed = grad_normed + dot(up_b_ref[span(at), :], weights_b[:, :left], NT)
        xhat = xhat_ref[span(at), :]
        bias_grad = bias_grad + jnp.sum(grad_normed.reshape(BLOCK // 8, 8, feats), axis=0)
        gain_grad = gain_grad + jnp.sum((grad_normed * xhat).reshape(BLOCK // 8, 8, feats), axis=0)
        grad_mid = cot_ref[span(at), :].astype(F32) + norm_back(
            xhat, inv_ref[span(at), 0:1], grad_normed * gain
        )
        mid_grad_ref[span(at), :] = grad_mid
        grad_act = dot(grad_mid.astype(BF16), proj_ref[...], NT)
        grad_pre = (grad_act * slope_ref[span(at), :].astype(F32)).astype(BF16)
        pre_grad_ref[span(at), :] = grad_pre
        if at == 0:
            halo_ref[0:BLOCK, :] = grad_pre
        halo_ref[pl.ds(BLOCK + at * per, per), :] = (
            dot(pool_rows[...], grad_pre) * np.float32(POOL)
        ).astype(BF16)
    vec_grad_ref[0:1, :] = jnp.sum(gain_grad, axis=0, keepdims=True)
    vec_grad_ref[1:2, :] = jnp.sum(bias_grad, axis=0, keepdims=True)
    vec_grad_ref[2:8, :] = jnp.zeros((6, feats), F32)


def output_kernel(mid_ref, hidden_a_ref, hidden_b_ref, weights_a, weights_b, out_ref):
    length, feats = mid_ref.shape
    count, left = hidden_a_ref.shape[1], hidden_b_ref.shape[1]
    for at in range(length // BLOCK):
        total = mid_ref[span(at), :] + dot(hidden_a_ref[span(at), :], weights_a[:, feats + count :], NT)
        total = total + dot(hidden_b_ref[span(at), :], weights_b[:, left:], NT)
        out_ref[span(at), :] = total.astype(BF16)


def taps_kernel(
    act_ref, mid_grad_ref, pre_grad_ref, halo_ref, win_ref, pool_win_ref, basis, fine_basis,
    coarse_basis, out_grad_ref, tap_grad_ref, z_ref, mid_bf_ref,
):
    length, feats = act_ref.shape
    blocks = length // BLOCK
    total = None
    for at in range(blocks):
        mid_bf_ref[span(at), :] = mid_grad_ref[span(at), :].astype(BF16)
        z = dot(basis[...], pre_grad_ref[span(at), :])
        z_ref[at] = z.astype(BF16)
        term = conj_product(quarters(win_ref[at]), quarters(z))
        total = term if total is None else [a + b for a, b in zip(total, term)]
    out_grad_ref[...] = dot(act_ref[...], mid_bf_ref[...], TN).astype(BF16)
    pooled = length // POOL
    z_pool = dot(basis[:, 0:pooled], halo_ref[BLOCK : BLOCK + pooled, :])
    pool_term = conj_product(quarters(pool_win_ref[...]), quarters(z_pool))
    tap_grad_ref[...] = (
        (dot(stacked(total), fine_basis[...], TN) + dot(stacked(pool_term), coarse_basis[...], TN))
        * np.float32(1 / FREQ)
    ).astype(BF16)


def backward_kernel(
    core_ref, z_ref, halo_ref, next_ref, pre_grad_ref, fine_h_ref, coarse_h_ref, basis, basis_t, back_pool,
    weights, vec_ref, vec_grad_ref, xhat_ref, out_grad_ref, tap_grad_ref, mixed_grad_ref, *rest
):
    *grad_refs, pool_ref = rest
    place = place_of(core_ref, grad_refs)
    length, feats = xhat_ref.shape
    blocks = length // BLOCK
    pooled = length // POOL
    gain, bias, skip = vec_ref[0:1, :], vec_ref[1:2, :], vec_ref[2:3, :]
    fine_q = quarters(fine_h_ref[...])
    pool_ref[0:pooled, :] = halo_ref[BLOCK : BLOCK + pooled, :]
    pool_ref[pooled : 2 * pooled, :] = next_ref[BLOCK : BLOCK + pooled, :]
    z_pool = quarters(dot(basis[...], pool_ref[...]))
    coarse_y = stacked([v * np.float32(1 / POOL) for v in conj_product(quarters(coarse_h_ref[...]), z_pool)])
    later = quarters(dot(basis[...], next_ref[0:BLOCK, :]))
    sums = jnp.zeros((8, feats), F32)
    for at in reversed(range(blocks)):
        now = quarters(z_ref[at])
        y = stacked(conj_product(fine_q, add_after(now, later)))
        later = now
        total = dot(basis_t[...], y) + dot(back_pool[span(at), :], coarse_y)
        grad_mixed = (
            total * np.float32(1 / FREQ) + skip * pre_grad_ref[span(at), :].astype(F32)
        ).astype(BF16)
        mixed_grad_ref[span(at), :] = grad_mixed
        sums = sums + jnp.sum(grad_mixed.astype(F32).reshape(BLOCK // 8, 8, feats), axis=0)
    back = dot(xhat_ref[...], mixed_grad_ref[...], TN)
    mixed_sum = jnp.sum(sums, axis=0, keepdims=True)
    padded = jnp.concatenate([vec_ref[...], vec_grad_ref[...], jnp.zeros((112, feats), F32)], axis=0)
    columns = padded.T
    put_rows(grad_refs, slice(0, feats), columns[:, 0:1] * back + columns[:, 1:2] * mixed_sum, place)
    put_rows(grad_refs, slice(feats, 2 * feats), out_grad_ref[...], place)
    put_rows(grad_refs, slice(2 * feats, 2 * feats + 256), tap_grad_ref[...], place)
    proj = weights[:, 0:feats]
    proj_f = proj.astype(F32)
    gain_grad = jnp.sum(proj_f * back, axis=1, keepdims=True)
    bias_grad = jnp.sum(proj_f * mixed_sum, axis=1, keepdims=True)
    lane = lax.broadcasted_iota(jnp.int32, (feats, 128), 1)
    columns = jnp.where(lane == 0, gain_grad, jnp.where(lane == 1, bias_grad, columns))
    put_rows(grad_refs, slice(2 * feats + 256, 2 * feats + 384), columns, place)


def input_kernel(mixed_grad_ref, weights, vec_ref, xhat_ref, inv_ref, mid_grad_ref, input_grad_ref):
    length, feats = xhat_ref.shape
    proj = weights[:, 0:feats]
    for at in range(length // BLOCK):
        grad_normed = dot(mixed_grad_ref[span(at), :], proj, NT)
        input_grad_ref[span(at), :] = mid_grad_ref[span(at), :] + norm_back(
            xhat_ref[span(at), :].astype(F32), inv_ref[span(at), 0:1], grad_normed * vec_ref[0:1, :]
        )


def final_kernel(n_mlp, param_ref, scale_ref, wide_ref, *rest):
    sources, outs = rest[: len(rest) - 10], rest[len(rest) - 10 :]
    up_ref, down_ref, in_ref, out_ref, param_grad_ref = outs[:5]
    totals = []
    for group in (sources[:n_mlp], sources[n_mlp:]):
        total = group[0][...].astype(F32)
        for source in group[1:]:
            total = total + source[...].astype(F32)
        totals.append(total)
    mlp, mixer = totals
    hidden = mlp.shape[1] // 2
    cut = first_part(hidden)
    up_ref[:, :cut], up_ref[:, cut:] = mlp[:, :cut], mlp[:, 2 * cut : cut + hidden]
    down_ref[:, :cut], down_ref[:, cut:] = mlp[:, cut : 2 * cut], mlp[:, cut + hidden :]
    feats = in_ref.shape[1]
    in_ref[...] = mixer[:, :feats]
    out_ref[...] = mixer[:, feats : 2 * feats]
    taps = param_ref.shape[1]
    tap_rows = mixer[:, 2 * feats : 2 * feats + taps]
    scale, wide = scale_ref[:, :taps], wide_ref[:, :taps]
    raw = param_ref[...].astype(F32) * scale
    inverse = lax.rsqrt(jnp.sum(raw * raw * wide, axis=1, keepdims=True) + 1e-05)
    own = raw * inverse
    along = jnp.sum(tap_rows * own, axis=1, keepdims=True)
    param_grad_ref[...] = scale * inverse * (tap_rows - wide * own * along)
    tail = mixer[:, 2 * feats + 256 :]
    rows = tail.shape[0]
    diagonal = lax.broadcasted_iota(jnp.int32, (rows, rows), 0) == lax.broadcasted_iota(
        jnp.int32, (rows, rows), 1
    )
    columns = (tail[:, 0:1], tail[:, 1:2], tap_rows[:, 0:1], tail[:, 8:9], tail[:, 9:10])
    for ref, column in zip(outs[5:], columns):
        ref[...] = jnp.sum(jnp.where(diagonal, column, 0.0), axis=0, keepdims=True)


def call(kernel, operands, outs, scratch=(), flops=0, spaces=None, limit=12):
    spaces = spaces or [pltpu.VMEM] * len(operands)
    operands = [
        pltpu.with_memory_space_constraint(operand, pltpu.HBM) if space is pltpu.HBM else operand
        for operand, space in zip(operands, spaces)
    ]
    return pl.pallas_call(
        kernel,
        out_shape=[jax.ShapeDtypeStruct(shape, dtype) for shape, dtype in outs],
        in_specs=[pl.BlockSpec(memory_space=space) for space in spaces],
        out_specs=[pl.BlockSpec(memory_space=pltpu.VMEM)] * len(outs),
        scratch_shapes=list(scratch),
        compiler_params=pltpu.CompilerParams(vmem_limit_bytes=limit << 20),
        cost_estimate=pl.CostEstimate(flops=flops, bytes_accessed=1 << 16, transcendentals=0),
    )(*operands)


def body(
    block_input,
    mixer_gain,
    mixer_bias,
    in_proj,
    kernel_param,
    skip_gain,
    out_proj,
    mlp_gain,
    mlp_bias,
    up_proj,
    down_proj,
    out_cotangent,
):
    _, length, feats = block_input.shape
    hidden = up_proj.shape[1]
    cut = first_part(hidden)
    left = hidden - cut
    blocks = length // BLOCK
    pooled = length // POOL
    taps = TAPS * SCALES
    own_rows = in_proj.shape[0]
    x_own, cot = block_input[0], out_cotangent[0]
    core_at = jnp.stack([lax.axis_index("seq"), lax.axis_index("dp")]).astype(jnp.int32)
    x_prior = lax.ppermute(x_own, "seq", [(0, 1)])
    vectors = [v.reshape(1, -1) for v in (mixer_gain, mixer_bias, skip_gain, mlp_gain, mlp_bias)]
    shard, shard_b = call(
        pack_kernel,
        [core_at, in_proj, kernel_param, out_proj, up_proj, down_proj, *vectors],
        [((own_rows, PACK + feats + 2 * cut), BF16), ((own_rows, 2 * left), BF16)],
        [
            pltpu.VMEM(kernel_param.shape, BF16), pltpu.VMEM((5, 1, own_rows), BF16),
            pltpu.SemaphoreType.DMA,
        ],
        spaces=[pltpu.SMEM] + [pltpu.HBM] * 10,
    )
    basis_np = odd_basis(np.arange(BLOCK))
    basis, basis_t = bf16_const(basis_np), bf16_const(basis_np.T)
    basis_pool = bf16_const(odd_basis(np.arange(-pooled, pooled)))
    back_pool = bf16_const(np.repeat(odd_basis(np.arange(pooled)).T, POOL, axis=0))
    fine_basis = bf16_const(tap_basis(0, 0))
    coarse_basis = bf16_const(tap_basis(OFFSET, TAPS * FINE))
    pool_rows = bf16_const(np.kron(np.eye(BLOCK // POOL), np.ones((1, POOL))) / POOL)
    scale_np = np.zeros((1, 256), np.float32)
    scale_np[0, :taps] = np.repeat(0.5 ** np.arange(SCALES), TAPS)
    wide_np = np.zeros((1, 256), np.float32)
    wide_np[0, :taps] = np.repeat(2.0 ** (np.arange(SCALES) % FINE), TAPS)

    xhat, inv_one, cot_t = call(
        prepare_kernel,
        [x_own, cot],
        [((length, feats), BF16), ((length, 128), F32), ((feats, length), BF16)],
        [
            pltpu.VMEM((length, feats), BF16), pltpu.VMEM((length, feats), BF16),
            pltpu.SemaphoreType.DMA((2, blocks)),
        ],
        spaces=[pltpu.HBM] * 2,
    )
    (prior_hat,) = call(prior_kernel, [x_prior], [((length, feats), BF16)])
    held_b = jnp.concatenate(gather_plane(tie(shard_b, prior_hat)[None]))
    held = shard[None]
    for at, step in enumerate(far_steps()):
        got = from_line(held, step)
        got = tie(got, xhat) if at == 0 else got
        held = paired(held, got)
    held = tie(held, xhat, prior_hat, held_b)
    steps = far_steps()
    held_b = held_b[None]
    for step in steps[:-1]:
        held_b = gather_line(held_b, step)
    xhat_in = tie(xhat, held_b)
    first, held_a = held[:, :, :PACK], held[:, :, PACK:]
    first = gather_near(first)
    pieces_a = gather_plane(held_a)
    first = in_order(gather_core(first), False)
    smem = pltpu.SMEM
    n_first = len(first)
    weights, vec, fine_h, coarse_h, window, pool_win, act, slope = call(
        lambda *refs: forward_kernel(n_first, *refs),
        [
            core_at, xhat_in, prior_hat, basis, basis_t, basis_pool,
            back_pool, fine_basis, coarse_basis, pool_rows, jnp.asarray(scale_np), jnp.asarray(wide_np),
            *first,
        ],
        [
            ((feats, PACK), BF16), ((8, feats), F32), ((2 * FREQ, feats), BF16),
            ((2 * FREQ, feats), BF16), ((blocks, 2 * FREQ, feats), BF16), ((2 * FREQ, feats), BF16),
            ((length, feats), BF16), ((length, feats), BF16),
        ],
        [
            pltpu.VMEM((length, feats), BF16), pltpu.VMEM((2 * pooled, feats), BF16),
        ],
        flops=6 << 30,
        spaces=[smem] + [pltpu.VMEM] * (11 + n_first),
    )
    got_b = [from_line(held_b, step) for step in steps[-1:]]
    *pieces_a, act = lax.optimization_barrier((*pieces_a, act))
    pieces_a = in_order(gather_core(pieces_a, 4), False)
    *got_b, act = lax.optimization_barrier((*got_b, act))
    for got in got_b:
        held_b = paired(held_b, got)
    held_b = held_b.reshape((-1,) + held_b.shape[2:])
    pieces_b = in_order(gather_core([held_b]), True)
    n_a = len(pieces_a)
    rows = own_rows


    def grad_shapes(columns):
        if rows % 16 == 0:
            return [((feats // (2 * rows), rows, columns), BF16)] * 2
        return [((feats, columns), BF16)]

    token_f32, token_bf16 = ((length, feats), F32), ((length, feats), BF16)
    vmem = pltpu.VMEM
    proj_out, mid, xhat_two, inv_two, normed, normed_t, hidden_a, grad_up_a, weights_a, *grads_a = call(
        lambda *refs: middle_first_kernel(n_a, *refs),
        [core_at, act, x_own, cot, cot_t, vec, *pieces_a],
        [
            ((feats, feats), BF16), token_f32, token_f32, ((length, 128), F32), token_bf16,
            ((feats, length), BF16), ((length, cut), BF16), ((length, cut), BF16),
            ((feats, feats + 2 * cut), BF16), *grad_shapes(2 * cut),
        ],
        flops=8 << 30,
        spaces=[smem] + [vmem] * (5 + n_a),
    )
    n_b = len(pieces_b)
    hidden_b, grad_up_b, weights_b, *grads_b = call(
        lambda *refs: middle_second_kernel(n_b, *refs),
        [core_at, cot, cot_t, normed, normed_t, *pieces_b],
        [((length, left), BF16), ((length, left), BF16), ((feats, 2 * left), BF16), *grad_shapes(2 * left)],
        flops=16 << 30,
        spaces=[smem] + [vmem] * (4 + n_b),
    )
    near_a = reduce_core(grads_a, hidden_b)
    grad_up_b = tie(grad_up_b, *near_a)
    spread_a = spread_near(near_a)
    grad_mid, vec_grad, grad_pre, halo = call(
        middle_third_kernel,
        [slope, cot, vec, pool_rows, proj_out, xhat_two, inv_two, grad_up_a, grad_up_b, weights_a, weights_b],
        [token_f32, ((8, feats), F32), token_bf16, ((BLOCK + pooled, feats), BF16)],
        flops=4 << 30,
    )
    after = lax.ppermute(halo, "seq", [(1, 0)])
    near_b = reduce_core(grads_b, grad_mid)
    grad_pre = tie(grad_pre, *near_b)
    spread_b = spread_near(near_b)
    out_grad, tap_grad, z_grad = call(
        taps_kernel,
        [act, grad_mid, grad_pre, halo, window, pool_win, basis, fine_basis, coarse_basis],
        [
            ((feats, feats), BF16), ((feats, 256), BF16), ((blocks, 2 * FREQ, feats), BF16),
        ],
        [pltpu.VMEM((length, feats), BF16)],
        flops=2 << 24,
    )
    z_grad = tie(z_grad, after)
    grad_mixed, *grads_c = call(
        backward_kernel,
        [
            core_at, z_grad, halo, after, grad_pre, fine_h, coarse_h, basis, basis_t, back_pool, weights,
            vec, vec_grad, xhat, out_grad, tap_grad,
        ],
        [token_bf16, *grad_shapes(2 * feats + 384)],
        [pltpu.VMEM((2 * pooled, feats), BF16)],
        flops=4 << 24,
        spaces=[smem] + [vmem] * 15,
    )
    (input_grad,) = call(
        input_kernel, [grad_mixed, weights, vec, xhat, inv_one, grad_mid], [token_f32], flops=2 << 24
    )
    part_a = add_up(tie(tuple(spread_a), grad_mixed), BF16)
    part_b = add_up(tie(tuple(spread_b), input_grad), BF16)
    part_ab = jnp.concatenate([part_a, part_b], axis=2)
    steps_ab = far_steps()[::-1]
    pairs = part_ab.reshape((-1, 2) + part_ab.shape[1:])
    far_ab = [pairs[:, 0], from_line(pairs[:, 1], steps_ab[0])] if steps_ab else [part_ab]
    near_c = reduce_core(grads_c, input_grad)
    spread_c = spread_near(near_c)
    (block_output,) = call(
        output_kernel, [tie(mid, *near_c), hidden_a, hidden_b, weights_a, weights_b], [token_bf16], flops=4 << 24
    )
    far_c = spread_far(add_up(tie(tuple(spread_c), block_output), BF16))
    if steps_ab:
        far_ab = [far_ab[0], tie(far_ab[1], block_output)]
    for step in steps_ab[1:]:
        held = add_up(far_ab, BF16)
        pairs = held.reshape((-1, 2) + held.shape[1:])
        far_ab = [pairs[:, 0], from_line(pairs[:, 1], step)]
    far_ab = [term[0] for term in far_ab]
    vector = ((1, rows), F32)
    up_sum, down_sum, in_sum, out_sum, param_sum, *vectors = call(
        lambda *refs: final_kernel(len(far_ab), *refs),
        [kernel_param, jnp.asarray(scale_np), jnp.asarray(wide_np), *far_ab, *far_c],
        [
            ((rows, hidden), F32), ((rows, hidden), F32), ((rows, feats), F32), ((rows, feats), F32),
            ((rows, taps), F32), vector, vector, vector, vector, vector,
        ],
    )
    gain_one, bias_one, skip_sum, gain_two, bias_two = (v.reshape(rows) for v in vectors)
    return (
        block_output[None], input_grad[None], gain_one, bias_one, in_sum, param_sum, skip_sum, out_sum,
        gain_two, bias_two, up_sum, down_sum,
    )


def solution(mesh):
    rows = P(("dp", "seq"), None)
    vector = P(("dp", "seq"))
    tokens = P("dp", "seq", None)
    return jax.shard_map(
        body,
        mesh=mesh,
        in_specs=(
            tokens, vector, vector, rows, rows, vector, rows, vector, vector, rows, rows, tokens,
        ),
        out_specs=(
            tokens, tokens, vector, vector, rows, rows, vector, rows, vector, vector, rows, rows,
        ),
        check_vma=False,
    )
```

```python
import math

import jax
import jax.numpy as jnp
import numpy as np
from jax import lax
from jax.experimental import pallas as pl
from jax.experimental.pallas import tpu as pltpu
from jax.sharding import PartitionSpec as P

TAPS = 32
SCALES = 6
FINE = 3
FREQ = 256
HALF = FREQ // 2
BLOCK = 256
POOL = 8
OFFSET = 28
TILE = 512
WIDE = 512
PACK = 768
F32 = jnp.float32
BF16 = jnp.bfloat16
NT = ((1,), (1,))
TN = ((0,), (0,))


def odd_basis(positions):
    order = np.concatenate([np.arange(0, FREQ, 2), np.arange(1, FREQ, 2)])
    angle = np.pi * np.outer(order + 0.5, positions) / FREQ
    return np.concatenate([np.cos(angle), -np.sin(angle)], axis=0)


def tap_basis(start, first):
    columns = np.zeros((2 * FREQ, 256))
    for scale_at in range(FINE):
        wide = 2**scale_at
        lag = start + TAPS * (wide - 1)
        for tap in range(TAPS):
            at = first + scale_at * TAPS + tap
            columns[:, at] = odd_basis(lag + tap * wide + np.arange(wide)).sum(axis=1)
    return columns


def bf16_const(array):
    return jnp.asarray(np.asarray(array, np.float32).astype(jnp.bfloat16))


def dot(a, b, contract=((1,), (0,))):
    return lax.dot_general(a, b, (contract, ((), ())), preferred_element_type=F32)


def normal_parts(values):
    cdf = 0.5 + 0.5 * lax.erf(values * np.float32(math.sqrt(0.5)))
    pdf = jnp.exp(-0.5 * values * values) * np.float32(1 / math.sqrt(2 * math.pi))
    return cdf, pdf


def split_dp(count):
    edge = round((count / 2) ** (1 / 3))
    return (2 * edge, edge * edge) if 2 * edge**3 == count else (1, count)


def swap_route(count, mask):
    return [(i, i ^ mask) for i in range(count)]


SWAP = [(0, 1), (1, 0)]


def tie(value, *others):
    return lax.optimization_barrier((value, *others))[0]


def far_steps():
    nz, _ = split_dp(lax.axis_size("dp"))
    return [1 << bit for bit in reversed(range(nz.bit_length() - 1))]


def from_line(held, step):
    dp_count = lax.axis_size("dp")
    _, nxy = split_dp(dp_count)
    return lax.ppermute(held, "dp", swap_route(dp_count, step * nxy))


def paired(held, got):
    return jnp.stack([held, got], axis=1).reshape((-1,) + held.shape[1:])


def gather_line(held, step):
    return paired(held, from_line(held, step))


def gather_far(shard):
    held = shard[None]
    for step in far_steps():
        held = gather_line(held, step)
    return held


def gather_near(held):
    dp_count = lax.axis_size("dp")
    _, nxy = split_dp(dp_count)
    return [held] + [lax.ppermute(held, "dp", swap_route(dp_count, k)) for k in range(1, nxy)]


def gather_core(pieces, parts=1):
    held = jnp.concatenate(pieces)
    size = held.shape[0] // parts
    held = [held[at * size : (at + 1) * size] for at in range(parts)]
    return held + [lax.ppermute(part, "seq", SWAP) for part in held]


def gather_plane(held):
    dp_count = lax.axis_size("dp")
    _, nxy = split_dp(dp_count)
    if nxy != 4:
        return gather_near(held)
    by_x = lax.ppermute(held, "dp", swap_route(dp_count, 1))
    by_y = lax.ppermute(held, "dp", swap_route(dp_count, 2))
    if held.shape[0] == 1:
        return [held, by_x, by_y, lax.ppermute(by_y, "dp", swap_route(dp_count, 1))]
    cut = held.shape[0] // 2
    return [
        held, by_x, by_y, lax.ppermute(by_y[:cut], "dp", swap_route(dp_count, 1)),
        lax.ppermute(by_x[cut:], "dp", swap_route(dp_count, 2)),
    ]


def row_place(at, count, plane_first, core_ref):
    nz, nxy = split_dp(count)
    other, at = divmod(at, count)
    if plane_first:
        z, xy = divmod(at, nxy)
    else:
        xy, z = divmod(at, nz)
    return ((z * nxy + xy) ^ core_ref[1]) * 2 + (other ^ core_ref[0])


def in_order(pieces, plane_first):
    if pieces[0].shape[1] % 16 == 0:
        return pieces
    dp_count = lax.axis_size("dp")
    nz, nxy = split_dp(dp_count)
    me, core = lax.axis_index("dp"), lax.axis_index("seq")
    by_dp = jnp.arange(dp_count).reshape(nz, nxy) ^ me
    by_dp = by_dp if plane_first else by_dp.T
    where = by_dp[None] * 2 + (jnp.arange(2)[:, None, None] ^ core)
    flat = jnp.concatenate(pieces)
    return [jnp.take(flat, jnp.argsort(where.reshape(-1)), axis=0).reshape(1, -1, flat.shape[2])]


def reduce_core(grads, *before):
    dp_count = lax.axis_size("dp")
    nz, nxy = split_dp(dp_count)
    if len(grads) == 1:
        core, me = lax.axis_index("seq"), lax.axis_index("dp")
        shaped = grads[0].reshape(dp_count, 2, -1, grads[0].shape[1])
        order = (jnp.arange(nz)[None, :] * nxy + jnp.arange(nxy)[:, None]) ^ me
        shaped = jnp.take(shaped, order.reshape(-1), axis=0)
        grads = [
            lax.dynamic_index_in_dim(shaped, 1 - core, 1, False),
            lax.dynamic_index_in_dim(shaped, core, 1, False),
        ]
    send, keep = grads
    got = lax.ppermute(send, "seq", SWAP)
    got = tie(got, *before)
    total = (keep.astype(F32) + got.astype(F32)).astype(BF16)
    return [total[k * nz : (k + 1) * nz] for k in range(nxy)]


def spread_near(pieces):
    dp_count = lax.axis_size("dp")
    return [pieces[0]] + [
        lax.ppermute(pieces[k], "dp", swap_route(dp_count, k)) for k in range(1, len(pieces))
    ]


def spread_far(part):
    dp_count = lax.axis_size("dp")
    nz, nxy = split_dp(dp_count)
    return [part[0]] + [
        lax.ppermute(part[k], "dp", swap_route(dp_count, k * nxy)) for k in range(1, nz)
    ]


def add_up(pieces, dtype=F32):
    total = pieces[0].astype(F32)
    for piece in pieces[1:]:
        total = total + piece.astype(F32)
    return total.astype(dtype)


def load_rows(core_ref, pieces, target, plane_first):
    if len(pieces) == 1:
        target[...] = pieces[0][0]
        return
    count = target.shape[0] // (2 * pieces[0].shape[1])
    at = 0
    for piece in pieces:
        held, rows, _ = piece.shape
        for i in range(held):
            start = row_place(at, count, plane_first, core_ref) * rows
            target[pl.ds(pl.multiple_of(start, 16), rows), :] = piece[i]
            at += 1


def span(at, size=BLOCK):
    return pl.ds(at * size, size)


def norm_stats(features):
    centre = features - jnp.mean(features, axis=-1, keepdims=True)
    inverse = lax.rsqrt(jnp.mean(centre * centre, axis=-1, keepdims=True) + 1e-05)
    return centre * inverse, inverse


def norm_back(xhat, inverse, scaled):
    return inverse * (
        scaled
        - jnp.mean(scaled, axis=-1, keepdims=True)
        - xhat * jnp.mean(scaled * xhat, axis=-1, keepdims=True)
    )


def quarters(spectrum):
    return [spectrum[i * HALF : (i + 1) * HALF].astype(F32) for i in range(4)]


def add_before(now, past):
    (re, ro, ie, io), (pre, pro, pie, pio) = now, past
    return re - pie, ro + pio, ie + pre, io - pro


def add_after(now, later):
    (re, ro, ie, io), (nre, nro, nie, nio) = now, later
    return re + nie, ro - nio, ie - nre, io + nro


def product(a, b):
    (are, aro, aie, aio), (bre, bro, bie, bio) = a, b
    return (
        are * bre - aie * bie,
        aro * bro - aio * bio,
        are * bie + aie * bre,
        aro * bio + aio * bro,
    )


def conj_product(a, b):
    (are, aro, aie, aio), (bre, bro, bie, bio) = a, b
    return (
        are * bre + aie * bie,
        aro * bro + aio * bio,
        are * bie - aie * bre,
        aro * bio - aio * bro,
    )


def stacked(parts):
    return jnp.concatenate([part.astype(BF16) for part in parts], axis=0)


def put_quarters(ref, at, parts):
    for i, part in enumerate(parts):
        ref[at, i * HALF : (i + 1) * HALF, :] = part.astype(ref.dtype)


def first_part(hidden):
    return hidden // 2


def pack_kernel(core_ref, in_ref, param_ref, out_ref, up_ref, down_ref, *rest):
    vectors, (a_ref, b_ref, param, small, sem) = rest[:5], rest[5:]
    rows, feats = in_ref.shape
    cut = first_part(up_ref.shape[1])
    left = up_ref.shape[1] - cut
    copies = [
        pltpu.make_async_copy(in_ref, a_ref.at[:, pl.ds(0, feats)], sem),
        pltpu.make_async_copy(param_ref, param, sem),
    ]
    for i, vector in enumerate(vectors):
        copies.append(pltpu.make_async_copy(vector, small.at[i], sem))
    for source, start, size, target, at in (
        (out_ref, 0, feats, a_ref, PACK), (up_ref, 0, cut, a_ref, PACK + feats),
        (down_ref, 0, cut, a_ref, PACK + feats + cut), (up_ref, cut, left, b_ref, 0),
        (down_ref, cut, left, b_ref, left),
    ):
        copies.append(
            pltpu.make_async_copy(
                source.at[:, pl.ds(start, size)], target.at[:, pl.ds(at, size)], sem
            )
        )
    for copy in copies:
        copy.start()
    for copy in copies:
        copy.wait()
    spare = PACK - feats - param.shape[1]
    row = lax.broadcasted_iota(jnp.int32, (rows, rows), 0)
    lane = lax.broadcasted_iota(jnp.int32, (rows, rows), 1)
    slot = lax.broadcasted_iota(jnp.int32, (rows, spare), 1)
    block = jnp.zeros((rows, spare), F32)
    for i in range(len(vectors)):
        value = small[i].astype(F32)
        column = jnp.sum(jnp.where(row == lane, value, 0.0), axis=1, keepdims=True)
        block = jnp.where(slot == i, column, block)
    tail = jnp.concatenate([param[...].astype(F32), block], axis=1)
    a_ref[:, feats:PACK] = tail.astype(BF16)


def prepare_kernel(x_ref, cot_ref, xhat_ref, inv_ref, cot_t_ref, cot_copy, x_copy, sem):
    blocks = x_ref.shape[0] // BLOCK
    copies = []
    for source, target, which in ((x_ref, x_copy, 0), (cot_ref, cot_copy, 1)):
        for at in range(blocks):
            copies.append(
                pltpu.make_async_copy(source.at[span(at), :], target.at[span(at), :], sem.at[which, at])
            )
    for copy in copies:
        copy.start()
    for at in range(blocks):
        copies[at].wait()
        xhat, inverse = norm_stats(x_copy[span(at), :].astype(F32))
        xhat_ref[span(at), :] = xhat.astype(BF16)
        inv_ref[span(at), :] = jnp.broadcast_to(inverse, (BLOCK, 128))
    for at in range(blocks):
        copies[blocks + at].wait()
        cot_t_ref[:, span(at)] = cot_copy[span(at), :].T


def prior_kernel(x_ref, xhat_ref):
    for at in range(x_ref.shape[0] // BLOCK):
        xhat_ref[span(at), :] = norm_stats(x_ref[span(at), :].astype(F32))[0].astype(BF16)


def forward_kernel(
    n_pieces, core_ref, xhat_ref, prior_ref, basis, basis_t, basis_pool, back_pool,
    fine_basis, coarse_basis, pool_rows, scale_ref, wide_ref, *rest,
):
    pieces, rest = rest[:n_pieces], rest[n_pieces:]
    weights, vec_ref, fine_h_ref, coarse_h_ref, win_ref, pool_win_ref, act_ref, slope_ref = rest[:8]
    mixed_ref, pooled_ref = rest[8:]
    load_rows(core_ref, pieces, weights, False)
    feats = xhat_ref.shape[1]
    blocks = xhat_ref.shape[0] // BLOCK
    tail = weights[:, feats : feats + 256].astype(F32)
    raw = tail * scale_ref[...]
    inverse = lax.rsqrt(jnp.sum(raw * raw * wide_ref[...], axis=1, keepdims=True) + 1e-05)
    taps = (raw * inverse).astype(BF16)
    vec = tail[:, 128:256].T[64:72]
    vec_ref[...] = vec
    gain, bias, skip = vec[0:1], vec[1:2], vec[2:3]
    fine_h = dot(fine_basis[...], taps, NT)
    coarse_h = dot(coarse_basis[...], taps, NT)
    fine_h_ref[...] = fine_h.astype(BF16)
    coarse_h_ref[...] = coarse_h.astype(BF16)
    proj = weights[:, :feats]
    has_prior = core_ref[0].astype(F32)
    per = BLOCK // POOL
    past = None
    total = dot((prior_ref[...].astype(F32) * gain + bias).astype(BF16), proj)
    for at in range(blocks):
        mixed = (total[at * BLOCK : (at + 1) * BLOCK] * has_prior).astype(BF16)
        pooled_ref[span(at, per), :] = dot(pool_rows[...], mixed).astype(BF16)
        if at == blocks - 1:
            past = quarters(dot(basis[...], mixed))
    total = dot((xhat_ref[...].astype(F32) * gain + bias).astype(BF16), proj)
    for at in range(blocks):
        mixed = total[at * BLOCK : (at + 1) * BLOCK].astype(BF16)
        mixed_ref[span(at), :] = mixed
        pooled_ref[span(blocks + at, per), :] = dot(pool_rows[...], mixed).astype(BF16)
    pool_win = dot(basis_pool[...], pooled_ref[...])
    pool_win_ref[...] = pool_win.astype(BF16)
    coarse_y = stacked(product(quarters(coarse_h), quarters(pool_win)))
    fine_q = quarters(fine_h)
    for at in range(blocks):
        mixed = mixed_ref[span(at), :]
        now = quarters(dot(basis[...], mixed))
        window = add_before(now, past)
        past = now
        put_quarters(win_ref, at, window)
        total = dot(basis_t[...], stacked(product(fine_q, window)))
        total = total + dot(back_pool[span(at), :], coarse_y)
        pre_act = total * np.float32(1 / FREQ) + skip * mixed.astype(F32)
        cdf, pdf = normal_parts(pre_act)
        act_ref[span(at), :] = (pre_act * cdf).astype(BF16)
        slope_ref[span(at), :] = (cdf + pre_act * pdf).astype(BF16)


def place_of(core_ref, grad_refs):
    nz, nxy = split_dp(grad_refs[0].shape[0])
    return core_ref[0], core_ref[1] // nxy, core_ref[1] % nxy, nz, nxy


def put_rows(refs, columns, value, place):
    value = value.astype(BF16)
    if len(refs) == 1:
        refs[0][:, columns] = value
        return
    send_ref, keep_ref = refs
    count, rows, _ = send_ref.shape
    core, me_z, me_xy, nz, nxy = place
    for at in range(count):
        slot = ((at % nxy) ^ me_xy) * nz + ((at // nxy) ^ me_z)
        first = value[2 * at * rows : (2 * at + 1) * rows]
        second = value[(2 * at + 1) * rows : (2 * at + 2) * rows]
        send_ref[slot, :, columns] = jnp.where(core == 0, second, first)
        keep_ref[slot, :, columns] = jnp.where(core == 0, first, second)


def hidden_part(place, normed_ref, normed_t_ref, cot_ref, cot_t_ref, up_at, down_at, weights, hidden_ref, grad_up_ref, grad_refs):
    length = normed_ref.shape[0]
    count = hidden_ref.shape[1]
    for at in range(0, count, WIDE):
        wide = min(WIDE, count - at)
        columns = slice(at, at + wide)
        up = weights[:, up_at + at : up_at + at + wide]
        down = weights[:, down_at + at : down_at + at + wide]
        for row in range(0, length, TILE):
            rows = slice(row, row + TILE)
            up_val = dot(normed_ref[rows, :], up)
            grad_hidden = dot(cot_ref[rows, :], down)
            cdf, pdf = normal_parts(up_val)
            hidden_ref[rows, columns] = (up_val * cdf).astype(BF16)
            grad_up_ref[rows, columns] = (grad_hidden * (cdf + up_val * pdf)).astype(BF16)
        put_rows(grad_refs, slice(at, at + wide), dot(normed_t_ref[...], grad_up_ref[:, columns]), place)
        put_rows(grad_refs, slice(count + at, count + at + wide), dot(cot_t_ref[...], hidden_ref[:, columns]), place)


def middle_first_kernel(
    n_pieces, core_ref, act_ref, x_ref, cot_ref, cot_t_ref, vec_ref, *rest
):
    pieces, rest = rest[:n_pieces], rest[n_pieces:]
    (proj_ref, mid_ref, xhat_ref, inv_ref, normed_ref, normed_t_ref, hidden_ref, grad_up_ref), rest = rest[:8], rest[8:]
    weights, *grad_refs = rest
    load_rows(core_ref, pieces, weights, False)
    length, feats = x_ref.shape
    count = hidden_ref.shape[1]
    gain, bias = vec_ref[3:4, :], vec_ref[4:5, :]
    proj_ref[...] = weights[:, :feats]
    for at in range(length // BLOCK):
        mid = x_ref[span(at), :].astype(F32) + dot(act_ref[span(at), :], proj_ref[...])
        xhat, inverse = norm_stats(mid)
        normed = (xhat * gain + bias).astype(BF16)
        mid_ref[span(at), :] = mid
        xhat_ref[span(at), :] = xhat
        inv_ref[span(at), :] = jnp.broadcast_to(inverse, (BLOCK, 128))
        normed_ref[span(at), :] = normed
        normed_t_ref[:, span(at)] = normed.T
    hidden_part(
        place_of(core_ref, grad_refs), normed_ref, normed_t_ref, cot_ref, cot_t_ref, feats, feats + count,
        weights, hidden_ref, grad_up_ref, grad_refs,
    )


def middle_second_kernel(
    n_pieces, core_ref, cot_ref, cot_t_ref, normed_ref, normed_t_ref, *rest
):
    pieces, rest = rest[:n_pieces], rest[n_pieces:]
    hidden_ref, grad_up_ref, weights, *grad_refs = rest
    load_rows(core_ref, pieces, weights, True)
    hidden_part(
        place_of(core_ref, grad_refs), normed_ref, normed_t_ref, cot_ref, cot_t_ref, 0,
        hidden_ref.shape[1], weights, hidden_ref, grad_up_ref, grad_refs,
    )


def middle_third_kernel(
    slope_ref, cot_ref, vec_ref, pool_rows, proj_ref, xhat_ref, inv_ref, up_a_ref, up_b_ref, weights_a,
    weights_b, mid_grad_ref, vec_grad_ref, pre_grad_ref, halo_ref,
):
    length, feats = xhat_ref.shape
    count, left = up_a_ref.shape[1], up_b_ref.shape[1]
    gain = vec_ref[3:4, :]
    gain_grad = jnp.zeros((8, feats), F32)
    bias_grad = jnp.zeros((8, feats), F32)
    per = BLOCK // POOL
    for at in range(length // BLOCK):
        grad_normed = dot(up_a_ref[span(at), :], weights_a[:, feats : feats + count], NT)
        grad_normed = grad_normed + dot(up_b_ref[span(at), :], weights_b[:, :left], NT)
        xhat = xhat_ref[span(at), :]
        bias_grad = bias_grad + jnp.sum(grad_normed.reshape(BLOCK // 8, 8, feats), axis=0)
        gain_grad = gain_grad + jnp.sum((grad_normed * xhat).reshape(BLOCK // 8, 8, feats), axis=0)
        grad_mid = cot_ref[span(at), :].astype(F32) + norm_back(
            xhat, inv_ref[span(at), 0:1], grad_normed * gain
        )
        mid_grad_ref[span(at), :] = grad_mid
        grad_act = dot(grad_mid.astype(BF16), proj_ref[...], NT)
        grad_pre = (grad_act * slope_ref[span(at), :].astype(F32)).astype(BF16)
        pre_grad_ref[span(at), :] = grad_pre
        if at == 0:
            halo_ref[0:BLOCK, :] = grad_pre
        halo_ref[pl.ds(BLOCK + at * per, per), :] = (
            dot(pool_rows[...], grad_pre) * np.float32(POOL)
        ).astype(BF16)
    vec_grad_ref[0:1, :] = jnp.sum(gain_grad, axis=0, keepdims=True)
    vec_grad_ref[1:2, :] = jnp.sum(bias_grad, axis=0, keepdims=True)
    vec_grad_ref[2:8, :] = jnp.zeros((6, feats), F32)


def output_kernel(mid_ref, hidden_a_ref, hidden_b_ref, weights_a, weights_b, out_ref, stage, sem):
    length, feats = mid_ref.shape
    count, left = hidden_a_ref.shape[1], hidden_b_ref.shape[1]
    copies = []
    for at in range(length // BLOCK):
        total = mid_ref[span(at), :] + dot(hidden_a_ref[span(at), :], weights_a[:, feats + count :], NT)
        total = total + dot(hidden_b_ref[span(at), :], weights_b[:, left:], NT)
        stage[span(at), :] = total.astype(BF16)
        copies.append(pltpu.make_async_copy(stage.at[span(at), :], out_ref.at[span(at), :], sem.at[at]))
        copies[-1].start()
    for copy in copies:
        copy.wait()


def taps_kernel(
    act_ref, mid_grad_ref, pre_grad_ref, halo_ref, win_ref, pool_win_ref, basis, fine_basis,
    coarse_basis, out_grad_ref, tap_grad_ref, z_ref, mid_bf_ref,
):
    length, feats = act_ref.shape
    blocks = length // BLOCK
    total = None
    for at in range(blocks):
        mid_bf_ref[span(at), :] = mid_grad_ref[span(at), :].astype(BF16)
        z = dot(basis[...], pre_grad_ref[span(at), :])
        z_ref[at] = z.astype(BF16)
        term = conj_product(quarters(win_ref[at]), quarters(z))
        total = term if total is None else [a + b for a, b in zip(total, term)]
    out_grad_ref[...] = dot(act_ref[...], mid_bf_ref[...], TN).astype(BF16)
    pooled = length // POOL
    z_pool = dot(basis[:, 0:pooled], halo_ref[BLOCK : BLOCK + pooled, :])
    pool_term = conj_product(quarters(pool_win_ref[...]), quarters(z_pool))
    tap_grad_ref[...] = (
        (dot(stacked(total), fine_basis[...], TN) + dot(stacked(pool_term), coarse_basis[...], TN))
        * np.float32(1 / FREQ)
    ).astype(BF16)


def backward_kernel(
    core_ref, z_ref, halo_ref, next_ref, pre_grad_ref, fine_h_ref, coarse_h_ref, basis, basis_t, back_pool,
    weights, vec_ref, vec_grad_ref, xhat_ref, out_grad_ref, tap_grad_ref, mixed_grad_ref, *rest
):
    *grad_refs, pool_ref = rest
    place = place_of(core_ref, grad_refs)
    length, feats = xhat_ref.shape
    blocks = length // BLOCK
    pooled = length // POOL
    gain, bias, skip = vec_ref[0:1, :], vec_ref[1:2, :], vec_ref[2:3, :]
    fine_q = quarters(fine_h_ref[...])
    pool_ref[0:pooled, :] = halo_ref[BLOCK : BLOCK + pooled, :]
    pool_ref[pooled : 2 * pooled, :] = next_ref[BLOCK : BLOCK + pooled, :]
    z_pool = quarters(dot(basis[...], pool_ref[...]))
    coarse_y = stacked([v * np.float32(1 / POOL) for v in conj_product(quarters(coarse_h_ref[...]), z_pool)])
    later = quarters(dot(basis[...], next_ref[0:BLOCK, :]))
    sums = jnp.zeros((8, feats), F32)
    for at in reversed(range(blocks)):
        now = quarters(z_ref[at])
        y = stacked(conj_product(fine_q, add_after(now, later)))
        later = now
        total = dot(basis_t[...], y) + dot(back_pool[span(at), :], coarse_y)
        grad_mixed = (
            total * np.float32(1 / FREQ) + skip * pre_grad_ref[span(at), :].astype(F32)
        ).astype(BF16)
        mixed_grad_ref[span(at), :] = grad_mixed
        sums = sums + jnp.sum(grad_mixed.astype(F32).reshape(BLOCK // 8, 8, feats), axis=0)
    back = dot(xhat_ref[...], mixed_grad_ref[...], TN)
    mixed_sum = jnp.sum(sums, axis=0, keepdims=True)
    padded = jnp.concatenate([vec_ref[...], vec_grad_ref[...], jnp.zeros((112, feats), F32)], axis=0)
    columns = padded.T
    put_rows(grad_refs, slice(0, feats), columns[:, 0:1] * back + columns[:, 1:2] * mixed_sum, place)
    put_rows(grad_refs, slice(feats, 2 * feats), out_grad_ref[...], place)
    put_rows(grad_refs, slice(2 * feats, 2 * feats + 256), tap_grad_ref[...], place)
    proj = weights[:, 0:feats]
    proj_f = proj.astype(F32)
    gain_grad = jnp.sum(proj_f * back, axis=1, keepdims=True)
    bias_grad = jnp.sum(proj_f * mixed_sum, axis=1, keepdims=True)
    lane = lax.broadcasted_iota(jnp.int32, (feats, 128), 1)
    columns = jnp.where(lane == 0, gain_grad, jnp.where(lane == 1, bias_grad, columns))
    put_rows(grad_refs, slice(2 * feats + 256, 2 * feats + 384), columns, place)


def input_kernel(mixed_grad_ref, weights, vec_ref, xhat_ref, inv_ref, mid_grad_ref, input_grad_ref):
    length, feats = xhat_ref.shape
    proj = weights[:, 0:feats]
    for at in range(length // BLOCK):
        grad_normed = dot(mixed_grad_ref[span(at), :], proj, NT)
        input_grad_ref[span(at), :] = mid_grad_ref[span(at), :] + norm_back(
            xhat_ref[span(at), :].astype(F32), inv_ref[span(at), 0:1], grad_normed * vec_ref[0:1, :]
        )


def final_kernel(n_mlp, param_ref, scale_ref, wide_ref, *rest):
    sources, outs = rest[: len(rest) - 10], rest[len(rest) - 10 :]
    up_ref, down_ref, in_ref, out_ref, param_grad_ref = outs[:5]
    totals = []
    for group in (sources[:n_mlp], sources[n_mlp:]):
        total = group[0][...].astype(F32)
        for source in group[1:]:
            total = total + source[...].astype(F32)
        totals.append(total)
    mlp, mixer = totals
    hidden = mlp.shape[1] // 2
    cut = first_part(hidden)
    up_ref[:, :cut], up_ref[:, cut:] = mlp[:, :cut], mlp[:, 2 * cut : cut + hidden]
    down_ref[:, :cut], down_ref[:, cut:] = mlp[:, cut : 2 * cut], mlp[:, cut + hidden :]
    feats = in_ref.shape[1]
    in_ref[...] = mixer[:, :feats]
    out_ref[...] = mixer[:, feats : 2 * feats]
    taps = param_ref.shape[1]
    tap_rows = mixer[:, 2 * feats : 2 * feats + taps]
    scale, wide = scale_ref[:, :taps], wide_ref[:, :taps]
    raw = param_ref[...].astype(F32) * scale
    inverse = lax.rsqrt(jnp.sum(raw * raw * wide, axis=1, keepdims=True) + 1e-05)
    own = raw * inverse
    along = jnp.sum(tap_rows * own, axis=1, keepdims=True)
    param_grad_ref[...] = scale * inverse * (tap_rows - wide * own * along)
    tail = mixer[:, 2 * feats + 256 :]
    rows = tail.shape[0]
    diagonal = lax.broadcasted_iota(jnp.int32, (rows, rows), 0) == lax.broadcasted_iota(
        jnp.int32, (rows, rows), 1
    )
    columns = (tail[:, 0:1], tail[:, 1:2], tap_rows[:, 0:1], tail[:, 8:9], tail[:, 9:10])
    for ref, column in zip(outs[5:], columns):
        ref[...] = jnp.sum(jnp.where(diagonal, column, 0.0), axis=0, keepdims=True)


def call(kernel, operands, outs, scratch=(), flops=0, spaces=None, limit=12, out_space=pltpu.VMEM):
    spaces = spaces or [pltpu.VMEM] * len(operands)
    operands = [
        pltpu.with_memory_space_constraint(operand, pltpu.HBM) if space is pltpu.HBM else operand
        for operand, space in zip(operands, spaces)
    ]
    return pl.pallas_call(
        kernel,
        out_shape=[jax.ShapeDtypeStruct(shape, dtype) for shape, dtype in outs],
        in_specs=[pl.BlockSpec(memory_space=space) for space in spaces],
        out_specs=[pl.BlockSpec(memory_space=out_space)] * len(outs),
        scratch_shapes=list(scratch),
        compiler_params=pltpu.CompilerParams(vmem_limit_bytes=limit << 20),
        cost_estimate=pl.CostEstimate(flops=flops, bytes_accessed=1 << 16, transcendentals=0),
    )(*operands)


def body(
    block_input,
    mixer_gain,
    mixer_bias,
    in_proj,
    kernel_param,
    skip_gain,
    out_proj,
    mlp_gain,
    mlp_bias,
    up_proj,
    down_proj,
    out_cotangent,
):
    _, length, feats = block_input.shape
    hidden = up_proj.shape[1]
    cut = first_part(hidden)
    left = hidden - cut
    blocks = length // BLOCK
    pooled = length // POOL
    taps = TAPS * SCALES
    own_rows = in_proj.shape[0]
    x_own, cot = block_input[0], out_cotangent[0]
    core_at = jnp.stack([lax.axis_index("seq"), lax.axis_index("dp")]).astype(jnp.int32)
    x_prior = lax.ppermute(x_own, "seq", [(0, 1)])
    vectors = [v.reshape(1, -1) for v in (mixer_gain, mixer_bias, skip_gain, mlp_gain, mlp_bias)]
    shard, shard_b = call(
        pack_kernel,
        [core_at, in_proj, kernel_param, out_proj, up_proj, down_proj, *vectors],
        [((own_rows, PACK + feats + 2 * cut), BF16), ((own_rows, 2 * left), BF16)],
        [
            pltpu.VMEM(kernel_param.shape, BF16), pltpu.VMEM((5, 1, own_rows), BF16),
            pltpu.SemaphoreType.DMA,
        ],
        spaces=[pltpu.SMEM] + [pltpu.HBM] * 10,
    )
    basis_np = odd_basis(np.arange(BLOCK))
    basis, basis_t = bf16_const(basis_np), bf16_const(basis_np.T)
    basis_pool = bf16_const(odd_basis(np.arange(-pooled, pooled)))
    back_pool = bf16_const(np.repeat(odd_basis(np.arange(pooled)).T, POOL, axis=0))
    fine_basis = bf16_const(tap_basis(0, 0))
    coarse_basis = bf16_const(tap_basis(OFFSET, TAPS * FINE))
    pool_rows = bf16_const(np.kron(np.eye(BLOCK // POOL), np.ones((1, POOL))) / POOL)
    scale_np = np.zeros((1, 256), np.float32)
    scale_np[0, :taps] = np.repeat(0.5 ** np.arange(SCALES), TAPS)
    wide_np = np.zeros((1, 256), np.float32)
    wide_np[0, :taps] = np.repeat(2.0 ** (np.arange(SCALES) % FINE), TAPS)

    xhat, inv_one, cot_t, cot, x_own = call(
        prepare_kernel,
        [x_own, cot],
        [
            ((length, feats), BF16), ((length, 128), F32), ((feats, length), BF16),
            ((length, feats), BF16), ((length, feats), BF16),
        ],
        [pltpu.SemaphoreType.DMA((2, blocks))],
        spaces=[pltpu.HBM] * 2,
    )
    (prior_hat,) = call(prior_kernel, [x_prior], [((length, feats), BF16)])
    held_b = jnp.concatenate(gather_plane(tie(shard_b, prior_hat)[None]))
    held = shard[None]
    for at, step in enumerate(far_steps()):
        got = from_line(held, step)
        got = tie(got, xhat) if at == 0 else got
        held = paired(held, got)
    held = tie(held, xhat, prior_hat, held_b)
    steps = far_steps()
    held_b = held_b[None]
    for step in steps[:-1]:
        held_b = gather_line(held_b, step)
    xhat_in = tie(xhat, held_b)
    first, held_a = held[:, :, :PACK], held[:, :, PACK:]
    first = gather_near(first)
    pieces_a = gather_plane(held_a)
    first = in_order(gather_core(first), False)
    smem = pltpu.SMEM
    n_first = len(first)
    weights, vec, fine_h, coarse_h, window, pool_win, act, slope = call(
        lambda *refs: forward_kernel(n_first, *refs),
        [
            core_at, xhat_in, prior_hat, basis, basis_t, basis_pool,
            back_pool, fine_basis, coarse_basis, pool_rows, jnp.asarray(scale_np), jnp.asarray(wide_np),
            *first,
        ],
        [
            ((feats, PACK), BF16), ((8, feats), F32), ((2 * FREQ, feats), BF16),
            ((2 * FREQ, feats), BF16), ((blocks, 2 * FREQ, feats), BF16), ((2 * FREQ, feats), BF16),
            ((length, feats), BF16), ((length, feats), BF16),
        ],
        [
            pltpu.VMEM((length, feats), BF16), pltpu.VMEM((2 * pooled, feats), BF16),
        ],
        flops=6 << 30,
        spaces=[smem] + [pltpu.VMEM] * (11 + n_first),
    )
    got_b = [from_line(held_b, step) for step in steps[-1:]]
    *pieces_a, act = lax.optimization_barrier((*pieces_a, act))
    pieces_a = in_order(gather_core(pieces_a, 4), False)
    *got_b, act = lax.optimization_barrier((*got_b, act))
    for got in got_b:
        held_b = paired(held_b, got)
    held_b = held_b.reshape((-1,) + held_b.shape[2:])
    pieces_b = in_order(gather_core([held_b]), True)
    n_a = len(pieces_a)
    rows = own_rows


    def grad_shapes(columns):
        if rows % 16 == 0:
            return [((feats // (2 * rows), rows, columns), BF16)] * 2
        return [((feats, columns), BF16)]

    token_f32, token_bf16 = ((length, feats), F32), ((length, feats), BF16)
    vmem = pltpu.VMEM
    proj_out, mid, xhat_two, inv_two, normed, normed_t, hidden_a, grad_up_a, weights_a, *grads_a = call(
        lambda *refs: middle_first_kernel(n_a, *refs),
        [core_at, act, x_own, cot, cot_t, vec, *pieces_a],
        [
            ((feats, feats), BF16), token_f32, token_f32, ((length, 128), F32), token_bf16,
            ((feats, length), BF16), ((length, cut), BF16), ((length, cut), BF16),
            ((feats, feats + 2 * cut), BF16), *grad_shapes(2 * cut),
        ],
        flops=8 << 30,
        spaces=[smem] + [vmem] * (5 + n_a),
    )
    n_b = len(pieces_b)
    hidden_b, grad_up_b, weights_b, *grads_b = call(
        lambda *refs: middle_second_kernel(n_b, *refs),
        [core_at, cot, cot_t, normed, normed_t, *pieces_b],
        [((length, left), BF16), ((length, left), BF16), ((feats, 2 * left), BF16), *grad_shapes(2 * left)],
        flops=16 << 30,
        spaces=[smem] + [vmem] * (4 + n_b),
    )
    near_a = reduce_core(grads_a, hidden_b)
    grad_up_b = tie(grad_up_b, *near_a)
    spread_a = spread_near(near_a)
    grad_mid, vec_grad, grad_pre, halo = call(
        middle_third_kernel,
        [slope, cot, vec, pool_rows, proj_out, xhat_two, inv_two, grad_up_a, grad_up_b, weights_a, weights_b],
        [token_f32, ((8, feats), F32), token_bf16, ((BLOCK + pooled, feats), BF16)],
        flops=4 << 30,
    )
    after = lax.ppermute(halo, "seq", [(1, 0)])
    near_b = reduce_core(grads_b, grad_mid)
    grad_pre = tie(grad_pre, *near_b)
    spread_b = spread_near(near_b)
    out_grad, tap_grad, z_grad = call(
        taps_kernel,
        [act, grad_mid, grad_pre, halo, window, pool_win, basis, fine_basis, coarse_basis],
        [
            ((feats, feats), BF16), ((feats, 256), BF16), ((blocks, 2 * FREQ, feats), BF16),
        ],
        [pltpu.VMEM((length, feats), BF16)],
        flops=2 << 24,
    )
    z_grad = tie(z_grad, after)
    grad_mixed, *grads_c = call(
        backward_kernel,
        [
            core_at, z_grad, halo, after, grad_pre, fine_h, coarse_h, basis, basis_t, back_pool, weights,
            vec, vec_grad, xhat, out_grad, tap_grad,
        ],
        [token_bf16, *grad_shapes(2 * feats + 384)],
        [pltpu.VMEM((2 * pooled, feats), BF16)],
        flops=4 << 24,
        spaces=[smem] + [vmem] * 15,
    )
    (input_grad,) = call(
        input_kernel, [grad_mixed, weights, vec, xhat, inv_one, grad_mid], [token_f32], flops=2 << 24
    )
    part_a = add_up(tie(tuple(spread_a), grad_mixed), BF16)
    part_b = add_up(tie(tuple(spread_b), input_grad), BF16)
    part_ab = jnp.concatenate([part_a, part_b], axis=2)
    steps_ab = far_steps()[::-1]
    pairs = part_ab.reshape((-1, 2) + part_ab.shape[1:])
    far_ab = [pairs[:, 0], from_line(pairs[:, 1], steps_ab[0])] if steps_ab else [part_ab]
    near_c = reduce_core(grads_c, input_grad)
    spread_c = spread_near(near_c)
    (block_output,) = call(
        output_kernel, [tie(mid, *near_c), hidden_a, hidden_b, weights_a, weights_b], [token_bf16],
        [pltpu.VMEM((length, feats), BF16), pltpu.SemaphoreType.DMA((blocks,))], flops=4 << 24, out_space=pltpu.HBM
    )
    far_c = spread_far(add_up(tie(tuple(spread_c), block_output), BF16))
    if steps_ab:
        far_ab = [far_ab[0], tie(far_ab[1], block_output)]
    for step in steps_ab[1:]:
        held = add_up(far_ab, BF16)
        pairs = held.reshape((-1, 2) + held.shape[1:])
        far_ab = [pairs[:, 0], from_line(pairs[:, 1], step)]
    far_ab = [term[0] for term in far_ab]
    vector = ((1, rows), F32)
    up_sum, down_sum, in_sum, out_sum, param_sum, *vectors = call(
        lambda *refs: final_kernel(len(far_ab), *refs),
        [kernel_param, jnp.asarray(scale_np), jnp.asarray(wide_np), *far_ab, *far_c],
        [
            ((rows, hidden), F32), ((rows, hidden), F32), ((rows, feats), F32), ((rows, feats), F32),
            ((rows, taps), F32), vector, vector, vector, vector, vector,
        ],
    )
    gain_one, bias_one, skip_sum, gain_two, bias_two = (v.reshape(rows) for v in vectors)
    return (
        block_output[None], input_grad[None], gain_one, bias_one, in_sum, param_sum, skip_sum, out_sum,
        gain_two, bias_two, up_sum, down_sum,
    )


def solution(mesh):
    rows = P(("dp", "seq"), None)
    vector = P(("dp", "seq"))
    tokens = P("dp", "seq", None)
    return jax.shard_map(
        body,
        mesh=mesh,
        in_specs=(
            tokens, vector, vector, rows, rows, vector, rows, vector, vector, rows, rows, tokens,
        ),
        out_specs=(
            tokens, tokens, vector, vector, rows, rows, vector, rows, vector, vector, rows, rows,
        ),
        check_vma=False,
    )
```

```python
import math

import jax
import jax.numpy as jnp
import numpy as np
from jax import lax
from jax.experimental import pallas as pl
from jax.experimental.pallas import tpu as pltpu
from jax.sharding import PartitionSpec as P

TAPS = 32
SCALES = 6
FINE = 3
FREQ = 256
HALF = FREQ // 2
BLOCK = 256
POOL = 8
OFFSET = 28
TILE = 512
WIDE = 512
PACK = 768
F32 = jnp.float32
BF16 = jnp.bfloat16
NT = ((1,), (1,))
TN = ((0,), (0,))


def odd_basis(positions):
    order = np.concatenate([np.arange(0, FREQ, 2), np.arange(1, FREQ, 2)])
    angle = np.pi * np.outer(order + 0.5, positions) / FREQ
    return np.concatenate([np.cos(angle), -np.sin(angle)], axis=0)


def tap_basis(start, first):
    columns = np.zeros((2 * FREQ, 256))
    for scale_at in range(FINE):
        wide = 2**scale_at
        lag = start + TAPS * (wide - 1)
        for tap in range(TAPS):
            at = first + scale_at * TAPS + tap
            columns[:, at] = odd_basis(lag + tap * wide + np.arange(wide)).sum(axis=1)
    return columns


def bf16_const(array):
    return jnp.asarray(np.asarray(array, np.float32).astype(jnp.bfloat16))


def dot(a, b, contract=((1,), (0,))):
    return lax.dot_general(a, b, (contract, ((), ())), preferred_element_type=F32)


def normal_parts(values):
    cdf = 0.5 + 0.5 * lax.erf(values * np.float32(math.sqrt(0.5)))
    pdf = jnp.exp(-0.5 * values * values) * np.float32(1 / math.sqrt(2 * math.pi))
    return cdf, pdf


def split_dp(count):
    edge = round((count / 2) ** (1 / 3))
    return (2 * edge, edge * edge) if 2 * edge**3 == count else (1, count)


def swap_route(count, mask):
    return [(i, i ^ mask) for i in range(count)]


SWAP = [(0, 1), (1, 0)]


def tie(value, *others):
    return lax.optimization_barrier((value, *others))[0]


def far_steps():
    nz, _ = split_dp(lax.axis_size("dp"))
    return [1 << bit for bit in reversed(range(nz.bit_length() - 1))]


def from_line(held, step):
    dp_count = lax.axis_size("dp")
    _, nxy = split_dp(dp_count)
    return lax.ppermute(held, "dp", swap_route(dp_count, step * nxy))


def paired(held, got):
    return jnp.stack([held, got], axis=1).reshape((-1,) + held.shape[1:])


def gather_line(held, step):
    return paired(held, from_line(held, step))


def gather_far(shard):
    held = shard[None]
    for step in far_steps():
        held = gather_line(held, step)
    return held


def gather_near(held):
    dp_count = lax.axis_size("dp")
    _, nxy = split_dp(dp_count)
    return [held] + [lax.ppermute(held, "dp", swap_route(dp_count, k)) for k in range(1, nxy)]


def gather_core(pieces, parts=1):
    held = jnp.concatenate(pieces)
    size = held.shape[0] // parts
    held = [held[at * size : (at + 1) * size] for at in range(parts)]
    return held + [lax.ppermute(part, "seq", SWAP) for part in held]


def gather_plane(held):
    dp_count = lax.axis_size("dp")
    _, nxy = split_dp(dp_count)
    if nxy != 4:
        return gather_near(held)
    by_x = lax.ppermute(held, "dp", swap_route(dp_count, 1))
    by_y = lax.ppermute(held, "dp", swap_route(dp_count, 2))
    if held.shape[0] == 1:
        return [held, by_x, by_y, lax.ppermute(by_y, "dp", swap_route(dp_count, 1))]
    cut = held.shape[0] // 2
    return [
        held, by_x, by_y, lax.ppermute(by_y[:cut], "dp", swap_route(dp_count, 1)),
        lax.ppermute(by_x[cut:], "dp", swap_route(dp_count, 2)),
    ]


def row_place(at, count, plane_first, core_ref):
    nz, nxy = split_dp(count)
    other, at = divmod(at, count)
    if plane_first:
        z, xy = divmod(at, nxy)
    else:
        xy, z = divmod(at, nz)
    return ((z * nxy + xy) ^ core_ref[1]) * 2 + (other ^ core_ref[0])


def in_order(pieces, plane_first):
    if pieces[0].shape[1] % 16 == 0:
        return pieces
    dp_count = lax.axis_size("dp")
    nz, nxy = split_dp(dp_count)
    me, core = lax.axis_index("dp"), lax.axis_index("seq")
    by_dp = jnp.arange(dp_count).reshape(nz, nxy) ^ me
    by_dp = by_dp if plane_first else by_dp.T
    where = by_dp[None] * 2 + (jnp.arange(2)[:, None, None] ^ core)
    flat = jnp.concatenate(pieces)
    return [jnp.take(flat, jnp.argsort(where.reshape(-1)), axis=0).reshape(1, -1, flat.shape[2])]


def reduce_core(grads, *before):
    dp_count = lax.axis_size("dp")
    nz, nxy = split_dp(dp_count)
    if len(grads) == 1:
        core, me = lax.axis_index("seq"), lax.axis_index("dp")
        shaped = grads[0].reshape(dp_count, 2, -1, grads[0].shape[1])
        order = (jnp.arange(nz)[None, :] * nxy + jnp.arange(nxy)[:, None]) ^ me
        shaped = jnp.take(shaped, order.reshape(-1), axis=0)
        grads = [
            lax.dynamic_index_in_dim(shaped, 1 - core, 1, False),
            lax.dynamic_index_in_dim(shaped, core, 1, False),
        ]
    send, keep = grads
    got = lax.ppermute(send, "seq", SWAP)
    got = tie(got, *before)
    total = (keep.astype(F32) + got.astype(F32)).astype(BF16)
    return [total[k * nz : (k + 1) * nz] for k in range(nxy)]


def spread_near(pieces):
    dp_count = lax.axis_size("dp")
    return [pieces[0]] + [
        lax.ppermute(pieces[k], "dp", swap_route(dp_count, k)) for k in range(1, len(pieces))
    ]


def spread_far(part):
    dp_count = lax.axis_size("dp")
    nz, nxy = split_dp(dp_count)
    return [part[0]] + [
        lax.ppermute(part[k], "dp", swap_route(dp_count, k * nxy)) for k in range(1, nz)
    ]


def add_up(pieces, dtype=F32):
    total = pieces[0].astype(F32)
    for piece in pieces[1:]:
        total = total + piece.astype(F32)
    return total.astype(dtype)


def load_rows(core_ref, pieces, target, plane_first):
    if len(pieces) == 1:
        target[...] = pieces[0][0]
        return
    count = target.shape[0] // (2 * pieces[0].shape[1])
    at = 0
    for piece in pieces:
        held, rows, _ = piece.shape
        for i in range(held):
            start = row_place(at, count, plane_first, core_ref) * rows
            target[pl.ds(pl.multiple_of(start, 16), rows), :] = piece[i]
            at += 1


def span(at, size=BLOCK):
    return pl.ds(at * size, size)


def norm_stats(features):
    centre = features - jnp.mean(features, axis=-1, keepdims=True)
    inverse = lax.rsqrt(jnp.mean(centre * centre, axis=-1, keepdims=True) + 1e-05)
    return centre * inverse, inverse


def norm_back(xhat, inverse, scaled):
    return inverse * (
        scaled
        - jnp.mean(scaled, axis=-1, keepdims=True)
        - xhat * jnp.mean(scaled * xhat, axis=-1, keepdims=True)
    )


def quarters(spectrum):
    return [spectrum[i * HALF : (i + 1) * HALF].astype(F32) for i in range(4)]


def add_before(now, past):
    (re, ro, ie, io), (pre, pro, pie, pio) = now, past
    return re - pie, ro + pio, ie + pre, io - pro


def add_after(now, later):
    (re, ro, ie, io), (nre, nro, nie, nio) = now, later
    return re + nie, ro - nio, ie - nre, io + nro


def product(a, b):
    (are, aro, aie, aio), (bre, bro, bie, bio) = a, b
    return (
        are * bre - aie * bie,
        aro * bro - aio * bio,
        are * bie + aie * bre,
        aro * bio + aio * bro,
    )


def conj_product(a, b):
    (are, aro, aie, aio), (bre, bro, bie, bio) = a, b
    return (
        are * bre + aie * bie,
        aro * bro + aio * bio,
        are * bie - aie * bre,
        aro * bio - aio * bro,
    )


def stacked(parts):
    return jnp.concatenate([part.astype(BF16) for part in parts], axis=0)


def put_quarters(ref, at, parts):
    for i, part in enumerate(parts):
        ref[at, i * HALF : (i + 1) * HALF, :] = part.astype(ref.dtype)


def first_part(hidden):
    return hidden // 2


def pack_kernel(core_ref, in_ref, param_ref, out_ref, up_ref, down_ref, *rest):
    vectors, (a_ref, b_ref, param, small, sem) = rest[:5], rest[5:]
    rows, feats = in_ref.shape
    cut = first_part(up_ref.shape[1])
    left = up_ref.shape[1] - cut
    copies = [
        pltpu.make_async_copy(in_ref, a_ref.at[:, pl.ds(0, feats)], sem),
        pltpu.make_async_copy(param_ref, param, sem),
    ]
    for i, vector in enumerate(vectors):
        copies.append(pltpu.make_async_copy(vector, small.at[i], sem))
    for source, start, size, target, at in (
        (out_ref, 0, feats, a_ref, PACK), (up_ref, 0, cut, a_ref, PACK + feats),
        (down_ref, 0, cut, a_ref, PACK + feats + cut), (up_ref, cut, left, b_ref, 0),
        (down_ref, cut, left, b_ref, left),
    ):
        copies.append(
            pltpu.make_async_copy(
                source.at[:, pl.ds(start, size)], target.at[:, pl.ds(at, size)], sem
            )
        )
    for copy in copies:
        copy.start()
    for copy in copies:
        copy.wait()
    spare = PACK - feats - param.shape[1]
    row = lax.broadcasted_iota(jnp.int32, (rows, rows), 0)
    lane = lax.broadcasted_iota(jnp.int32, (rows, rows), 1)
    slot = lax.broadcasted_iota(jnp.int32, (rows, spare), 1)
    block = jnp.zeros((rows, spare), F32)
    for i in range(len(vectors)):
        value = small[i].astype(F32)
        column = jnp.sum(jnp.where(row == lane, value, 0.0), axis=1, keepdims=True)
        block = jnp.where(slot == i, column, block)
    tail = jnp.concatenate([param[...].astype(F32), block], axis=1)
    a_ref[:, feats:PACK] = tail.astype(BF16)


def prepare_kernel(x_ref, cot_ref, xhat_ref, inv_ref, cot_t_ref, cot_copy, x_copy, sem):
    blocks = x_ref.shape[0] // BLOCK
    copies = []
    for source, target, which in ((x_ref, x_copy, 0), (cot_ref, cot_copy, 1)):
        for at in range(blocks):
            copies.append(
                pltpu.make_async_copy(source.at[span(at), :], target.at[span(at), :], sem.at[which, at])
            )
    for copy in copies:
        copy.start()
    for at in range(blocks):
        copies[at].wait()
        xhat, inverse = norm_stats(x_copy[span(at), :].astype(F32))
        xhat_ref[span(at), :] = xhat.astype(BF16)
        inv_ref[span(at), :] = jnp.broadcast_to(inverse, (BLOCK, 128))
    for at in range(blocks):
        copies[blocks + at].wait()
        cot_t_ref[:, span(at)] = cot_copy[span(at), :].T


def prior_kernel(x_ref, xhat_ref):
    for at in range(x_ref.shape[0] // BLOCK):
        xhat_ref[span(at), :] = norm_stats(x_ref[span(at), :].astype(F32))[0].astype(BF16)


def forward_kernel(
    n_pieces, core_ref, xhat_ref, prior_ref, basis, basis_t, basis_pool, back_pool,
    fine_basis, coarse_basis, pool_rows, scale_ref, wide_ref, *rest,
):
    pieces, rest = rest[:n_pieces], rest[n_pieces:]
    weights, vec_ref, fine_h_ref, coarse_h_ref, win_ref, pool_win_ref, act_ref, slope_ref = rest[:8]
    mixed_ref, pooled_ref = rest[8:]
    load_rows(core_ref, pieces, weights, False)
    feats = xhat_ref.shape[1]
    blocks = xhat_ref.shape[0] // BLOCK
    tail = weights[:, feats : feats + 256].astype(F32)
    raw = tail * scale_ref[...]
    inverse = lax.rsqrt(jnp.sum(raw * raw * wide_ref[...], axis=1, keepdims=True) + 1e-05)
    taps = (raw * inverse).astype(BF16)
    vec = tail[:, 128:256].T[64:72]
    vec_ref[...] = vec
    gain, bias, skip = vec[0:1], vec[1:2], vec[2:3]
    fine_h = dot(fine_basis[...], taps, NT)
    coarse_h = dot(coarse_basis[...], taps, NT)
    fine_h_ref[...] = fine_h.astype(BF16)
    coarse_h_ref[...] = coarse_h.astype(BF16)
    proj = weights[:, :feats]
    has_prior = core_ref[0].astype(F32)
    per = BLOCK // POOL
    past = None
    total = dot((prior_ref[...].astype(F32) * gain + bias).astype(BF16), proj)
    for at in range(blocks):
        mixed = (total[at * BLOCK : (at + 1) * BLOCK] * has_prior).astype(BF16)
        pooled_ref[span(at, per), :] = dot(pool_rows[...], mixed).astype(BF16)
        if at == blocks - 1:
            past = quarters(dot(basis[...], mixed))
    total = dot((xhat_ref[...].astype(F32) * gain + bias).astype(BF16), proj)
    for at in range(blocks):
        mixed = total[at * BLOCK : (at + 1) * BLOCK].astype(BF16)
        mixed_ref[span(at), :] = mixed
        pooled_ref[span(blocks + at, per), :] = dot(pool_rows[...], mixed).astype(BF16)
    pool_win = dot(basis_pool[...], pooled_ref[...])
    pool_win_ref[...] = pool_win.astype(BF16)
    coarse_y = stacked(product(quarters(coarse_h), quarters(pool_win)))
    fine_q = quarters(fine_h)
    for at in range(blocks):
        mixed = mixed_ref[span(at), :]
        now = quarters(dot(basis[...], mixed))
        window = add_before(now, past)
        past = now
        put_quarters(win_ref, at, window)
        total = dot(basis_t[...], stacked(product(fine_q, window)))
        total = total + dot(back_pool[span(at), :], coarse_y)
        pre_act = total * np.float32(1 / FREQ) + skip * mixed.astype(F32)
        cdf, pdf = normal_parts(pre_act)
        act_ref[span(at), :] = (pre_act * cdf).astype(BF16)
        slope_ref[span(at), :] = (cdf + pre_act * pdf).astype(BF16)


def place_of(core_ref, grad_refs):
    nz, nxy = split_dp(grad_refs[0].shape[0])
    return core_ref[0], core_ref[1] // nxy, core_ref[1] % nxy, nz, nxy


def put_rows(refs, columns, value, place):
    value = value.astype(BF16)
    if len(refs) == 1:
        refs[0][:, columns] = value
        return
    send_ref, keep_ref = refs
    count, rows, _ = send_ref.shape
    core, me_z, me_xy, nz, nxy = place
    for at in range(count):
        slot = ((at % nxy) ^ me_xy) * nz + ((at // nxy) ^ me_z)
        first = value[2 * at * rows : (2 * at + 1) * rows]
        second = value[(2 * at + 1) * rows : (2 * at + 2) * rows]
        send_ref[slot, :, columns] = jnp.where(core == 0, second, first)
        keep_ref[slot, :, columns] = jnp.where(core == 0, first, second)


def hidden_part(place, normed_ref, normed_t_ref, cot_ref, cot_t_ref, up_at, down_at, weights, hidden_ref, grad_up_ref, grad_refs):
    length = normed_ref.shape[0]
    count = hidden_ref.shape[1]
    for at in range(0, count, WIDE):
        wide = min(WIDE, count - at)
        columns = slice(at, at + wide)
        up = weights[:, up_at + at : up_at + at + wide]
        down = weights[:, down_at + at : down_at + at + wide]
        for row in range(0, length, TILE):
            rows = slice(row, row + TILE)
            up_val = dot(normed_ref[rows, :], up)
            grad_hidden = dot(cot_ref[rows, :], down)
            cdf, pdf = normal_parts(up_val)
            hidden_ref[rows, columns] = (up_val * cdf).astype(BF16)
            grad_up_ref[rows, columns] = (grad_hidden * (cdf + up_val * pdf)).astype(BF16)
        put_rows(grad_refs, slice(at, at + wide), dot(normed_t_ref[...], grad_up_ref[:, columns]), place)
        put_rows(grad_refs, slice(count + at, count + at + wide), dot(cot_t_ref[...], hidden_ref[:, columns]), place)


def middle_first_kernel(
    n_pieces, core_ref, act_ref, x_ref, cot_ref, cot_t_ref, vec_ref, *rest
):
    pieces, rest = rest[:n_pieces], rest[n_pieces:]
    (proj_ref, mid_ref, xhat_ref, inv_ref, normed_ref, normed_t_ref, hidden_ref, grad_up_ref), rest = rest[:8], rest[8:]
    weights, *grad_refs = rest
    load_rows(core_ref, pieces, weights, False)
    length, feats = x_ref.shape
    count = hidden_ref.shape[1]
    gain, bias = vec_ref[3:4, :], vec_ref[4:5, :]
    proj_ref[...] = weights[:, :feats]
    for at in range(length // BLOCK):
        mid = x_ref[span(at), :].astype(F32) + dot(act_ref[span(at), :], proj_ref[...])
        xhat, inverse = norm_stats(mid)
        normed = (xhat * gain + bias).astype(BF16)
        mid_ref[span(at), :] = mid
        xhat_ref[span(at), :] = xhat
        inv_ref[span(at), :] = jnp.broadcast_to(inverse, (BLOCK, 128))
        normed_ref[span(at), :] = normed
        normed_t_ref[:, span(at)] = normed.T
    hidden_part(
        place_of(core_ref, grad_refs), normed_ref, normed_t_ref, cot_ref, cot_t_ref, feats, feats + count,
        weights, hidden_ref, grad_up_ref, grad_refs,
    )


def middle_second_kernel(
    n_pieces, core_ref, cot_ref, cot_t_ref, normed_ref, normed_t_ref, *rest
):
    pieces, rest = rest[:n_pieces], rest[n_pieces:]
    hidden_ref, grad_up_ref, weights, *grad_refs = rest
    load_rows(core_ref, pieces, weights, True)
    hidden_part(
        place_of(core_ref, grad_refs), normed_ref, normed_t_ref, cot_ref, cot_t_ref, 0,
        hidden_ref.shape[1], weights, hidden_ref, grad_up_ref, grad_refs,
    )


def middle_third_kernel(
    slope_ref, cot_ref, vec_ref, pool_rows, proj_ref, xhat_ref, inv_ref, up_a_ref, up_b_ref, weights_a,
    weights_b, mid_grad_ref, vec_grad_ref, pre_grad_ref, halo_ref,
):
    length, feats = xhat_ref.shape
    count, left = up_a_ref.shape[1], up_b_ref.shape[1]
    gain = vec_ref[3:4, :]
    gain_grad = jnp.zeros((8, feats), F32)
    bias_grad = jnp.zeros((8, feats), F32)
    per = BLOCK // POOL
    for at in range(length // BLOCK):
        grad_normed = dot(up_a_ref[span(at), :], weights_a[:, feats : feats + count], NT)
        grad_normed = grad_normed + dot(up_b_ref[span(at), :], weights_b[:, :left], NT)
        xhat = xhat_ref[span(at), :]
        bias_grad = bias_grad + jnp.sum(grad_normed.reshape(BLOCK // 8, 8, feats), axis=0)
        gain_grad = gain_grad + jnp.sum((grad_normed * xhat).reshape(BLOCK // 8, 8, feats), axis=0)
        grad_mid = cot_ref[span(at), :].astype(F32) + norm_back(
            xhat, inv_ref[span(at), 0:1], grad_normed * gain
        )
        mid_grad_ref[span(at), :] = grad_mid
        grad_act = dot(grad_mid.astype(BF16), proj_ref[...], NT)
        grad_pre = (grad_act * slope_ref[span(at), :].astype(F32)).astype(BF16)
        pre_grad_ref[span(at), :] = grad_pre
        if at == 0:
            halo_ref[0:BLOCK, :] = grad_pre
        halo_ref[pl.ds(BLOCK + at * per, per), :] = (
            dot(pool_rows[...], grad_pre) * np.float32(POOL)
        ).astype(BF16)
    vec_grad_ref[0:1, :] = jnp.sum(gain_grad, axis=0, keepdims=True)
    vec_grad_ref[1:2, :] = jnp.sum(bias_grad, axis=0, keepdims=True)
    vec_grad_ref[2:8, :] = jnp.zeros((6, feats), F32)


def output_kernel(mid_ref, hidden_a_ref, hidden_b_ref, weights_a, weights_b, out_ref, stage, sem):
    length, feats = mid_ref.shape
    count, left = hidden_a_ref.shape[1], hidden_b_ref.shape[1]
    copies = []
    for at in range(length // BLOCK):
        total = mid_ref[span(at), :] + dot(hidden_a_ref[span(at), :], weights_a[:, feats + count :], NT)
        total = total + dot(hidden_b_ref[span(at), :], weights_b[:, left:], NT)
        stage[span(at), :] = total.astype(BF16)
        copies.append(pltpu.make_async_copy(stage.at[span(at), :], out_ref.at[span(at), :], sem.at[at]))
        copies[-1].start()
    for copy in copies:
        copy.wait()


def taps_kernel(
    act_ref, mid_grad_ref, pre_grad_ref, halo_ref, win_ref, pool_win_ref, basis, fine_basis,
    coarse_basis, out_grad_ref, tap_grad_ref, z_ref, mid_bf_ref,
):
    length, feats = act_ref.shape
    blocks = length // BLOCK
    total = None
    for at in range(blocks):
        mid_bf_ref[span(at), :] = mid_grad_ref[span(at), :].astype(BF16)
        z = dot(basis[...], pre_grad_ref[span(at), :])
        z_ref[at] = z.astype(BF16)
        term = conj_product(quarters(win_ref[at]), quarters(z))
        total = term if total is None else [a + b for a, b in zip(total, term)]
    out_grad_ref[...] = dot(act_ref[...], mid_bf_ref[...], TN).astype(BF16)
    pooled = length // POOL
    z_pool = dot(basis[:, 0:pooled], halo_ref[BLOCK : BLOCK + pooled, :])
    pool_term = conj_product(quarters(pool_win_ref[...]), quarters(z_pool))
    tap_grad_ref[...] = (
        (dot(stacked(total), fine_basis[...], TN) + dot(stacked(pool_term), coarse_basis[...], TN))
        * np.float32(1 / FREQ)
    ).astype(BF16)


def backward_kernel(
    core_ref, z_ref, halo_ref, next_ref, pre_grad_ref, fine_h_ref, coarse_h_ref, basis, basis_t, back_pool,
    weights, vec_ref, vec_grad_ref, xhat_ref, out_grad_ref, tap_grad_ref, mixed_grad_ref, *rest
):
    *grad_refs, pool_ref = rest
    place = place_of(core_ref, grad_refs)
    length, feats = xhat_ref.shape
    blocks = length // BLOCK
    pooled = length // POOL
    gain, bias, skip = vec_ref[0:1, :], vec_ref[1:2, :], vec_ref[2:3, :]
    fine_q = quarters(fine_h_ref[...])
    pool_ref[0:pooled, :] = halo_ref[BLOCK : BLOCK + pooled, :]
    pool_ref[pooled : 2 * pooled, :] = next_ref[BLOCK : BLOCK + pooled, :]
    z_pool = quarters(dot(basis[...], pool_ref[...]))
    coarse_y = stacked([v * np.float32(1 / POOL) for v in conj_product(quarters(coarse_h_ref[...]), z_pool)])
    later = quarters(dot(basis[...], next_ref[0:BLOCK, :]))
    sums = jnp.zeros((8, feats), F32)
    for at in reversed(range(blocks)):
        now = quarters(z_ref[at])
        y = stacked(conj_product(fine_q, add_after(now, later)))
        later = now
        total = dot(basis_t[...], y) + dot(back_pool[span(at), :], coarse_y)
        grad_mixed = (
            total * np.float32(1 / FREQ) + skip * pre_grad_ref[span(at), :].astype(F32)
        ).astype(BF16)
        mixed_grad_ref[span(at), :] = grad_mixed
        sums = sums + jnp.sum(grad_mixed.astype(F32).reshape(BLOCK // 8, 8, feats), axis=0)
    back = dot(xhat_ref[...], mixed_grad_ref[...], TN)
    mixed_sum = jnp.sum(sums, axis=0, keepdims=True)
    padded = jnp.concatenate([vec_ref[...], vec_grad_ref[...], jnp.zeros((112, feats), F32)], axis=0)
    columns = padded.T
    put_rows(grad_refs, slice(0, feats), columns[:, 0:1] * back + columns[:, 1:2] * mixed_sum, place)
    put_rows(grad_refs, slice(feats, 2 * feats), out_grad_ref[...], place)
    put_rows(grad_refs, slice(2 * feats, 2 * feats + 256), tap_grad_ref[...], place)
    proj = weights[:, 0:feats]
    proj_f = proj.astype(F32)
    gain_grad = jnp.sum(proj_f * back, axis=1, keepdims=True)
    bias_grad = jnp.sum(proj_f * mixed_sum, axis=1, keepdims=True)
    lane = lax.broadcasted_iota(jnp.int32, (feats, 128), 1)
    columns = jnp.where(lane == 0, gain_grad, jnp.where(lane == 1, bias_grad, columns))
    put_rows(grad_refs, slice(2 * feats + 256, 2 * feats + 384), columns, place)


def input_kernel(mixed_grad_ref, weights, vec_ref, xhat_ref, inv_ref, mid_grad_ref, input_grad_ref):
    length, feats = xhat_ref.shape
    proj = weights[:, 0:feats]
    for at in range(length // BLOCK):
        grad_normed = dot(mixed_grad_ref[span(at), :], proj, NT)
        input_grad_ref[span(at), :] = mid_grad_ref[span(at), :] + norm_back(
            xhat_ref[span(at), :].astype(F32), inv_ref[span(at), 0:1], grad_normed * vec_ref[0:1, :]
        )


def final_kernel(n_mlp, param_ref, scale_ref, wide_ref, *rest):
    sources, outs = rest[: len(rest) - 10], rest[len(rest) - 10 :]
    up_ref, down_ref, in_ref, out_ref, param_grad_ref = outs[:5]
    totals = []
    for group in (sources[:n_mlp], sources[n_mlp:]):
        total = group[0][...].astype(F32)
        for source in group[1:]:
            total = total + source[...].astype(F32)
        totals.append(total)
    mlp, mixer = totals
    hidden = mlp.shape[1] // 2
    cut = first_part(hidden)
    up_ref[:, :cut], up_ref[:, cut:] = mlp[:, :cut], mlp[:, 2 * cut : cut + hidden]
    down_ref[:, :cut], down_ref[:, cut:] = mlp[:, cut : 2 * cut], mlp[:, cut + hidden :]
    feats = in_ref.shape[1]
    in_ref[...] = mixer[:, :feats]
    out_ref[...] = mixer[:, feats : 2 * feats]
    taps = param_ref.shape[1]
    tap_rows = mixer[:, 2 * feats : 2 * feats + taps]
    scale, wide = scale_ref[:, :taps], wide_ref[:, :taps]
    raw = param_ref[...].astype(F32) * scale
    inverse = lax.rsqrt(jnp.sum(raw * raw * wide, axis=1, keepdims=True) + 1e-05)
    own = raw * inverse
    along = jnp.sum(tap_rows * own, axis=1, keepdims=True)
    param_grad_ref[...] = scale * inverse * (tap_rows - wide * own * along)
    tail = mixer[:, 2 * feats + 256 :]
    rows = tail.shape[0]
    diagonal = lax.broadcasted_iota(jnp.int32, (rows, rows), 0) == lax.broadcasted_iota(
        jnp.int32, (rows, rows), 1
    )
    columns = (tail[:, 0:1], tail[:, 1:2], tap_rows[:, 0:1], tail[:, 8:9], tail[:, 9:10])
    for ref, column in zip(outs[5:], columns):
        ref[...] = jnp.sum(jnp.where(diagonal, column, 0.0), axis=0, keepdims=True)


def call(kernel, operands, outs, scratch=(), flops=0, spaces=None, limit=12, out_space=pltpu.VMEM):
    spaces = spaces or [pltpu.VMEM] * len(operands)
    operands = [
        pltpu.with_memory_space_constraint(operand, pltpu.HBM) if space is pltpu.HBM else operand
        for operand, space in zip(operands, spaces)
    ]
    return pl.pallas_call(
        kernel,
        out_shape=[jax.ShapeDtypeStruct(shape, dtype) for shape, dtype in outs],
        in_specs=[pl.BlockSpec(memory_space=space) for space in spaces],
        out_specs=[pl.BlockSpec(memory_space=out_space)] * len(outs),
        scratch_shapes=list(scratch),
        compiler_params=pltpu.CompilerParams(vmem_limit_bytes=limit << 20),
        cost_estimate=pl.CostEstimate(flops=flops, bytes_accessed=1 << 16, transcendentals=0),
    )(*operands)


def body(
    block_input,
    mixer_gain,
    mixer_bias,
    in_proj,
    kernel_param,
    skip_gain,
    out_proj,
    mlp_gain,
    mlp_bias,
    up_proj,
    down_proj,
    out_cotangent,
):
    _, length, feats = block_input.shape
    hidden = up_proj.shape[1]
    cut = first_part(hidden)
    left = hidden - cut
    blocks = length // BLOCK
    pooled = length // POOL
    taps = TAPS * SCALES
    own_rows = in_proj.shape[0]
    x_own, cot = block_input[0], out_cotangent[0]
    core_at = jnp.stack([lax.axis_index("seq"), lax.axis_index("dp")]).astype(jnp.int32)
    x_prior = lax.ppermute(x_own, "seq", [(0, 1)])
    vectors = [v.reshape(1, -1) for v in (mixer_gain, mixer_bias, skip_gain, mlp_gain, mlp_bias)]
    shard, shard_b = call(
        pack_kernel,
        [core_at, in_proj, kernel_param, out_proj, up_proj, down_proj, *vectors],
        [((own_rows, PACK + feats + 2 * cut), BF16), ((own_rows, 2 * left), BF16)],
        [
            pltpu.VMEM(kernel_param.shape, BF16), pltpu.VMEM((5, 1, own_rows), BF16),
            pltpu.SemaphoreType.DMA,
        ],
        spaces=[pltpu.SMEM] + [pltpu.HBM] * 10,
    )
    basis_np = odd_basis(np.arange(BLOCK))
    basis, basis_t = bf16_const(basis_np), bf16_const(basis_np.T)
    basis_pool = bf16_const(odd_basis(np.arange(-pooled, pooled)))
    back_pool = bf16_const(np.repeat(odd_basis(np.arange(pooled)).T, POOL, axis=0))
    fine_basis = bf16_const(tap_basis(0, 0))
    coarse_basis = bf16_const(tap_basis(OFFSET, TAPS * FINE))
    pool_rows = bf16_const(np.kron(np.eye(BLOCK // POOL), np.ones((1, POOL))) / POOL)
    scale_np = np.zeros((1, 256), np.float32)
    scale_np[0, :taps] = np.repeat(0.5 ** np.arange(SCALES), TAPS)
    wide_np = np.zeros((1, 256), np.float32)
    wide_np[0, :taps] = np.repeat(2.0 ** (np.arange(SCALES) % FINE), TAPS)

    xhat, inv_one, cot_t, cot, x_own = call(
        prepare_kernel,
        [x_own, cot],
        [
            ((length, feats), BF16), ((length, 128), F32), ((feats, length), BF16),
            ((length, feats), BF16), ((length, feats), BF16),
        ],
        [pltpu.SemaphoreType.DMA((2, blocks))],
        spaces=[pltpu.HBM] * 2,
    )
    (prior_hat,) = call(prior_kernel, [x_prior], [((length, feats), BF16)])
    held_b = jnp.concatenate(gather_near(tie(shard_b, prior_hat)[None]))
    held = shard[None]
    for at, step in enumerate(far_steps()):
        got = from_line(held, step)
        got = tie(got, xhat) if at == 0 else got
        held = paired(held, got)
    held = tie(held, xhat, prior_hat, held_b)
    steps = far_steps()
    held_b = held_b[None]
    for step in steps[:-1]:
        held_b = gather_line(held_b, step)
    xhat_in = tie(xhat, held_b)
    first, held_a = held[:, :, :PACK], held[:, :, PACK:]
    first = gather_near(first)
    pieces_a = gather_plane(held_a)
    first = in_order(gather_core(first), False)
    smem = pltpu.SMEM
    n_first = len(first)
    weights, vec, fine_h, coarse_h, window, pool_win, act, slope = call(
        lambda *refs: forward_kernel(n_first, *refs),
        [
            core_at, xhat_in, prior_hat, basis, basis_t, basis_pool,
            back_pool, fine_basis, coarse_basis, pool_rows, jnp.asarray(scale_np), jnp.asarray(wide_np),
            *first,
        ],
        [
            ((feats, PACK), BF16), ((8, feats), F32), ((2 * FREQ, feats), BF16),
            ((2 * FREQ, feats), BF16), ((blocks, 2 * FREQ, feats), BF16), ((2 * FREQ, feats), BF16),
            ((length, feats), BF16), ((length, feats), BF16),
        ],
        [
            pltpu.VMEM((length, feats), BF16), pltpu.VMEM((2 * pooled, feats), BF16),
        ],
        flops=6 << 30,
        spaces=[smem] + [pltpu.VMEM] * (11 + n_first),
    )
    got_b = [from_line(held_b, step) for step in steps[-1:]]
    *pieces_a, act = lax.optimization_barrier((*pieces_a, act))
    pieces_a = in_order(gather_core(pieces_a, 4), False)
    *got_b, act = lax.optimization_barrier((*got_b, act))
    for got in got_b:
        held_b = paired(held_b, got)
    held_b = held_b.reshape((-1,) + held_b.shape[2:])
    pieces_b = in_order(gather_core([held_b]), True)
    n_a = len(pieces_a)
    rows = own_rows


    def grad_shapes(columns):
        if rows % 16 == 0:
            return [((feats // (2 * rows), rows, columns), BF16)] * 2
        return [((feats, columns), BF16)]

    token_f32, token_bf16 = ((length, feats), F32), ((length, feats), BF16)
    vmem = pltpu.VMEM
    proj_out, mid, xhat_two, inv_two, normed, normed_t, hidden_a, grad_up_a, weights_a, *grads_a = call(
        lambda *refs: middle_first_kernel(n_a, *refs),
        [core_at, act, x_own, cot, cot_t, vec, *pieces_a],
        [
            ((feats, feats), BF16), token_f32, token_f32, ((length, 128), F32), token_bf16,
            ((feats, length), BF16), ((length, cut), BF16), ((length, cut), BF16),
            ((feats, feats + 2 * cut), BF16), *grad_shapes(2 * cut),
        ],
        flops=8 << 30,
        spaces=[smem] + [vmem] * (5 + n_a),
    )
    n_b = len(pieces_b)
    hidden_b, grad_up_b, weights_b, *grads_b = call(
        lambda *refs: middle_second_kernel(n_b, *refs),
        [core_at, cot, cot_t, normed, normed_t, *pieces_b],
        [((length, left), BF16), ((length, left), BF16), ((feats, 2 * left), BF16), *grad_shapes(2 * left)],
        flops=16 << 30,
        spaces=[smem] + [vmem] * (4 + n_b),
    )
    near_a = reduce_core(grads_a, hidden_b)
    grad_up_b = tie(grad_up_b, *near_a)
    spread_a = spread_near(near_a)
    grad_mid, vec_grad, grad_pre, halo = call(
        middle_third_kernel,
        [slope, cot, vec, pool_rows, proj_out, xhat_two, inv_two, grad_up_a, grad_up_b, weights_a, weights_b],
        [token_f32, ((8, feats), F32), token_bf16, ((BLOCK + pooled, feats), BF16)],
        flops=4 << 30,
    )
    after = lax.ppermute(halo, "seq", [(1, 0)])
    near_b = reduce_core(grads_b, grad_mid)
    grad_pre = tie(grad_pre, *near_b)
    spread_b = spread_near(near_b)
    out_grad, tap_grad, z_grad = call(
        taps_kernel,
        [act, grad_mid, grad_pre, halo, window, pool_win, basis, fine_basis, coarse_basis],
        [
            ((feats, feats), BF16), ((feats, 256), BF16), ((blocks, 2 * FREQ, feats), BF16),
        ],
        [pltpu.VMEM((length, feats), BF16)],
        flops=2 << 24,
    )
    z_grad = tie(z_grad, after)
    grad_mixed, *grads_c = call(
        backward_kernel,
        [
            core_at, z_grad, halo, after, grad_pre, fine_h, coarse_h, basis, basis_t, back_pool, weights,
            vec, vec_grad, xhat, out_grad, tap_grad,
        ],
        [token_bf16, *grad_shapes(2 * feats + 384)],
        [pltpu.VMEM((2 * pooled, feats), BF16)],
        flops=4 << 24,
        spaces=[smem] + [vmem] * 15,
    )
    (input_grad,) = call(
        input_kernel, [grad_mixed, weights, vec, xhat, inv_one, grad_mid], [token_f32], flops=2 << 24
    )
    part_a = add_up(tie(tuple(spread_a), grad_mixed), BF16)
    part_b = add_up(tie(tuple(spread_b), input_grad), BF16)
    part_ab = jnp.concatenate([part_a, part_b], axis=2)
    steps_ab = far_steps()[::-1]
    pairs = part_ab.reshape((-1, 2) + part_ab.shape[1:])
    far_ab = [pairs[:, 0], from_line(pairs[:, 1], steps_ab[0])] if steps_ab else [part_ab]
    near_c = reduce_core(grads_c, input_grad)
    spread_c = spread_near(near_c)
    (block_output,) = call(
        output_kernel, [tie(mid, *near_c), hidden_a, hidden_b, weights_a, weights_b], [token_bf16],
        [pltpu.VMEM((length, feats), BF16), pltpu.SemaphoreType.DMA((blocks,))], flops=4 << 24, out_space=pltpu.HBM
    )
    far_c = spread_far(add_up(tie(tuple(spread_c), block_output), BF16))
    if steps_ab:
        far_ab = [far_ab[0], tie(far_ab[1], block_output)]
    for step in steps_ab[1:]:
        held = add_up(far_ab, BF16)
        pairs = held.reshape((-1, 2) + held.shape[1:])
        far_ab = [pairs[:, 0], from_line(pairs[:, 1], step)]
    far_ab = [term[0] for term in far_ab]
    vector = ((1, rows), F32)
    up_sum, down_sum, in_sum, out_sum, param_sum, *vectors = call(
        lambda *refs: final_kernel(len(far_ab), *refs),
        [kernel_param, jnp.asarray(scale_np), jnp.asarray(wide_np), *far_ab, *far_c],
        [
            ((rows, hidden), F32), ((rows, hidden), F32), ((rows, feats), F32), ((rows, feats), F32),
            ((rows, taps), F32), vector, vector, vector, vector, vector,
        ],
    )
    gain_one, bias_one, skip_sum, gain_two, bias_two = (v.reshape(rows) for v in vectors)
    return (
        block_output[None], input_grad[None], gain_one, bias_one, in_sum, param_sum, skip_sum, out_sum,
        gain_two, bias_two, up_sum, down_sum,
    )


def solution(mesh):
    rows = P(("dp", "seq"), None)
    vector = P(("dp", "seq"))
    tokens = P("dp", "seq", None)
    return jax.shard_map(
        body,
        mesh=mesh,
        in_specs=(
            tokens, vector, vector, rows, rows, vector, rows, vector, vector, rows, rows, tokens,
        ),
        out_specs=(
            tokens, tokens, vector, vector, rows, rows, vector, rows, vector, vector, rows, rows,
        ),
        check_vma=False,
    )
```

```python
import math

import jax
import jax.numpy as jnp
import numpy as np
from jax import lax
from jax.experimental import pallas as pl
from jax.experimental.pallas import tpu as pltpu
from jax.sharding import PartitionSpec as P

TAPS = 32
SCALES = 6
FINE = 3
FREQ = 256
HALF = FREQ // 2
BLOCK = 256
POOL = 8
OFFSET = 28
TILE = 512
WIDE = 512
PACK = 768
F32 = jnp.float32
BF16 = jnp.bfloat16
NT = ((1,), (1,))
TN = ((0,), (0,))


def odd_basis(positions):
    order = np.concatenate([np.arange(0, FREQ, 2), np.arange(1, FREQ, 2)])
    angle = np.pi * np.outer(order + 0.5, positions) / FREQ
    return np.concatenate([np.cos(angle), -np.sin(angle)], axis=0)


def tap_basis(start, first):
    columns = np.zeros((2 * FREQ, 256))
    for scale_at in range(FINE):
        wide = 2**scale_at
        lag = start + TAPS * (wide - 1)
        for tap in range(TAPS):
            at = first + scale_at * TAPS + tap
            columns[:, at] = odd_basis(lag + tap * wide + np.arange(wide)).sum(axis=1)
    return columns


def bf16_const(array):
    return jnp.asarray(np.asarray(array, np.float32).astype(jnp.bfloat16))


def dot(a, b, contract=((1,), (0,))):
    return lax.dot_general(a, b, (contract, ((), ())), preferred_element_type=F32)


def normal_parts(values):
    cdf = 0.5 + 0.5 * lax.erf(values * np.float32(math.sqrt(0.5)))
    pdf = jnp.exp(-0.5 * values * values) * np.float32(1 / math.sqrt(2 * math.pi))
    return cdf, pdf


def split_dp(count):
    edge = round((count / 2) ** (1 / 3))
    return (2 * edge, edge * edge) if 2 * edge**3 == count else (1, count)


def swap_route(count, mask):
    return [(i, i ^ mask) for i in range(count)]


SWAP = [(0, 1), (1, 0)]


def tie(value, *others):
    return lax.optimization_barrier((value, *others))[0]


def far_steps():
    nz, _ = split_dp(lax.axis_size("dp"))
    return [1 << bit for bit in reversed(range(nz.bit_length() - 1))]


def from_line(held, step):
    dp_count = lax.axis_size("dp")
    _, nxy = split_dp(dp_count)
    return lax.ppermute(held, "dp", swap_route(dp_count, step * nxy))


def paired(held, got):
    return jnp.stack([held, got], axis=1).reshape((-1,) + held.shape[1:])


def gather_line(held, step):
    return paired(held, from_line(held, step))


def gather_far(shard):
    held = shard[None]
    for step in far_steps():
        held = gather_line(held, step)
    return held


def gather_near(held):
    dp_count = lax.axis_size("dp")
    _, nxy = split_dp(dp_count)
    return [held] + [lax.ppermute(held, "dp", swap_route(dp_count, k)) for k in range(1, nxy)]


def gather_core(pieces, parts=1):
    held = jnp.concatenate(pieces)
    size = held.shape[0] // parts
    held = [held[at * size : (at + 1) * size] for at in range(parts)]
    return held + [lax.ppermute(part, "seq", SWAP) for part in held]


def gather_plane(held):
    dp_count = lax.axis_size("dp")
    _, nxy = split_dp(dp_count)
    if nxy != 4:
        return gather_near(held)
    by_x = lax.ppermute(held, "dp", swap_route(dp_count, 1))
    by_y = lax.ppermute(held, "dp", swap_route(dp_count, 2))
    if held.shape[0] == 1:
        return [held, by_x, by_y, lax.ppermute(by_y, "dp", swap_route(dp_count, 1))]
    cut = held.shape[0] // 2
    return [
        held, by_x, by_y, lax.ppermute(by_y[:cut], "dp", swap_route(dp_count, 1)),
        lax.ppermute(by_x[cut:], "dp", swap_route(dp_count, 2)),
    ]


def row_place(at, count, plane_first, core_ref):
    nz, nxy = split_dp(count)
    other, at = divmod(at, count)
    if plane_first:
        z, xy = divmod(at, nxy)
    else:
        xy, z = divmod(at, nz)
    return ((z * nxy + xy) ^ core_ref[1]) * 2 + (other ^ core_ref[0])


def in_order(pieces, plane_first):
    if pieces[0].shape[1] % 16 == 0:
        return pieces
    dp_count = lax.axis_size("dp")
    nz, nxy = split_dp(dp_count)
    me, core = lax.axis_index("dp"), lax.axis_index("seq")
    by_dp = jnp.arange(dp_count).reshape(nz, nxy) ^ me
    by_dp = by_dp if plane_first else by_dp.T
    where = by_dp[None] * 2 + (jnp.arange(2)[:, None, None] ^ core)
    flat = jnp.concatenate(pieces)
    return [jnp.take(flat, jnp.argsort(where.reshape(-1)), axis=0).reshape(1, -1, flat.shape[2])]


def reduce_core(grads, *before):
    dp_count = lax.axis_size("dp")
    nz, nxy = split_dp(dp_count)
    if len(grads) == 1:
        core, me = lax.axis_index("seq"), lax.axis_index("dp")
        shaped = grads[0].reshape(dp_count, 2, -1, grads[0].shape[1])
        order = (jnp.arange(nz)[None, :] * nxy + jnp.arange(nxy)[:, None]) ^ me
        shaped = jnp.take(shaped, order.reshape(-1), axis=0)
        grads = [
            lax.dynamic_index_in_dim(shaped, 1 - core, 1, False),
            lax.dynamic_index_in_dim(shaped, core, 1, False),
        ]
    send, keep = grads
    got = lax.ppermute(send, "seq", SWAP)
    got = tie(got, *before)
    total = (keep.astype(F32) + got.astype(F32)).astype(BF16)
    return [total[k * nz : (k + 1) * nz] for k in range(nxy)]


def spread_near(pieces):
    dp_count = lax.axis_size("dp")
    return [pieces[0]] + [
        lax.ppermute(pieces[k], "dp", swap_route(dp_count, k)) for k in range(1, len(pieces))
    ]


def spread_far(part):
    dp_count = lax.axis_size("dp")
    nz, nxy = split_dp(dp_count)
    return [part[0]] + [
        lax.ppermute(part[k], "dp", swap_route(dp_count, k * nxy)) for k in range(1, nz)
    ]


def add_up(pieces, dtype=F32):
    total = pieces[0].astype(F32)
    for piece in pieces[1:]:
        total = total + piece.astype(F32)
    return total.astype(dtype)


def load_rows(core_ref, pieces, target, plane_first):
    if len(pieces) == 1:
        target[...] = pieces[0][0]
        return
    count = target.shape[0] // (2 * pieces[0].shape[1])
    at = 0
    for piece in pieces:
        held, rows, _ = piece.shape
        for i in range(held):
            start = row_place(at, count, plane_first, core_ref) * rows
            target[pl.ds(pl.multiple_of(start, 16), rows), :] = piece[i]
            at += 1


def span(at, size=BLOCK):
    return pl.ds(at * size, size)


def norm_stats(features):
    centre = features - jnp.mean(features, axis=-1, keepdims=True)
    inverse = lax.rsqrt(jnp.mean(centre * centre, axis=-1, keepdims=True) + 1e-05)
    return centre * inverse, inverse


def norm_back(xhat, inverse, scaled):
    return inverse * (
        scaled
        - jnp.mean(scaled, axis=-1, keepdims=True)
        - xhat * jnp.mean(scaled * xhat, axis=-1, keepdims=True)
    )


def quarters(spectrum):
    return [spectrum[i * HALF : (i + 1) * HALF].astype(F32) for i in range(4)]


def add_before(now, past):
    (re, ro, ie, io), (pre, pro, pie, pio) = now, past
    return re - pie, ro + pio, ie + pre, io - pro


def add_after(now, later):
    (re, ro, ie, io), (nre, nro, nie, nio) = now, later
    return re + nie, ro - nio, ie - nre, io + nro


def product(a, b):
    (are, aro, aie, aio), (bre, bro, bie, bio) = a, b
    return (
        are * bre - aie * bie,
        aro * bro - aio * bio,
        are * bie + aie * bre,
        aro * bio + aio * bro,
    )


def conj_product(a, b):
    (are, aro, aie, aio), (bre, bro, bie, bio) = a, b
    return (
        are * bre + aie * bie,
        aro * bro + aio * bio,
        are * bie - aie * bre,
        aro * bio - aio * bro,
    )


def stacked(parts):
    return jnp.concatenate([part.astype(BF16) for part in parts], axis=0)


def put_quarters(ref, at, parts):
    for i, part in enumerate(parts):
        ref[at, i * HALF : (i + 1) * HALF, :] = part.astype(ref.dtype)


def first_part(hidden):
    return hidden // 2


def pack_kernel(core_ref, in_ref, param_ref, out_ref, up_ref, down_ref, *rest):
    vectors, (a_ref, b_ref, param, small, sem) = rest[:5], rest[5:]
    rows, feats = in_ref.shape
    cut = first_part(up_ref.shape[1])
    left = up_ref.shape[1] - cut
    copies = [
        pltpu.make_async_copy(in_ref, a_ref.at[:, pl.ds(0, feats)], sem),
        pltpu.make_async_copy(param_ref, param, sem),
    ]
    for i, vector in enumerate(vectors):
        copies.append(pltpu.make_async_copy(vector, small.at[i], sem))
    for source, start, size, target, at in (
        (out_ref, 0, feats, a_ref, PACK), (up_ref, 0, cut, a_ref, PACK + feats),
        (down_ref, 0, cut, a_ref, PACK + feats + cut), (up_ref, cut, left, b_ref, 0),
        (down_ref, cut, left, b_ref, left),
    ):
        copies.append(
            pltpu.make_async_copy(
                source.at[:, pl.ds(start, size)], target.at[:, pl.ds(at, size)], sem
            )
        )
    for copy in copies:
        copy.start()
    for copy in copies:
        copy.wait()
    spare = PACK - feats - param.shape[1]
    row = lax.broadcasted_iota(jnp.int32, (rows, rows), 0)
    lane = lax.broadcasted_iota(jnp.int32, (rows, rows), 1)
    slot = lax.broadcasted_iota(jnp.int32, (rows, spare), 1)
    block = jnp.zeros((rows, spare), F32)
    for i in range(len(vectors)):
        value = small[i].astype(F32)
        column = jnp.sum(jnp.where(row == lane, value, 0.0), axis=1, keepdims=True)
        block = jnp.where(slot == i, column, block)
    tail = jnp.concatenate([param[...].astype(F32), block], axis=1)
    a_ref[:, feats:PACK] = tail.astype(BF16)


def prepare_kernel(x_ref, cot_ref, xhat_ref, inv_ref, cot_t_ref, cot_copy, x_copy, sem):
    blocks = x_ref.shape[0] // BLOCK
    copies = []
    for source, target, which in ((x_ref, x_copy, 0), (cot_ref, cot_copy, 1)):
        for at in range(blocks):
            copies.append(
                pltpu.make_async_copy(source.at[span(at), :], target.at[span(at), :], sem.at[which, at])
            )
    for copy in copies:
        copy.start()
    for at in range(blocks):
        copies[at].wait()
        xhat, inverse = norm_stats(x_copy[span(at), :].astype(F32))
        xhat_ref[span(at), :] = xhat.astype(BF16)
        inv_ref[span(at), :] = jnp.broadcast_to(inverse, (BLOCK, 128))
    for at in range(blocks):
        copies[blocks + at].wait()
        cot_t_ref[:, span(at)] = cot_copy[span(at), :].T


def prior_kernel(x_ref, xhat_ref):
    for at in range(x_ref.shape[0] // BLOCK):
        xhat_ref[span(at), :] = norm_stats(x_ref[span(at), :].astype(F32))[0].astype(BF16)


def forward_kernel(
    n_pieces, core_ref, xhat_ref, prior_ref, basis, basis_t, basis_pool, back_pool,
    fine_basis, coarse_basis, pool_rows, scale_ref, wide_ref, *rest,
):
    pieces, rest = rest[:n_pieces], rest[n_pieces:]
    weights, vec_ref, fine_h_ref, coarse_h_ref, win_ref, pool_win_ref, act_ref, slope_ref = rest[:8]
    mixed_ref, pooled_ref = rest[8:]
    load_rows(core_ref, pieces, weights, False)
    feats = xhat_ref.shape[1]
    blocks = xhat_ref.shape[0] // BLOCK
    tail = weights[:, feats : feats + 256].astype(F32)
    raw = tail * scale_ref[...]
    inverse = lax.rsqrt(jnp.sum(raw * raw * wide_ref[...], axis=1, keepdims=True) + 1e-05)
    taps = (raw * inverse).astype(BF16)
    vec = tail[:, 128:256].T[64:72]
    vec_ref[...] = vec
    gain, bias, skip = vec[0:1], vec[1:2], vec[2:3]
    fine_h = dot(fine_basis[...], taps, NT)
    coarse_h = dot(coarse_basis[...], taps, NT)
    fine_h_ref[...] = fine_h.astype(BF16)
    coarse_h_ref[...] = coarse_h.astype(BF16)
    proj = weights[:, :feats]
    has_prior = core_ref[0].astype(F32)
    per = BLOCK // POOL
    past = None
    total = dot((prior_ref[...].astype(F32) * gain + bias).astype(BF16), proj)
    for at in range(blocks):
        mixed = (total[at * BLOCK : (at + 1) * BLOCK] * has_prior).astype(BF16)
        pooled_ref[span(at, per), :] = dot(pool_rows[...], mixed).astype(BF16)
        if at == blocks - 1:
            past = quarters(dot(basis[...], mixed))
    total = dot((xhat_ref[...].astype(F32) * gain + bias).astype(BF16), proj)
    for at in range(blocks):
        mixed = total[at * BLOCK : (at + 1) * BLOCK].astype(BF16)
        mixed_ref[span(at), :] = mixed
        pooled_ref[span(blocks + at, per), :] = dot(pool_rows[...], mixed).astype(BF16)
    pool_win = dot(basis_pool[...], pooled_ref[...])
    pool_win_ref[...] = pool_win.astype(BF16)
    coarse_y = stacked(product(quarters(coarse_h), quarters(pool_win)))
    fine_q = quarters(fine_h)
    for at in range(blocks):
        mixed = mixed_ref[span(at), :]
        now = quarters(dot(basis[...], mixed))
        window = add_before(now, past)
        past = now
        put_quarters(win_ref, at, window)
        total = dot(basis_t[...], stacked(product(fine_q, window)))
        total = total + dot(back_pool[span(at), :], coarse_y)
        pre_act = total * np.float32(1 / FREQ) + skip * mixed.astype(F32)
        cdf, pdf = normal_parts(pre_act)
        act_ref[span(at), :] = (pre_act * cdf).astype(BF16)
        slope_ref[span(at), :] = (cdf + pre_act * pdf).astype(BF16)


def place_of(core_ref, grad_refs):
    nz, nxy = split_dp(grad_refs[0].shape[0])
    return core_ref[0], core_ref[1] // nxy, core_ref[1] % nxy, nz, nxy


def put_rows(refs, columns, value, place):
    value = value.astype(BF16)
    if len(refs) == 1:
        refs[0][:, columns] = value
        return
    send_ref, keep_ref = refs
    count, rows, _ = send_ref.shape
    core, me_z, me_xy, nz, nxy = place
    for at in range(count):
        slot = ((at % nxy) ^ me_xy) * nz + ((at // nxy) ^ me_z)
        first = value[2 * at * rows : (2 * at + 1) * rows]
        second = value[(2 * at + 1) * rows : (2 * at + 2) * rows]
        send_ref[slot, :, columns] = jnp.where(core == 0, second, first)
        keep_ref[slot, :, columns] = jnp.where(core == 0, first, second)


def hidden_part(place, normed_ref, normed_t_ref, cot_ref, cot_t_ref, up_at, down_at, weights, hidden_ref, grad_up_ref, grad_refs):
    length = normed_ref.shape[0]
    count = hidden_ref.shape[1]
    for at in range(0, count, WIDE):
        wide = min(WIDE, count - at)
        columns = slice(at, at + wide)
        up = weights[:, up_at + at : up_at + at + wide]
        down = weights[:, down_at + at : down_at + at + wide]
        for row in range(0, length, TILE):
            rows = slice(row, row + TILE)
            up_val = dot(normed_ref[rows, :], up)
            grad_hidden = dot(cot_ref[rows, :], down)
            cdf, pdf = normal_parts(up_val)
            hidden_ref[rows, columns] = (up_val * cdf).astype(BF16)
            grad_up_ref[rows, columns] = (grad_hidden * (cdf + up_val * pdf)).astype(BF16)
        put_rows(grad_refs, slice(at, at + wide), dot(normed_t_ref[...], grad_up_ref[:, columns]), place)
        put_rows(grad_refs, slice(count + at, count + at + wide), dot(cot_t_ref[...], hidden_ref[:, columns]), place)


def middle_first_kernel(
    n_pieces, core_ref, act_ref, x_ref, cot_ref, cot_t_ref, vec_ref, *rest
):
    pieces, rest = rest[:n_pieces], rest[n_pieces:]
    (proj_ref, mid_ref, xhat_ref, inv_ref, normed_ref, normed_t_ref, hidden_ref, grad_up_ref), rest = rest[:8], rest[8:]
    weights, *grad_refs = rest
    load_rows(core_ref, pieces, weights, False)
    length, feats = x_ref.shape
    count = hidden_ref.shape[1]
    gain, bias = vec_ref[3:4, :], vec_ref[4:5, :]
    proj_ref[...] = weights[:, :feats]
    for at in range(length // BLOCK):
        mid = x_ref[span(at), :].astype(F32) + dot(act_ref[span(at), :], proj_ref[...])
        xhat, inverse = norm_stats(mid)
        normed = (xhat * gain + bias).astype(BF16)
        mid_ref[span(at), :] = mid
        xhat_ref[span(at), :] = xhat
        inv_ref[span(at), :] = jnp.broadcast_to(inverse, (BLOCK, 128))
        normed_ref[span(at), :] = normed
        normed_t_ref[:, span(at)] = normed.T
    hidden_part(
        place_of(core_ref, grad_refs), normed_ref, normed_t_ref, cot_ref, cot_t_ref, feats, feats + count,
        weights, hidden_ref, grad_up_ref, grad_refs,
    )


def middle_second_kernel(
    n_pieces, core_ref, cot_ref, cot_t_ref, normed_ref, normed_t_ref, *rest
):
    pieces, rest = rest[:n_pieces], rest[n_pieces:]
    hidden_ref, grad_up_ref, weights, *grad_refs = rest
    load_rows(core_ref, pieces, weights, True)
    hidden_part(
        place_of(core_ref, grad_refs), normed_ref, normed_t_ref, cot_ref, cot_t_ref, 0,
        hidden_ref.shape[1], weights, hidden_ref, grad_up_ref, grad_refs,
    )


def middle_third_kernel(
    slope_ref, cot_ref, vec_ref, pool_rows, proj_ref, xhat_ref, inv_ref, up_a_ref, up_b_ref, weights_a,
    weights_b, mid_grad_ref, vec_grad_ref, pre_grad_ref, halo_ref,
):
    length, feats = xhat_ref.shape
    count, left = up_a_ref.shape[1], up_b_ref.shape[1]
    gain = vec_ref[3:4, :]
    gain_grad = jnp.zeros((8, feats), F32)
    bias_grad = jnp.zeros((8, feats), F32)
    per = BLOCK // POOL
    for at in range(length // BLOCK):
        grad_normed = dot(up_a_ref[span(at), :], weights_a[:, feats : feats + count], NT)
        grad_normed = grad_normed + dot(up_b_ref[span(at), :], weights_b[:, :left], NT)
        xhat = xhat_ref[span(at), :]
        bias_grad = bias_grad + jnp.sum(grad_normed.reshape(BLOCK // 8, 8, feats), axis=0)
        gain_grad = gain_grad + jnp.sum((grad_normed * xhat).reshape(BLOCK // 8, 8, feats), axis=0)
        grad_mid = cot_ref[span(at), :].astype(F32) + norm_back(
            xhat, inv_ref[span(at), 0:1], grad_normed * gain
        )
        mid_grad_ref[span(at), :] = grad_mid
        grad_act = dot(grad_mid.astype(BF16), proj_ref[...], NT)
        grad_pre = (grad_act * slope_ref[span(at), :].astype(F32)).astype(BF16)
        pre_grad_ref[span(at), :] = grad_pre
        if at == 0:
            halo_ref[0:BLOCK, :] = grad_pre
        halo_ref[pl.ds(BLOCK + at * per, per), :] = (
            dot(pool_rows[...], grad_pre) * np.float32(POOL)
        ).astype(BF16)
    vec_grad_ref[0:1, :] = jnp.sum(gain_grad, axis=0, keepdims=True)
    vec_grad_ref[1:2, :] = jnp.sum(bias_grad, axis=0, keepdims=True)
    vec_grad_ref[2:8, :] = jnp.zeros((6, feats), F32)


def output_kernel(mid_ref, hidden_a_ref, hidden_b_ref, weights_a, weights_b, out_ref, stage, sem):
    length, feats = mid_ref.shape
    count, left = hidden_a_ref.shape[1], hidden_b_ref.shape[1]
    copies = []
    for at in range(length // BLOCK):
        total = mid_ref[span(at), :] + dot(hidden_a_ref[span(at), :], weights_a[:, feats + count :], NT)
        total = total + dot(hidden_b_ref[span(at), :], weights_b[:, left:], NT)
        stage[span(at), :] = total.astype(BF16)
        copies.append(pltpu.make_async_copy(stage.at[span(at), :], out_ref.at[span(at), :], sem.at[at]))
        copies[-1].start()
    for copy in copies:
        copy.wait()


def taps_kernel(
    act_ref, mid_grad_ref, pre_grad_ref, halo_ref, win_ref, pool_win_ref, basis, fine_basis,
    coarse_basis, out_grad_ref, tap_grad_ref, z_ref, mid_bf_ref,
):
    length, feats = act_ref.shape
    blocks = length // BLOCK
    total = None
    for at in range(blocks):
        mid_bf_ref[span(at), :] = mid_grad_ref[span(at), :].astype(BF16)
        z = dot(basis[...], pre_grad_ref[span(at), :])
        z_ref[at] = z.astype(BF16)
        term = conj_product(quarters(win_ref[at]), quarters(z))
        total = term if total is None else [a + b for a, b in zip(total, term)]
    out_grad_ref[...] = dot(act_ref[...], mid_bf_ref[...], TN).astype(BF16)
    pooled = length // POOL
    z_pool = dot(basis[:, 0:pooled], halo_ref[BLOCK : BLOCK + pooled, :])
    pool_term = conj_product(quarters(pool_win_ref[...]), quarters(z_pool))
    tap_grad_ref[...] = (
        (dot(stacked(total), fine_basis[...], TN) + dot(stacked(pool_term), coarse_basis[...], TN))
        * np.float32(1 / FREQ)
    ).astype(BF16)


def backward_kernel(
    core_ref, z_ref, halo_ref, next_ref, pre_grad_ref, fine_h_ref, coarse_h_ref, basis, basis_t, back_pool,
    weights, vec_ref, vec_grad_ref, xhat_ref, out_grad_ref, tap_grad_ref, mixed_grad_ref, *rest
):
    *grad_refs, pool_ref = rest
    place = place_of(core_ref, grad_refs)
    length, feats = xhat_ref.shape
    blocks = length // BLOCK
    pooled = length // POOL
    gain, bias, skip = vec_ref[0:1, :], vec_ref[1:2, :], vec_ref[2:3, :]
    fine_q = quarters(fine_h_ref[...])
    pool_ref[0:pooled, :] = halo_ref[BLOCK : BLOCK + pooled, :]
    pool_ref[pooled : 2 * pooled, :] = next_ref[BLOCK : BLOCK + pooled, :]
    z_pool = quarters(dot(basis[...], pool_ref[...]))
    coarse_y = stacked([v * np.float32(1 / POOL) for v in conj_product(quarters(coarse_h_ref[...]), z_pool)])
    later = quarters(dot(basis[...], next_ref[0:BLOCK, :]))
    sums = jnp.zeros((8, feats), F32)
    for at in reversed(range(blocks)):
        now = quarters(z_ref[at])
        y = stacked(conj_product(fine_q, add_after(now, later)))
        later = now
        total = dot(basis_t[...], y) + dot(back_pool[span(at), :], coarse_y)
        grad_mixed = (
            total * np.float32(1 / FREQ) + skip * pre_grad_ref[span(at), :].astype(F32)
        ).astype(BF16)
        mixed_grad_ref[span(at), :] = grad_mixed
        sums = sums + jnp.sum(grad_mixed.astype(F32).reshape(BLOCK // 8, 8, feats), axis=0)
    back = dot(xhat_ref[...], mixed_grad_ref[...], TN)
    mixed_sum = jnp.sum(sums, axis=0, keepdims=True)
    blank = jnp.zeros((64, feats), F32)
    padded = jnp.concatenate([blank, vec_ref[...], vec_grad_ref[...], blank[:48]], axis=0)
    columns = padded.T
    put_rows(grad_refs, slice(0, feats), columns[:, 64:65] * back + columns[:, 65:66] * mixed_sum, place)
    put_rows(grad_refs, slice(feats, 2 * feats), out_grad_ref[...], place)
    put_rows(grad_refs, slice(2 * feats, 2 * feats + 128), tap_grad_ref[:, :128], place)
    proj = weights[:, 0:feats]
    proj_f = proj.astype(F32)
    gain_grad = jnp.sum(proj_f * back, axis=1, keepdims=True)
    bias_grad = jnp.sum(proj_f * mixed_sum, axis=1, keepdims=True)
    lane = lax.broadcasted_iota(jnp.int32, (feats, 128), 1)
    columns = jnp.where(lane == 64, gain_grad, jnp.where(lane == 65, bias_grad, columns))
    columns = jnp.where(lane < 64, tap_grad_ref[:, 128:].astype(F32), columns)
    put_rows(grad_refs, slice(2 * feats + 128, 2 * feats + 256), columns, place)


def input_kernel(mixed_grad_ref, weights, vec_ref, xhat_ref, inv_ref, mid_grad_ref, input_grad_ref):
    length, feats = xhat_ref.shape
    proj = weights[:, 0:feats]
    for at in range(length // BLOCK):
        grad_normed = dot(mixed_grad_ref[span(at), :], proj, NT)
        input_grad_ref[span(at), :] = mid_grad_ref[span(at), :] + norm_back(
            xhat_ref[span(at), :].astype(F32), inv_ref[span(at), 0:1], grad_normed * vec_ref[0:1, :]
        )


def final_kernel(n_mlp, param_ref, scale_ref, wide_ref, *rest):
    sources, outs = rest[: len(rest) - 10], rest[len(rest) - 10 :]
    up_ref, down_ref, in_ref, out_ref, param_grad_ref = outs[:5]
    totals = []
    for group in (sources[:n_mlp], sources[n_mlp:]):
        total = group[0][...].astype(F32)
        for source in group[1:]:
            total = total + source[...].astype(F32)
        totals.append(total)
    mlp, mixer = totals
    hidden = mlp.shape[1] // 2
    cut = first_part(hidden)
    up_ref[:, :cut], up_ref[:, cut:] = mlp[:, :cut], mlp[:, 2 * cut : cut + hidden]
    down_ref[:, :cut], down_ref[:, cut:] = mlp[:, cut : 2 * cut], mlp[:, cut + hidden :]
    feats = in_ref.shape[1]
    in_ref[...] = mixer[:, :feats]
    out_ref[...] = mixer[:, feats : 2 * feats]
    taps = param_ref.shape[1]
    tap_rows = mixer[:, 2 * feats : 2 * feats + taps]
    scale, wide = scale_ref[:, :taps], wide_ref[:, :taps]
    raw = param_ref[...].astype(F32) * scale
    inverse = lax.rsqrt(jnp.sum(raw * raw * wide, axis=1, keepdims=True) + 1e-05)
    own = raw * inverse
    along = jnp.sum(tap_rows * own, axis=1, keepdims=True)
    param_grad_ref[...] = scale * inverse * (tap_rows - wide * own * along)
    tail = mixer[:, 2 * feats + 128 :]
    rows = tail.shape[0]
    diagonal = lax.broadcasted_iota(jnp.int32, (rows, rows), 0) == lax.broadcasted_iota(
        jnp.int32, (rows, rows), 1
    )
    columns = (tail[:, 64:65], tail[:, 65:66], tap_rows[:, 0:1], tail[:, 72:73], tail[:, 73:74])
    for ref, column in zip(outs[5:], columns):
        ref[...] = jnp.sum(jnp.where(diagonal, column, 0.0), axis=0, keepdims=True)


def call(kernel, operands, outs, scratch=(), flops=0, spaces=None, limit=12, out_space=pltpu.VMEM):
    spaces = spaces or [pltpu.VMEM] * len(operands)
    operands = [
        pltpu.with_memory_space_constraint(operand, pltpu.HBM) if space is pltpu.HBM else operand
        for operand, space in zip(operands, spaces)
    ]
    return pl.pallas_call(
        kernel,
        out_shape=[jax.ShapeDtypeStruct(shape, dtype) for shape, dtype in outs],
        in_specs=[pl.BlockSpec(memory_space=space) for space in spaces],
        out_specs=[pl.BlockSpec(memory_space=out_space)] * len(outs),
        scratch_shapes=list(scratch),
        compiler_params=pltpu.CompilerParams(vmem_limit_bytes=limit << 20),
        cost_estimate=pl.CostEstimate(flops=flops, bytes_accessed=1 << 16, transcendentals=0),
    )(*operands)


def body(
    block_input,
    mixer_gain,
    mixer_bias,
    in_proj,
    kernel_param,
    skip_gain,
    out_proj,
    mlp_gain,
    mlp_bias,
    up_proj,
    down_proj,
    out_cotangent,
):
    _, length, feats = block_input.shape
    hidden = up_proj.shape[1]
    cut = first_part(hidden)
    left = hidden - cut
    blocks = length // BLOCK
    pooled = length // POOL
    taps = TAPS * SCALES
    own_rows = in_proj.shape[0]
    x_own, cot = block_input[0], out_cotangent[0]
    core_at = jnp.stack([lax.axis_index("seq"), lax.axis_index("dp")]).astype(jnp.int32)
    x_prior = lax.ppermute(x_own, "seq", [(0, 1)])
    vectors = [v.reshape(1, -1) for v in (mixer_gain, mixer_bias, skip_gain, mlp_gain, mlp_bias)]
    shard, shard_b = call(
        pack_kernel,
        [core_at, in_proj, kernel_param, out_proj, up_proj, down_proj, *vectors],
        [((own_rows, PACK + feats + 2 * cut), BF16), ((own_rows, 2 * left), BF16)],
        [
            pltpu.VMEM(kernel_param.shape, BF16), pltpu.VMEM((5, 1, own_rows), BF16),
            pltpu.SemaphoreType.DMA,
        ],
        spaces=[pltpu.SMEM] + [pltpu.HBM] * 10,
    )
    basis_np = odd_basis(np.arange(BLOCK))
    basis, basis_t = bf16_const(basis_np), bf16_const(basis_np.T)
    basis_pool = bf16_const(odd_basis(np.arange(-pooled, pooled)))
    back_pool = bf16_const(np.repeat(odd_basis(np.arange(pooled)).T, POOL, axis=0))
    fine_basis = bf16_const(tap_basis(0, 0))
    coarse_basis = bf16_const(tap_basis(OFFSET, TAPS * FINE))
    pool_rows = bf16_const(np.kron(np.eye(BLOCK // POOL), np.ones((1, POOL))) / POOL)
    scale_np = np.zeros((1, 256), np.float32)
    scale_np[0, :taps] = np.repeat(0.5 ** np.arange(SCALES), TAPS)
    wide_np = np.zeros((1, 256), np.float32)
    wide_np[0, :taps] = np.repeat(2.0 ** (np.arange(SCALES) % FINE), TAPS)

    xhat, inv_one, cot_t, cot, x_own = call(
        prepare_kernel,
        [x_own, cot],
        [
            ((length, feats), BF16), ((length, 128), F32), ((feats, length), BF16),
            ((length, feats), BF16), ((length, feats), BF16),
        ],
        [pltpu.SemaphoreType.DMA((2, blocks))],
        spaces=[pltpu.HBM] * 2,
    )
    (prior_hat,) = call(prior_kernel, [x_prior], [((length, feats), BF16)])
    held_b = jnp.concatenate(gather_near(tie(shard_b, prior_hat)[None]))
    held = shard[None]
    for at, step in enumerate(far_steps()):
        got = from_line(held, step)
        got = tie(got, xhat) if at == 0 else got
        held = paired(held, got)
    held = tie(held, xhat, prior_hat, held_b)
    steps = far_steps()
    held_b = held_b[None]
    for step in steps[:-1]:
        held_b = gather_line(held_b, step)
    xhat_in = tie(xhat, held_b)
    first, held_a = held[:, :, :PACK], held[:, :, PACK:]
    first = gather_near(first)
    pieces_a = gather_plane(held_a)
    first = in_order(gather_core(first), False)
    smem = pltpu.SMEM
    n_first = len(first)
    weights, vec, fine_h, coarse_h, window, pool_win, act, slope = call(
        lambda *refs: forward_kernel(n_first, *refs),
        [
            core_at, xhat_in, prior_hat, basis, basis_t, basis_pool,
            back_pool, fine_basis, coarse_basis, pool_rows, jnp.asarray(scale_np), jnp.asarray(wide_np),
            *first,
        ],
        [
            ((feats, PACK), BF16), ((8, feats), F32), ((2 * FREQ, feats), BF16),
            ((2 * FREQ, feats), BF16), ((blocks, 2 * FREQ, feats), BF16), ((2 * FREQ, feats), BF16),
            ((length, feats), BF16), ((length, feats), BF16),
        ],
        [
            pltpu.VMEM((length, feats), BF16), pltpu.VMEM((2 * pooled, feats), BF16),
        ],
        flops=6 << 30,
        spaces=[smem] + [pltpu.VMEM] * (11 + n_first),
    )
    got_b = [from_line(held_b, step) for step in steps[-1:]]
    *pieces_a, act = lax.optimization_barrier((*pieces_a, act))
    pieces_a = in_order(gather_core(pieces_a, 4), False)
    *got_b, act = lax.optimization_barrier((*got_b, act))
    for got in got_b:
        held_b = paired(held_b, got)
    held_b = held_b.reshape((-1,) + held_b.shape[2:])
    pieces_b = in_order(gather_core([held_b]), True)
    n_a = len(pieces_a)
    rows = own_rows


    def grad_shapes(columns):
        if rows % 16 == 0:
            return [((feats // (2 * rows), rows, columns), BF16)] * 2
        return [((feats, columns), BF16)]

    token_f32, token_bf16 = ((length, feats), F32), ((length, feats), BF16)
    vmem = pltpu.VMEM
    proj_out, mid, xhat_two, inv_two, normed, normed_t, hidden_a, grad_up_a, weights_a, *grads_a = call(
        lambda *refs: middle_first_kernel(n_a, *refs),
        [core_at, act, x_own, cot, cot_t, vec, *pieces_a],
        [
            ((feats, feats), BF16), token_f32, token_f32, ((length, 128), F32), token_bf16,
            ((feats, length), BF16), ((length, cut), BF16), ((length, cut), BF16),
            ((feats, feats + 2 * cut), BF16), *grad_shapes(2 * cut),
        ],
        flops=8 << 30,
        spaces=[smem] + [vmem] * (5 + n_a),
    )
    n_b = len(pieces_b)
    hidden_b, grad_up_b, weights_b, *grads_b = call(
        lambda *refs: middle_second_kernel(n_b, *refs),
        [core_at, cot, cot_t, normed, normed_t, *pieces_b],
        [((length, left), BF16), ((length, left), BF16), ((feats, 2 * left), BF16), *grad_shapes(2 * left)],
        flops=16 << 30,
        spaces=[smem] + [vmem] * (4 + n_b),
    )
    near_a = reduce_core(grads_a, hidden_b)
    grad_up_b = tie(grad_up_b, *near_a)
    spread_a = spread_near(near_a)
    grad_mid, vec_grad, grad_pre, halo = call(
        middle_third_kernel,
        [slope, cot, vec, pool_rows, proj_out, xhat_two, inv_two, grad_up_a, grad_up_b, weights_a, weights_b],
        [token_f32, ((8, feats), F32), token_bf16, ((BLOCK + pooled, feats), BF16)],
        flops=4 << 30,
    )
    after = lax.ppermute(halo, "seq", [(1, 0)])
    near_b = reduce_core(grads_b, grad_mid)
    grad_pre = tie(grad_pre, *near_b)
    spread_b = spread_near(near_b)
    out_grad, tap_grad, z_grad = call(
        taps_kernel,
        [act, grad_mid, grad_pre, halo, window, pool_win, basis, fine_basis, coarse_basis],
        [
            ((feats, feats), BF16), ((feats, 256), BF16), ((blocks, 2 * FREQ, feats), BF16),
        ],
        [pltpu.VMEM((length, feats), BF16)],
        flops=2 << 24,
    )
    z_grad = tie(z_grad, after)
    grad_mixed, *grads_c = call(
        backward_kernel,
        [
            core_at, z_grad, halo, after, grad_pre, fine_h, coarse_h, basis, basis_t, back_pool, weights,
            vec, vec_grad, xhat, out_grad, tap_grad,
        ],
        [token_bf16, *grad_shapes(2 * feats + 256)],
        [pltpu.VMEM((2 * pooled, feats), BF16)],
        flops=4 << 24,
        spaces=[smem] + [vmem] * 15,
    )
    (input_grad,) = call(
        input_kernel, [grad_mixed, weights, vec, xhat, inv_one, grad_mid], [token_f32], flops=2 << 24
    )
    part_a = add_up(tie(tuple(spread_a), grad_mixed), BF16)
    part_b = add_up(tie(tuple(spread_b), input_grad), BF16)
    part_ab = jnp.concatenate([part_a, part_b], axis=2)
    steps_ab = far_steps()[::-1]
    pairs = part_ab.reshape((-1, 2) + part_ab.shape[1:])
    far_ab = [pairs[:, 0], from_line(pairs[:, 1], steps_ab[0])] if steps_ab else [part_ab]
    near_c = reduce_core(grads_c, input_grad)
    spread_c = spread_near(near_c)
    (block_output,) = call(
        output_kernel, [tie(mid, *near_c), hidden_a, hidden_b, weights_a, weights_b], [token_bf16],
        [pltpu.VMEM((length, feats), BF16), pltpu.SemaphoreType.DMA((blocks,))], flops=4 << 24, out_space=pltpu.HBM
    )
    far_c = spread_far(add_up(tie(tuple(spread_c), block_output), BF16))
    if steps_ab:
        far_ab = [far_ab[0], tie(far_ab[1], block_output)]
    for step in steps_ab[1:]:
        held = add_up(far_ab, BF16)
        pairs = held.reshape((-1, 2) + held.shape[1:])
        far_ab = [pairs[:, 0], from_line(pairs[:, 1], step)]
    far_ab = [term[0] for term in far_ab]
    vector = ((1, rows), F32)
    up_sum, down_sum, in_sum, out_sum, param_sum, *vectors = call(
        lambda *refs: final_kernel(len(far_ab), *refs),
        [kernel_param, jnp.asarray(scale_np), jnp.asarray(wide_np), *far_ab, *far_c],
        [
            ((rows, hidden), F32), ((rows, hidden), F32), ((rows, feats), F32), ((rows, feats), F32),
            ((rows, taps), F32), vector, vector, vector, vector, vector,
        ],
    )
    gain_one, bias_one, skip_sum, gain_two, bias_two = (v.reshape(rows) for v in vectors)
    return (
        block_output[None], input_grad[None], gain_one, bias_one, in_sum, param_sum, skip_sum, out_sum,
        gain_two, bias_two, up_sum, down_sum,
    )


def solution(mesh):
    rows = P(("dp", "seq"), None)
    vector = P(("dp", "seq"))
    tokens = P("dp", "seq", None)
    return jax.shard_map(
        body,
        mesh=mesh,
        in_specs=(
            tokens, vector, vector, rows, rows, vector, rows, vector, vector, rows, rows, tokens,
        ),
        out_specs=(
            tokens, tokens, vector, vector, rows, rows, vector, rows, vector, vector, rows, rows,
        ),
        check_vma=False,
    )
```
